128 devices in a mesh: section: 2 (over core), gx: 4 (over x), gy: 16 (over z, y).
Axes of the slice: x: 4, y: 4, z: 4, core: 2. Of those that a mesh axis runs over, the one named last changes fastest.
Arguments:
- inputs: bfloat16 [2, 16, 512, 960], P(None, 'gy', 'gx'), may hold values from -6 to 6
- cotangent: bfloat16 [2, 16, 512, 960], P(None, 'gy', 'gx'), may hold values from -6 to 6
- segment_ids: int32 [2, 16, 512], P(None, 'gy'), may hold values from 0 to 3, as said below
- gain_attn: bfloat16 [2, 960], P('section', ('gx', 'gy')), may hold values from 0.5 to 1.5
- w_qkv: bfloat16 [2, 960, 1600], P('section', ('gx', 'gy')), may hold values from -0.1875 to 0.1875
- w_out: bfloat16 [2, 960, 960], P('section', ('gx', 'gy')), may hold values from -1 to 1
- gain_ffn: bfloat16 [2, 960], P('section', ('gx', 'gy')), may hold values from 0.5 to 1.5
- w_gate: bfloat16 [2, 960, 2560], P('section', 'gx', 'gy'), may hold values from -0.1875 to 0.1875
- w_up: bfloat16 [2, 960, 2560], P('section', 'gx', 'gy'), may hold values from -0.1875 to 0.1875
- w_down: bfloat16 [2, 2560, 960], P('section', 'gy', 'gx'), may hold values from -0.125 to 0.125
Outputs:
- layer_out: bfloat16 [2, 2, 16, 512, 960], P('section', None, 'gy', 'gx')
- input_grad: bfloat16 [2, 2, 16, 512, 960], P('section', None, 'gy', 'gx')
- grad_gain_attn: float32 [2, 960], P('section', ('gx', 'gy'))
- grad_w_qkv: float32 [2, 960, 1600], P('section', ('gx', 'gy'))
- grad_w_out: float32 [2, 960, 960], P('section', ('gx', 'gy'))
- grad_gain_ffn: float32 [2, 960], P('section', ('gx', 'gy'))
- grad_w_gate: float32 [2, 960, 2560], P('section', 'gx', 'gy')
- grad_w_up: float32 [2, 960, 2560], P('section', 'gx', 'gy')
- grad_w_down: float32 [2, 2560, 960], P('section', 'gy', 'gx')
The draws below stay inside these ranges and needn't reach their ends.
Inputs may be any that keep to these rules, and one draw needn't show every extreme that they name: `segment_ids`: along each sequence the segment ids never fall, start at 0 and reach 3; the last document of every sequence begins within its first 128 tokens.
All inputs are finite; a program needn't handle non-finite values.
Results may differ from the reference program's by a relative error of at most 0.02.
Values may be sent and summed in bfloat16 or wider, within the bound.
No kernel may reach another device: no remote copies, remote signals or barrier semaphores. Data moves between devices by JAX's collectives and lax.ppermute only.
A program may use at most 192 MiB of HBM per device.

```python
import jax
import jax.numpy as jnp
from jax import lax

D = 960
HQ = 15
HK = 5
HD = 64
F = 2560
TOK_DEV = 128
MB = 2
NDOC = 4
LEN = 512
NSEQ = 16
QW = 960
KW = 320
N_SECTION = 2


def draw_segment_ids(key, part):
    key = jax.random.fold_in(key, 11)
    token_index = jnp.arange(LEN, dtype=jnp.int32)
    stacked = []
    for batch_slot in range(MB):
        rows = []
        for seq_slot in range(NSEQ):
            shuffled = jax.random.permutation(jax.random.fold_in(key, batch_slot * NSEQ + seq_slot + 2), TOK_DEV - 1)
            breaks = shuffled[:NDOC - 1].astype(jnp.int32) + 1
            numbers = jnp.sum((token_index[:, None] >= breaks[None, :]).astype(jnp.int32), axis=1)
            rows.append(numbers)
        stacked.append(jnp.stack(rows))
    return jnp.stack(stacked).astype(jnp.int32)


def levels(key, dims, shards, smallest, high):
    loudness, own = 1.0, jax.random.fold_in(key, 6)
    for dim, shards_of in shards:
        steps = jnp.exp(jax.random.uniform(jax.random.fold_in(own, dim), (shards_of,), jnp.float32, smallest / len(shards), high / len(shards)))
        loudness = loudness * jnp.repeat(steps, dims[dim] // shards_of).reshape([-1 if axis == dim else 1 for axis in range(len(dims))])
    return loudness


def scatter_about(rng, extent, scale, bound, pieces=(), held_as=jnp.bfloat16):
    drawn = jax.random.normal(rng, extent, jnp.float32) * scale
    if len(pieces) > 0:
        drawn = levels(rng, extent, pieces, -0.22, 0.18) * drawn
    return jnp.clip(drawn, min=-bound, max=bound).astype(held_as)


def setup_inputs(seed: int = 0) -> dict:
    splits = jax.random.split(jax.random.key(seed), 11)
    inputs = scatter_about(splits[0], (MB, NSEQ, LEN, D), 1.0, 6.0, ((1, 16), (2, 4)))
    cotangent = scatter_about(splits[1], (MB, NSEQ, LEN, D), 1.0, 6.0, ((1, 16), (2, 4)))
    segment_ids = draw_segment_ids(jax.random.fold_in(splits[10], 71), 0)
    gain_attn = jnp.clip(1.0 + 0.1 * jax.random.normal(splits[3], (N_SECTION, D), jnp.float32), 0.5, 1.5).astype(jnp.bfloat16)
    w_qkv = scatter_about(splits[4], (N_SECTION, D, QW + 2 * KW), D ** -0.5, 0.1875, ((0, 2), (1, 64)))
    w_out = scatter_about(splits[5], (N_SECTION, QW, D), (HD // 2) ** -0.5, 1.0, ((0, 2), (1, 64)))
    gain_ffn = jnp.clip(1.0 + 0.1 * jax.random.normal(splits[6], (N_SECTION, D), jnp.float32), 0.5, 1.5).astype(jnp.bfloat16)
    w_gate = scatter_about(splits[7], (N_SECTION, D, F), D ** -0.5, 0.1875, ((0, 2), (1, 4), (2, 16)))
    w_up = scatter_about(splits[8], (N_SECTION, D, F), D ** -0.5, 0.1875, ((0, 2), (1, 4), (2, 16)))
    w_down = scatter_about(splits[9], (N_SECTION, F, D), F ** -0.5, 0.125, ((0, 2), (1, 16), (2, 4)))
    return {"inputs": inputs, "cotangent": cotangent, "segment_ids": segment_ids, "gain_attn": gain_attn, "w_qkv": w_qkv, "w_out": w_out, "gain_ffn": gain_ffn, "w_gate": w_gate, "w_up": w_up, "w_down": w_down}


epsilon = 1e-05
rope_base = 100000.0
masked_score = -1e+30

@jax.custom_vjp
def low(v):
    return lax.optimization_barrier(v.astype(jnp.bfloat16)).astype(jnp.float32)

@jax.custom_vjp
def low_back(v):
    return v

def low_keep(v):
    return (low(v), None)

def low_pass(kept, grad):
    return (grad,)

def back_keep(v):
    return (v, None)

def back_low(kept, grad):
    return (low(grad),)
low.defvjp(low_keep, low_pass)
low_back.defvjp(back_keep, back_low)

def rope_tables(positions):
    half_width = HD // 2
    frequency = rope_base ** (-(jnp.arange(half_width, dtype=jnp.float32) * 2.0) / HD)
    angles = positions.astype(jnp.float32)[:, None] * frequency[None, :]
    cosine = jnp.cos(angles)
    sine_part = jnp.sin(angles)
    return (jnp.concatenate([cosine, cosine], 1), jnp.concatenate([sine_part, sine_part], 1))

def rotate(values, cosine, sine_part, head_count):
    row_count = values.shape[0]
    shaped = values.reshape(row_count, head_count, HD)
    half_width = HD // 2
    turned = jnp.concatenate([-shaped[:, :, half_width:], shaped[:, :, :half_width]], 2)
    return (shaped * cosine[:, None, :] + turned * sine_part[:, None, :]).reshape(row_count, head_count * HD)

def attention(queries, keys, values, segments):
    block_rows = min(512, LEN)
    block_count = LEN // block_rows
    token_index = jnp.arange(LEN, dtype=jnp.int32)
    key_heads = keys.reshape(LEN, HK, HD)
    value_heads = values.reshape(LEN, HK, HD)
    grouped = queries.reshape(block_count, block_rows, HK, HQ // HK, HD)

    @jax.checkpoint
    def one_block(items):
        query_block, query_index, query_ids = items
        scores = jnp.einsum('nhgd,shd->hgns', query_block, key_heads, precision=lax.Precision.HIGHEST) * 0.125
        scores = low_back(scores)
        allowed = (query_ids[:, None] == segments[None, :]) & (token_index[None, :] <= query_index[:, None])
        scores = jnp.where(allowed[None, None], scores, masked_score)
        highest = lax.optimization_barrier(jnp.max(scores, axis=3, keepdims=True))
        exponent_terms = jnp.exp(scores - highest)
        probs = low(exponent_terms / lax.optimization_barrier(jnp.sum(exponent_terms, axis=3, keepdims=True)))
        result = jnp.einsum('hgns,shd->nhgd', probs, value_heads, precision=lax.Precision.HIGHEST)
        return result.reshape(block_rows, QW)
    blocks = lax.map(one_block, (grouped, token_index.reshape(block_count, block_rows), segments.reshape(block_count, block_rows)))
    return blocks.reshape(LEN, QW)

def layer_forward(section_in, segments, weights):
    gain_one, qkv_matrix, out_matrix, gain_two, gate_matrix, up_matrix, down_matrix = weights
    resid = low_back(section_in)
    rstd_one = lax.rsqrt(lax.optimization_barrier(jnp.mean(resid * resid, axis=1, keepdims=True)) + epsilon)
    normed_one = low(resid * rstd_one * gain_one)
    projected = low_back(jnp.dot(normed_one, qkv_matrix, precision=lax.Precision.HIGHEST))
    token_index = jnp.arange(LEN, dtype=jnp.int32)
    doc_start = lax.optimization_barrier(jnp.sum((segments[None, :] < segments[:, None]).astype(jnp.int32), axis=1))
    cosine, sine_part = rope_tables(token_index - doc_start)
    queries = low(rotate(projected[:, :QW], cosine, sine_part, HQ))
    keys = low(rotate(projected[:, QW:QW + KW], cosine, sine_part, HK))
    values = low(projected[:, QW + KW:])
    attended = low(low_back(attention(queries, keys, values, segments)))
    middle = resid + low_back(jnp.dot(attended, out_matrix, precision=lax.Precision.HIGHEST))
    rstd_two = lax.rsqrt(lax.optimization_barrier(jnp.mean(middle * middle, axis=1, keepdims=True)) + epsilon)
    normed_two = low(middle * rstd_two * gain_two)
    gate = low_back(jnp.dot(normed_two, gate_matrix, precision=lax.Precision.HIGHEST))
    up_part = low_back(jnp.dot(normed_two, up_matrix, precision=lax.Precision.HIGHEST))
    hidden = low(jax.nn.silu(gate) * up_part)
    return middle + low_back(jnp.dot(hidden, down_matrix, precision=lax.Precision.HIGHEST))

def section_apply(section_in, segments, weights):

    def one_sequence(items):
        return layer_forward(items[0], items[1], weights)
    return lax.map(one_sequence, (section_in, segments))

def reference(inputs, cotangent, segment_ids, gain_attn, w_qkv, w_out, gain_ffn, w_gate, w_up, w_down):
    weights = tuple((member.astype(jnp.float32) for member in (gain_attn, w_qkv, w_out, gain_ffn, w_gate, w_up, w_down)))
    section_inputs = inputs.astype(jnp.float32)
    between = jnp.zeros((MB, NSEQ, LEN, D), jnp.float32)

    def forward(weights, section_inputs, between):
        firsts = []
        lasts = []
        first_weights = tuple((member[0] for member in weights))
        last_weights = tuple((member[1] for member in weights))
        for batch_slot in range(MB):
            segments = segment_ids[batch_slot]
            early = low(section_apply(section_inputs[batch_slot], segments, first_weights))
            early = early + between[batch_slot]
            late = section_apply(early, segments, last_weights)
            firsts.append(early)
            lasts.append(late)
        return (jnp.stack(firsts), jnp.stack(lasts))
    (firsts, lasts), pullback = jax.vjp(forward, weights, section_inputs, between)
    grad_weights, grad_inputs, grad_between = pullback((jnp.zeros_like(firsts), cotangent.astype(jnp.float32)))
    layer_out = jnp.stack([firsts, lasts]).astype(jnp.bfloat16)
    input_grad = jnp.stack([grad_inputs, grad_between]).astype(jnp.bfloat16)
    return (layer_out, input_grad, grad_weights[0], grad_weights[1], grad_weights[2], grad_weights[3], grad_weights[4], grad_weights[5], grad_weights[6])
```

```python
import functools

import jax
import jax.numpy as jnp
from jax import lax
from jax.experimental import pallas as pl
from jax.experimental.pallas import tpu as pltpu
from jax.sharding import PartitionSpec as P

HQ, HK, HD = 15, 5, 64
D, QW, KW = 960, 960, 320
TOK, LEN = 128, 512
WA = 1024
QKVW = 1792
FROWS, AROWS = 480, 176
epsilon = 1e-05
rope_base = 100000.0
masked_score = -1e30
VMEM = 60 * 2**20
bf16, f32 = jnp.bfloat16, jnp.float32


def nn(a, b):
    return jnp.dot(a, b, preferred_element_type=f32)


def nt(a, b):
    return lax.dot_general(a, b, (((1,), (1,)), ((), ())), preferred_element_type=f32)


def tn(a, b):
    return lax.dot_general(a, b, (((0,), (0,)), ((), ())), preferred_element_type=f32)


def call(kernel, outs, ins, specs=None, scratch=(), grid=None, out_specs=None, name=None):
    vm = pl.BlockSpec(memory_space=pltpu.VMEM)
    kwargs = {}
    if grid is not None:
        kwargs["grid"] = grid
    return pl.pallas_call(
        kernel,
        out_shape=outs,
        in_specs=specs if specs is not None else [vm] * len(ins),
        out_specs=out_specs if out_specs is not None else [vm] * len(outs),
        scratch_shapes=list(scratch),
        compiler_params=pltpu.CompilerParams(vmem_limit_bytes=VMEM),
        name=name,
        **kwargs,
    )(*ins)


def sds(shape, dt):
    return jax.ShapeDtypeStruct(shape, dt)


def pick(sel_ref, own, recv, first, rows, buf, sem):
    @pl.when(sel_ref[0] == 0)
    def _():
        pltpu.make_async_copy(own.at[:, pl.ds(first, rows), :], buf, sem).start()

    @pl.when(sel_ref[0] != 0)
    def _():
        pltpu.make_async_copy(recv.at[:, pl.ds(first, rows), :], buf, sem).start()


def arrived(own, first, rows, buf, sem):
    pltpu.make_async_copy(own.at[:, pl.ds(first, rows), :], buf, sem).wait()


def chunk_of(buf, j):
    return buf[:, 16 * j : 16 * j + 16, :].reshape(WA, 256)


def rstd_of(v):
    return lax.rsqrt(jnp.sum(v * v, axis=1, keepdims=True) * (1.0 / D) + epsilon)


def lane_in_head(shape):
    return lax.broadcasted_iota(jnp.int32, shape, 1) % HD


def project_kernel(has_x, sel, own, recv, pab, pba, cosw, sinw, *rest):
    if has_x:
        x_ref, norm_ref, qkv_ref, kv_ref, gain_ref, buf, sem = rest
    else:
        mid_ref, yo_ref, yr_ref, x_out, norm_ref, qkv_ref, kv_ref, gain_ref, buf, sem = rest
    pick(sel, own, recv, 0, 112, buf, sem)
    if has_x:
        x = x_ref[...].astype(f32)
    else:
        xb = (mid_ref[...] + yo_ref[...] + yr_ref[...]).astype(bf16)
        x_out[...] = xb
        x = xb.astype(f32)
    rstd = rstd_of(x)
    arrived(own, 0, 112, buf, sem)
    gains = nn(chunk_of(buf, 6).astype(f32).T.astype(bf16), pba[...])[64:72, :]
    gain_ref[...] = gains
    normed = (x * rstd * gains[0:1, :]).astype(bf16)
    norm_b = nn(normed, pab[...]).astype(bf16)
    norm_ref[...] = norm_b
    proj = jnp.concatenate([nn(norm_b, chunk_of(buf, j)) for j in range(7)], axis=1)
    low = lane_in_head(proj.shape) < HD // 2
    turned = jnp.where(low, -pltpu.roll(proj, QKVW - 32, 1), pltpu.roll(proj, 32, 1))
    out = (proj * cosw[...] + turned * sinw[...]).astype(bf16)
    qkv_ref[...] = out
    kv_ref[...] = out[:, : 2 * KW]


def heads_of(ref, base, i):
    return jnp.concatenate([ref[:, base + HD * (3 * i + h) : base + HD * (3 * i + h + 1)] for h in range(3)], axis=0)


def softmax_terms(q3, kg, allowed3):
    scores = nt(q3, kg) * 0.125
    scores = jnp.where(allowed3, scores, masked_score)
    highest = jnp.max(scores, axis=1, keepdims=True)
    terms = jnp.exp(scores - highest)
    return terms / jnp.sum(terms, axis=1, keepdims=True)


def attend_kernel(sel, own, recv, qkv, r1, r2, r3, mask, x_ref, gain_ref, pnb, attb_ref, mid_ref, n2_ref, buf, kvs, att, sem):
    pick(sel, own, recv, 112, 64, buf, sem)
    for k, part in enumerate((r3, r2, r1)):
        kvs[TOK * k : TOK * k + TOK, :] = part[...]
    kvs[3 * TOK :, :] = qkv[:, : 2 * KW]
    allowed = mask[...] > 0.5
    allowed3 = jnp.concatenate([allowed] * 3, axis=0)
    for i in range(HK):
        kg = kvs[:, HD * i : HD * i + HD]
        vg = kvs[:, KW + HD * i : KW + HD * i + HD]
        probs = softmax_terms(heads_of(qkv, 2 * KW, i), kg, allowed3).astype(bf16)
        o3 = nn(probs, vg).astype(bf16)
        for h in range(3):
            lane = HD * (3 * i + h)
            att[:, lane : lane + HD] = o3[TOK * h : TOK * h + TOK, :]
    attb = nn(att[...], pnb[...]).astype(bf16)
    attb_ref[...] = attb
    arrived(own, 112, 64, buf, sem)
    out = jnp.concatenate([nn(attb, chunk_of(buf, j)) for j in range(4)], axis=1)
    mid = x_ref[...].astype(f32) + out
    mid_ref[...] = mid
    n2_ref[...] = (mid * rstd_of(mid) * gain_ref[1:2, :]).astype(bf16)


def hidden_parts(xs, wg, wu):
    gate = up = None
    for g in range(4):
        xg = xs[:, 256 * g : 256 * g + 256]
        a, b = nt(xg, wg[g].reshape(320, 256)), nt(xg, wu[g].reshape(320, 256))
        gate, up = (a, b) if g == 0 else (gate + a, up + b)
    return gate, up, 1.0 / (1.0 + jnp.exp(-gate))


def ffn_kernel(xo, xr, wg, wu, wd, yo, yr):
    j = pl.program_id(0)

    @pl.when(j == 0)
    def _():
        yo[...] = jnp.zeros_like(yo)
        yr[...] = jnp.zeros_like(yr)

    xs = jnp.concatenate([xo[...], xr[...]], axis=0)
    gate, up, sigma = hidden_parts(xs, wg, wu)
    hidden = (gate * sigma * up).astype(bf16)
    for g in range(4):
        y = nn(hidden, wd[g].reshape(320, 256))
        yo[:, 256 * g : 256 * g + 256] += y[:TOK]
        yr[:, 256 * g : 256 * g + 256] += y[TOK:]


def ffn_back_kernel(xo, xr, do, dr, wg, wu, wd, grads, no, nr):
    j = pl.program_id(0)

    @pl.when(j == 0)
    def _():
        no[...] = jnp.zeros_like(no)
        nr[...] = jnp.zeros_like(nr)

    xs = jnp.concatenate([xo[...], xr[...]], axis=0)
    ds = jnp.concatenate([do[...], dr[...]], axis=0)
    gate, up, sigma = hidden_parts(xs, wg, wu)
    hidden = gate * sigma * up
    d_hidden = None
    for g in range(4):
        a = nt(ds[:, 256 * g : 256 * g + 256], wd[g].reshape(320, 256))
        d_hidden = a if g == 0 else d_hidden + a
    d_gate = (d_hidden * up * sigma * (1.0 + gate * (1.0 - sigma))).astype(bf16)
    d_up = (d_hidden * gate * sigma).astype(bf16)
    hid_t = hidden.astype(bf16).T
    dg_t = d_gate.T
    du_t = d_up.T
    for g in range(4):
        xg = xs[:, 256 * g : 256 * g + 256]
        grads[g, :, 0:80, :] = nn(dg_t, xg).astype(bf16).reshape(4, 80, 256)
        grads[g, :, 80:160, :] = nn(du_t, xg).astype(bf16).reshape(4, 80, 256)
        grads[g, :, 160:240, :] = nn(hid_t, ds[:, 256 * g : 256 * g + 256]).astype(bf16).reshape(4, 80, 256)
        dn = nn(d_gate, wg[g].reshape(320, 256)) + nn(d_up, wu[g].reshape(320, 256))
        no[:, 256 * g : 256 * g + 256] += dn[:TOK]
        nr[:, 256 * g : 256 * g + 256] += dn[TOK:]


def norm_back(e, z, rstd):
    return rstd * (e - z * (jnp.sum(e * z, axis=1, keepdims=True) * (1.0 / D)))


def attend_back_kernel(
    sel, own, recv, no, nr, mid_ref, gain_ref, dy_ref, qkv, r1, r2, r3, mask, pnb,
    dmid_ref, dproj_ref, gg_ref, dq_ref, dkv_ref, d1, d2, d3, buf, kvs, dkv, sem,
):
    pick(sel, own, recv, 112, 64, buf, sem)
    for k, part in enumerate((r3, r2, r1)):
        kvs[TOK * k : TOK * k + TOK, :] = part[...]
    kvs[3 * TOK :, :] = qkv[:, : 2 * KW]
    mid = mid_ref[...]
    rstd = rstd_of(mid)
    z = mid * rstd
    dn = no[...] + nr[...]
    gg_ref[...] = jnp.broadcast_to(jnp.sum(dn * z, axis=0, keepdims=True), gg_ref.shape)
    dmid = dy_ref[...].astype(f32) + norm_back(dn * gain_ref[1:2, :], z, rstd)
    dmid_ref[...] = dmid
    dproj = dmid.astype(bf16)
    dproj_ref[...] = dproj
    arrived(own, 112, 64, buf, sem)
    datt = None
    for j in range(4):
        a = nt(dproj[:, 256 * j : 256 * j + 256], chunk_of(buf, j))
        datt = a if j == 0 else datt + a
    datt = nt(datt.astype(bf16), pnb[...]).astype(bf16)
    allowed = mask[...] > 0.5
    allowed3 = jnp.concatenate([allowed] * 3, axis=0)
    dq_ref[:, 896:] = jnp.zeros((TOK, 256), f32)
    for i in range(HK):
        kg = kvs[:, HD * i : HD * i + HD]
        vg = kvs[:, KW + HD * i : KW + HD * i + HD]
        q3 = heads_of(qkv, 2 * KW, i)
        do3 = jnp.concatenate([datt[:, HD * (3 * i + h) : HD * (3 * i + h + 1)] for h in range(3)], axis=0)
        probs = softmax_terms(q3, kg, allowed3)
        d_probs = nt(do3, vg)
        inner = jnp.sum(probs * d_probs, axis=1, keepdims=True)
        d_scores = (probs * (d_probs - inner)).astype(bf16)
        dq3 = nn(d_scores, kg) * 0.125
        for h in range(3):
            lane = HD * (3 * i + h)
            dq_ref[:, lane : lane + HD] = dq3[TOK * h : TOK * h + TOK, :]
        dkv[:, HD * i : HD * i + HD] = tn(d_scores, q3) * 0.125
        dkv[:, KW + HD * i : KW + HD * i + HD] = tn(probs.astype(bf16), do3)
    dkv_ref[...] = dkv[3 * TOK :, :]
    for k, part in enumerate((d3, d2, d1)):
        part[...] = dkv[TOK * k : TOK * k + TOK, :].astype(bf16)


def split3(v):
    hi = v.astype(bf16)
    rest = v - hi.astype(f32)
    middle = rest.astype(bf16)
    return hi, middle, (rest - middle.astype(f32)).astype(bf16)


def project_back_kernel(
    sel, own, recv, dq, dkv, e1, e2, e3, cosw, sinw, norm_ref, x_ref, gain_ref, dmid_ref, pba, attb, dproj, gg,
    dx_ref, grads, buf, sem,
):
    pick(sel, own, recv, 0, 112, buf, sem)
    kv = dkv[...] + e1[...].astype(f32) + e2[...].astype(f32) + e3[...].astype(f32)
    d = jnp.concatenate([kv, dq[...]], axis=1)
    low = lane_in_head(d.shape) < HD // 2
    scaled = d * sinw[...]
    turned = jnp.where(low, pltpu.roll(scaled, QKVW - 32, 1), -pltpu.roll(scaled, 32, 1))
    dp = (d * cosw[...] + turned).astype(bf16)
    arrived(own, 0, 112, buf, sem)
    dn_b = None
    for j in range(7):
        a = nt(dp[:, 256 * j : 256 * j + 256], chunk_of(buf, j))
        dn_b = a if j == 0 else dn_b + a
    hi, middle, lo = split3(dn_b)
    dn = nn(hi, pba[...]) + nn(middle, pba[...]) + nn(lo, pba[...])
    x = x_ref[...].astype(f32)
    rstd = rstd_of(x)
    z = x * rstd
    g1 = jnp.sum(dn * z, axis=0, keepdims=True)
    dx_ref[...] = (dmid_ref[...] + norm_back(dn * gain_ref[0:1, :], z, rstd)).astype(bf16)
    row = lax.broadcasted_iota(jnp.int32, (256, WA), 0)
    gains = jnp.where(row == 64, g1, jnp.where(row == 65, gg[0:1, :], 0.0)).astype(bf16)
    norm_t = norm_ref[...].T
    for j in range(7):
        g = nn(norm_t, dp[:, 256 * j : 256 * j + 256])
        if j == 6:
            g = g + nt(pba[...], gains)
        grads[:, 16 * j : 16 * j + 16, :] = g.astype(bf16).reshape(64, 16, 256)
    att_t = attb[...].T
    for j in range(4):
        g = nn(att_t, dproj[:, 256 * j : 256 * j + 256])
        grads[:, 112 + 16 * j : 128 + 16 * j, :] = g.astype(bf16).reshape(64, 16, 256)
    grads[:, 176:192, :] = jnp.zeros((64, 16, 256), bf16)


VM = pl.BlockSpec(memory_space=pltpu.VMEM)
ANY = pl.BlockSpec(memory_space=pl.ANY)
SM = pl.BlockSpec(memory_space=pltpu.SMEM)


def weight_scratch(rows):
    return pltpu.VMEM((64, rows, 256), bf16)


def project(sel, own, recv, pab, pba, cosw, sinw, x=None, parts=None):
    outs = [sds((TOK, WA), bf16), sds((TOK, QKVW), bf16), sds((TOK, 2 * KW), bf16), sds((8, WA), f32)]
    ins = [sel, own, recv, pab, pba, cosw, sinw] + ([x] if parts is None else list(parts))
    if parts is not None:
        outs = [sds((TOK, WA), bf16)] + outs
    res = call(
        functools.partial(project_kernel, parts is None),
        outs, ins, [SM, ANY, ANY] + [VM] * (len(ins) - 3),
        [weight_scratch(112), pltpu.SemaphoreType.DMA], name="project",
    )
    return ([x] + list(res)) if parts is None else res


def attend(sel, own, recv, qkv, chunks, mask, x, gains, pnb):
    ins = [sel, own, recv, qkv, *chunks, mask, x, gains, pnb]
    return call(
        attend_kernel,
        [sds((TOK, WA), bf16), sds((TOK, WA), f32), sds((TOK, WA), bf16)],
        ins, [SM, ANY, ANY] + [VM] * (len(ins) - 3),
        [weight_scratch(64), pltpu.VMEM((LEN, 2 * KW), bf16), pltpu.VMEM((TOK, QW), bf16), pltpu.SemaphoreType.DMA],
        name="attend",
    )


def weight_specs(section):
    return [pl.BlockSpec((4, 4, 80, 256), lambda j, m=m: (0, j, 3 * section + m, 0)) for m in range(3)]


def whole(shape):
    return pl.BlockSpec(shape, lambda j: (0,) * len(shape))


def ffn(section, xo, xr, packed):
    row = whole((TOK, WA))
    return call(
        ffn_kernel, [sds((TOK, WA), f32)] * 2, [xo, xr, packed, packed, packed],
        [row, row] + weight_specs(section), grid=(4,), out_specs=[row, row], name="ffn",
    )


def ffn_back(section, xo, xr, do, dr, packed):
    row = whole((TOK, WA))
    return call(
        ffn_back_kernel, [sds((4, 16, 240, 256), bf16)] + [sds((TOK, WA), f32)] * 2,
        [xo, xr, do, dr, packed, packed, packed],
        [row] * 4 + weight_specs(section), grid=(4,),
        out_specs=[pl.BlockSpec((4, 4, 240, 256), lambda j: (0, j, 0, 0)), row, row], name="ffn_back",
    )


def attend_back(sel, own, recv, no, nr, mid, gains, dy, qkv, chunks, mask, pnb):
    ins = [sel, own, recv, no, nr, mid, gains, dy, qkv, *chunks, mask, pnb]
    small = sds((TOK, 2 * KW), bf16)
    return call(
        attend_back_kernel,
        [sds((TOK, WA), f32), sds((TOK, WA), bf16), sds((8, WA), f32), sds((TOK, 1152), f32), sds((TOK, 2 * KW), f32), small, small, small],
        ins, [SM, ANY, ANY] + [VM] * (len(ins) - 3),
        [weight_scratch(64), pltpu.VMEM((LEN, 2 * KW), bf16), pltpu.VMEM((LEN, 2 * KW), f32), pltpu.SemaphoreType.DMA],
        name="attend_back",
    )


def project_back(sel, own, recv, *rest):
    ins = [sel, own, recv, *rest]
    return call(
        project_back_kernel, [sds((TOK, WA), bf16), sds((64, 192, 256), bf16)],
        ins, [SM, ANY, ANY] + [VM] * (len(ins) - 3),
        [weight_scratch(112), pltpu.SemaphoreType.DMA], name="project_back",
    )


def other_core(v):
    return lax.ppermute(v, "section", [(0, 1), (1, 0)])


def shift_perm(name, k):
    if name == "x":
        return "gx", [(i, (i + k) % 4) for i in range(4)]
    if name == "z":
        return "gy", [(i, (i + 4 * k) % 16) for i in range(16)]
    return "gy", [(i, (i // 4) * 4 + (i % 4 + k) % 4) for i in range(16)]


def reduce_stage(v, dim, name, me):
    got = []
    for k in (1, 3, 2):
        piece = lax.dynamic_index_in_dim(v, (me + k) % 4, dim, keepdims=False)
        axis, perm = shift_perm(name, k)
        got.append(lax.ppermute(piece, axis, perm))
    total = lax.dynamic_index_in_dim(v, me, dim, keepdims=False).astype(f32)
    for piece in got:
        total = total + piece.astype(f32)
    return total.astype(bf16)


def reduce_parts(parts, place):
    names = ["x", "z", "y"]
    orders = [["x", "y", "z"], ["y", "z", "x"], ["z", "x", "y"]]
    state = [(p, list(names)) for p in parts]
    for step in range(3):
        after = []
        for index, (v, left) in enumerate(state):
            name = orders[index % 3][step]
            dim = left.index(name)
            v = reduce_stage(v, dim, name, place[name])
            after.append((v, [n for n in left if n != name]))
        state = after
    return [v for v, _ in state]


def rope_tables(positions):
    frequency = rope_base ** (-(jnp.arange(HD // 2, dtype=f32) * 2.0) / HD)
    angles = positions.astype(f32)[:, None] * frequency[None, :]
    cosine, sine = jnp.cos(angles), jnp.sin(angles)
    cosine, sine = jnp.concatenate([cosine, cosine], 1), jnp.concatenate([sine, sine], 1)

    def wide(table, plain):
        rest = jnp.full((TOK, KW), plain, f32)
        return jnp.concatenate([jnp.tile(table, (1, HK)), rest, jnp.tile(table, (1, HQ)), jnp.full((TOK, 192), plain, f32)], 1)

    return wide(cosine, 1.0), wide(sine, 0.0)


def to_a(v):
    rows = v.shape[0]
    return jnp.pad(v.reshape(rows, 4, 240), ((0, 0), (0, 0), (0, 16))).reshape(rows, WA)


def from_a(v):
    return v.reshape(v.shape[:-1] + (4, 256))[..., :240].reshape(v.shape[:-1] + (D,))


def place_matrices():
    a = jnp.arange(WA, dtype=jnp.int32)
    in_a = jnp.where(a % 256 < 240, (a // 256) * 240 + a % 256, -1)
    in_b = jnp.where(a % 16 < 15, (a // 16) * 15 + a % 16, -2)
    pab = (in_a[:, None] == in_b[None, :]).astype(bf16)
    pba = (in_b[:, None] == in_a[None, :]).astype(bf16)
    pnb = (jnp.arange(QW, dtype=jnp.int32)[:, None] == in_b[None, :]).astype(bf16)
    return pab, pba, pnb


def per_device(inputs, cotangent, segment_ids, gain_attn, w_qkv, w_out, gain_ffn, w_gate, w_up, w_down):
    core = lax.axis_index("section")
    gx = lax.axis_index("gx")
    gy = lax.axis_index("gy")
    first = core == 0
    place = {"x": gx, "z": gy // 4, "y": gy % 4}

    pieces = jnp.stack([w_gate[0].T, w_up[0].T, w_down[0]]).reshape(3, 2, 80, 240)
    keep = jnp.where(first, pieces[:, 0], pieces[:, 1])
    got = other_core(jnp.where(first, pieces[:, 1], pieces[:, 0]))
    halves = jnp.concatenate([jnp.where(first, keep, got), jnp.where(first, got, keep)], 0)
    halves = jnp.pad(halves.reshape(FROWS, 240), ((0, 0), (0, 16)))
    attn = jnp.concatenate(
        [
            w_qkv[0][:, QW:],
            w_qkv[0][:, :QW],
            gain_attn[0][:, None],
            gain_ffn[0][:, None],
            jnp.zeros((15, 190), bf16),
            to_a(w_out[0]),
        ],
        1,
    )
    attn = jnp.pad(attn, ((0, 1), (0, 0))).reshape(16, 11, 256).transpose(1, 0, 2).reshape(AROWS, 256)
    packed = lax.all_gather(jnp.concatenate([halves, attn], 0)[None], ("gx", "gy"), axis=0, tiled=True)
    own = packed[:, FROWS:, :]
    recv = other_core(own)
    packed = packed.reshape(4, 16, FROWS + AROWS, 256)

    own_in = to_a(jnp.where(first, inputs[0, 0], inputs[1, 0]))
    cot0, cot1 = to_a(cotangent[0, 0]), to_a(cotangent[1, 0])
    cot_own, cot_other = jnp.where(first, cot0, cot1), jnp.where(first, cot1, cot0)
    segments = jnp.where(first, segment_ids[0, 0], segment_ids[1, 0])
    local_ids = lax.dynamic_slice_in_dim(segments, gx * TOK, TOK, 0)
    own_index = gx * TOK + jnp.arange(TOK, dtype=jnp.int32)
    doc_start = jnp.sum((segments[None, :] < local_ids[:, None]).astype(jnp.int32), axis=1)
    key_index = (gx - 3) * TOK + jnp.arange(LEN, dtype=jnp.int32)
    key_ids = lax.dynamic_slice_in_dim(jnp.pad(segments, (3 * TOK, 0), constant_values=-1), gx * TOK, LEN, 0)
    mask = ((local_ids[:, None] == key_ids[None, :]) & (key_index[None, :] <= own_index[:, None])).astype(f32)
    cosw, sinw = rope_tables(own_index - doc_start)
    pab, pba, pnb = place_matrices()

    def ahead(v, k):
        return lax.ppermute(v, "gx", [(i, i + k) for i in range(4 - k)])

    def back(v, k):
        return lax.ppermute(v, "gx", [(i + k, i) for i in range(4 - k)])

    sels = [core[None].astype(jnp.int32), (1 - core)[None].astype(jnp.int32)]
    kept = []
    x, parts = own_in, None
    for section in range(2):
        sel = sels[section]
        x, norm_b, qkv, kv, gains = project(sel, own, recv, pab, pba, cosw, sinw, x, parts)
        chunks = [ahead(kv, 1), ahead(kv, 2), ahead(kv, 3)]
        attb, mid, n2 = attend(sel, own, recv, qkv, chunks, mask, x, gains, pnb)
        n2_other = other_core(n2)
        yo, yr = ffn(section, n2, n2_other, packed)
        parts = (mid, yo, other_core(yr))
        kept.append((x, norm_b, qkv, gains, chunks, attb, mid, n2, n2_other))
    outs = [kept[1][0], (parts[0] + parts[1] + parts[2]).astype(bf16)]

    dy, dy_other = cot_own, cot_other
    grads_in, ffn_grads, attn_grads = [None, None], [None, None], [None, None]
    for section in (1, 0):
        sel = sels[section]
        x, norm_b, qkv, gains, chunks, attb, mid, n2, n2_other = kept[section]
        ffn_grads[section], no, nr = ffn_back(section, n2, n2_other, dy, dy_other, packed)
        dmid, dproj, gg, dq, dkv, d1, d2, d3 = attend_back(
            sel, own, recv, no, other_core(nr), mid, gains, dy, qkv, chunks, mask, pnb
        )
        dy, attn_grads[section] = project_back(
            sel, own, recv, dq, dkv, back(d1, 1), back(d2, 2), back(d3, 3),
            cosw, sinw, norm_b, x, gains, dmid, pba, attb, dproj, gg,
        )
        grads_in[section] = dy
        if section == 1:
            dy_other = other_core(dy)

    late = lax.psum_scatter(ffn_grads[1], "gx", scatter_dimension=0, tiled=True)
    late = lax.psum_scatter(late[0], "gy", scatter_dimension=0, tiled=True)[0]

    def half_sum(v):
        send = lax.dynamic_slice_in_dim(v, (1 - core) * 96, 96, 1)
        mine = lax.dynamic_slice_in_dim(v, core * 96, 96, 1)
        return (mine.astype(f32) + other_core(send).astype(f32)).astype(bf16)

    halved = [half_sum(attn_grads[0]), half_sum(attn_grads[1])]
    early = ffn_grads[0].reshape(64, 240, 256)
    chunks = [
        jnp.concatenate([early[:, :144]], 1),
        jnp.concatenate([early[:, 144:], halved[0][:, :48]], 1),
        jnp.concatenate([halved[0][:, 48:], halved[1]], 1),
    ]
    done = reduce_parts([c.reshape(4, 4, 4, 144, 256) for c in chunks], place)
    flat = jnp.concatenate(done, 0)
    half = [jnp.concatenate([flat[:240], flat[240:336]], 0), jnp.concatenate([late, flat[336:432]], 0)]
    mine = jnp.where(first, half[0], half[1])
    theirs = other_core(jnp.where(first, half[1], half[0]))
    low, high = jnp.where(first, mine, theirs), jnp.where(first, theirs, mine)
    ff = jnp.concatenate([low[:240].reshape(3, 80, 256), high[:240].reshape(3, 80, 256)], 1)[:, :, :240].astype(f32)
    at = jnp.concatenate([low[240:], high[240:]], 0).reshape(12, 16, 256)[:, :15].astype(f32)
    qkv_grad = at[:7].transpose(1, 0, 2).reshape(15, QKVW)
    out_grad = at[7:11].transpose(1, 0, 2)[:, :, :240].reshape(15, D)
    grad_qkv = jnp.concatenate([qkv_grad[:, 2 * KW : 1600], qkv_grad[:, : 2 * KW]], 1)

    def placed(pair):
        a = jnp.where(first, pair[0], pair[1])
        b = other_core(jnp.where(first, pair[1], pair[0]))
        both = jnp.stack([jnp.where(first, a, b), jnp.where(first, b, a)])
        return from_a(both)[None, :, None]

    return (
        placed(outs),
        placed(grads_in),
        qkv_grad[:, 1600][None],
        grad_qkv[None],
        out_grad[None],
        qkv_grad[:, 1601][None],
        ff[0].T[None],
        ff[1].T[None],
        ff[2][None],
    )


def solution(mesh):
    return jax.shard_map(
        per_device,
        mesh=mesh,
        in_specs=(
            P(None, "gy", "gx", None),
            P(None, "gy", "gx", None),
            P(None, "gy", None),
            P("section", ("gx", "gy")),
            P("section", ("gx", "gy"), None),
            P("section", ("gx", "gy"), None),
            P("section", ("gx", "gy")),
            P("section", "gx", "gy"),
            P("section", "gx", "gy"),
            P("section", "gy", "gx"),
        ),
        out_specs=(
            P("section", None, "gy", "gx", None),
            P("section", None, "gy", "gx", None),
            P("section", ("gx", "gy")),
            P("section", ("gx", "gy"), None),
            P("section", ("gx", "gy"), None),
            P("section", ("gx", "gy")),
            P("section", "gx", "gy"),
            P("section", "gx", "gy"),
            P("section", "gy", "gx"),
        ),
        check_vma=False,
    )
```

```python
import functools

import jax
import jax.numpy as jnp
from jax import lax
from jax.experimental import pallas as pl
from jax.experimental.pallas import tpu as pltpu
from jax.sharding import PartitionSpec as P

HQ, HK, HD = 15, 5, 64
D, QW, KW = 960, 960, 320
TOK, LEN = 128, 512
WA = 1024
QKVW = 1792
FROWS, AROWS = 480, 176
epsilon = 1e-05
rope_base = 100000.0
masked_score = -1e30
VMEM = 60 * 2**20
bf16, f32 = jnp.bfloat16, jnp.float32


def nn(a, b):
    return jnp.dot(a, b, preferred_element_type=f32)


def nt(a, b):
    return lax.dot_general(a, b, (((1,), (1,)), ((), ())), preferred_element_type=f32)


def tn(a, b):
    return lax.dot_general(a, b, (((0,), (0,)), ((), ())), preferred_element_type=f32)


def call(kernel, outs, ins, specs=None, scratch=(), grid=None, out_specs=None, name=None):
    vm = pl.BlockSpec(memory_space=pltpu.VMEM)
    kwargs = {}
    if grid is not None:
        kwargs["grid"] = grid
    return pl.pallas_call(
        kernel,
        out_shape=outs,
        in_specs=specs if specs is not None else [vm] * len(ins),
        out_specs=out_specs if out_specs is not None else [vm] * len(outs),
        scratch_shapes=list(scratch),
        compiler_params=pltpu.CompilerParams(vmem_limit_bytes=VMEM),
        name=name,
        **kwargs,
    )(*ins)


def sds(shape, dt):
    return jax.ShapeDtypeStruct(shape, dt)


def pick(sel_ref, own, recv, buf, sems):
    def start(sources):
        row = 0
        for i, source in enumerate(sources):
            rows = source.shape[1]
            pltpu.make_async_copy(source, buf.at[:, pl.ds(row, rows), :], sems.at[i]).start()
            row += rows

    @pl.when(sel_ref[0] == 0)
    def _():
        start(own)

    @pl.when(sel_ref[0] != 0)
    def _():
        start(recv)


def arrived(own, buf, sems):
    row = 0
    for i, source in enumerate(own):
        rows = source.shape[1]
        pltpu.make_async_copy(source, buf.at[:, pl.ds(row, rows), :], sems.at[i]).wait()
        row += rows


def chunk_of(buf, j):
    return buf[:, 16 * j : 16 * j + 16, :].reshape(WA, 256)


def rstd_of(v):
    return lax.rsqrt(jnp.sum(v * v, axis=1, keepdims=True) * (1.0 / D) + epsilon)


def lane_in_head(shape):
    return lax.broadcasted_iota(jnp.int32, shape, 1) % HD


def project_kernel(has_x, sel, own_a, own_b, recv_a, recv_b, pab, pba, cosw, sinw, *rest):
    if has_x:
        x_ref, norm_ref, qkv_ref, kv_ref, gain_ref, buf, sems = rest
    else:
        mid_ref, yo_ref, yr_ref, x_out, norm_ref, qkv_ref, kv_ref, gain_ref, buf, sems = rest
    pick(sel, (own_a, own_b), (recv_a, recv_b), buf, sems)
    if has_x:
        x = x_ref[...].astype(f32)
    else:
        xb = (mid_ref[...] + yo_ref[...] + yr_ref[...]).astype(bf16)
        x_out[...] = xb
        x = xb.astype(f32)
    rstd = rstd_of(x)
    arrived((own_a, own_b), buf, sems)
    gains = nn(chunk_of(buf, 6).astype(f32).T.astype(bf16), pba[...])[64:72, :]
    gain_ref[...] = gains
    normed = (x * rstd * gains[0:1, :]).astype(bf16)
    norm_b = nn(normed, pab[...]).astype(bf16)
    norm_ref[...] = norm_b
    proj = jnp.concatenate([nn(norm_b, chunk_of(buf, j)) for j in range(7)], axis=1)
    low = lane_in_head(proj.shape) < HD // 2
    turned = jnp.where(low, -pltpu.roll(proj, QKVW - 32, 1), pltpu.roll(proj, 32, 1))
    out = (proj * cosw[...] + turned * sinw[...]).astype(bf16)
    qkv_ref[...] = out
    kv_ref[...] = out[:, : 2 * KW]


def heads_of(ref, base, i):
    return jnp.concatenate([ref[:, base + HD * (3 * i + h) : base + HD * (3 * i + h + 1)] for h in range(3)], axis=0)


def softmax_terms(q3, kg, allowed3):
    scores = nt(q3, kg) * 0.125
    scores = jnp.where(allowed3, scores, masked_score)
    highest = jnp.max(scores, axis=1, keepdims=True)
    terms = jnp.exp(scores - highest)
    return terms / jnp.sum(terms, axis=1, keepdims=True)


def attend_kernel(sel, own, recv, qkv, r1, r2, r3, mask, x_ref, gain_ref, pnb, attb_ref, mid_ref, n2_ref, buf, kvs, att, sems):
    pick(sel, (own,), (recv,), buf, sems)
    for k, part in enumerate((r3, r2, r1)):
        kvs[TOK * k : TOK * k + TOK, :] = part[...]
    kvs[3 * TOK :, :] = qkv[:, : 2 * KW]
    allowed = mask[...] > 0.5
    allowed3 = jnp.concatenate([allowed] * 3, axis=0)
    for i in range(HK):
        kg = kvs[:, HD * i : HD * i + HD]
        vg = kvs[:, KW + HD * i : KW + HD * i + HD]
        probs = softmax_terms(heads_of(qkv, 2 * KW, i), kg, allowed3).astype(bf16)
        o3 = nn(probs, vg).astype(bf16)
        for h in range(3):
            lane = HD * (3 * i + h)
            att[:, lane : lane + HD] = o3[TOK * h : TOK * h + TOK, :]
    attb = nn(att[...], pnb[...]).astype(bf16)
    attb_ref[...] = attb
    arrived((own,), buf, sems)
    out = jnp.concatenate([nn(attb, chunk_of(buf, j)) for j in range(4)], axis=1)
    mid = x_ref[...].astype(f32) + out
    mid_ref[...] = mid
    n2_ref[...] = (mid * rstd_of(mid) * gain_ref[1:2, :]).astype(bf16)


def hidden_parts(xs, wg, wu):
    gate = up = None
    for g in range(4):
        xg = xs[:, 256 * g : 256 * g + 256]
        a, b = nt(xg, wg[g].reshape(320, 256)), nt(xg, wu[g].reshape(320, 256))
        gate, up = (a, b) if g == 0 else (gate + a, up + b)
    return gate, up, 1.0 / (1.0 + jnp.exp(-gate))


def ffn_kernel(xo, xr, wg, wu, wd, yo, yr):
    j = pl.program_id(0)

    @pl.when(j == 0)
    def _():
        yo[...] = jnp.zeros_like(yo)
        yr[...] = jnp.zeros_like(yr)

    xs = jnp.concatenate([xo[...], xr[...]], axis=0)
    gate, up, sigma = hidden_parts(xs, wg, wu)
    hidden = (gate * sigma * up).astype(bf16)
    for g in range(4):
        y = nn(hidden, wd[g].reshape(320, 256))
        yo[:, 256 * g : 256 * g + 256] += y[:TOK]
        yr[:, 256 * g : 256 * g + 256] += y[TOK:]


def ffn_back_kernel(xo, xr, do, dr, wg, wu, wd, grads, no, nr):
    j = pl.program_id(0)

    @pl.when(j == 0)
    def _():
        no[...] = jnp.zeros_like(no)
        nr[...] = jnp.zeros_like(nr)

    xs = jnp.concatenate([xo[...], xr[...]], axis=0)
    ds = jnp.concatenate([do[...], dr[...]], axis=0)
    gate, up, sigma = hidden_parts(xs, wg, wu)
    hidden = gate * sigma * up
    d_hidden = None
    for g in range(4):
        a = nt(ds[:, 256 * g : 256 * g + 256], wd[g].reshape(320, 256))
        d_hidden = a if g == 0 else d_hidden + a
    d_gate = (d_hidden * up * sigma * (1.0 + gate * (1.0 - sigma))).astype(bf16)
    d_up = (d_hidden * gate * sigma).astype(bf16)
    hid_t = hidden.astype(bf16).T
    dg_t = d_gate.T
    du_t = d_up.T
    for g in range(4):
        xg = xs[:, 256 * g : 256 * g + 256]
        grads[:, g, 0:80, :] = nn(dg_t, xg).astype(bf16).reshape(4, 80, 256)
        grads[:, g, 80:160, :] = nn(du_t, xg).astype(bf16).reshape(4, 80, 256)
        grads[:, g, 160:240, :] = nn(hid_t, ds[:, 256 * g : 256 * g + 256]).astype(bf16).reshape(4, 80, 256)
        dn = nn(d_gate, wg[g].reshape(320, 256)) + nn(d_up, wu[g].reshape(320, 256))
        no[:, 256 * g : 256 * g + 256] += dn[:TOK]
        nr[:, 256 * g : 256 * g + 256] += dn[TOK:]


def norm_back(e, z, rstd):
    return rstd * (e - z * (jnp.sum(e * z, axis=1, keepdims=True) * (1.0 / D)))


def attend_back_kernel(
    sel, own, recv, no, nr, mid_ref, gain_ref, dy_ref, qkv, r1, r2, r3, mask, pnb,
    dmid_ref, dproj_ref, gg_ref, dq_ref, dkv_ref, d1, d2, d3, buf, kvs, dkv, sems,
):
    pick(sel, (own,), (recv,), buf, sems)
    for k, part in enumerate((r3, r2, r1)):
        kvs[TOK * k : TOK * k + TOK, :] = part[...]
    kvs[3 * TOK :, :] = qkv[:, : 2 * KW]
    mid = mid_ref[...]
    rstd = rstd_of(mid)
    z = mid * rstd
    dn = no[...] + nr[...]
    gg_ref[...] = jnp.broadcast_to(jnp.sum(dn * z, axis=0, keepdims=True), gg_ref.shape)
    dmid = dy_ref[...].astype(f32) + norm_back(dn * gain_ref[1:2, :], z, rstd)
    dmid_ref[...] = dmid
    dproj = dmid.astype(bf16)
    dproj_ref[...] = dproj
    arrived((own,), buf, sems)
    datt = None
    for j in range(4):
        a = nt(dproj[:, 256 * j : 256 * j + 256], chunk_of(buf, j))
        datt = a if j == 0 else datt + a
    datt = nt(datt.astype(bf16), pnb[...]).astype(bf16)
    allowed = mask[...] > 0.5
    allowed3 = jnp.concatenate([allowed] * 3, axis=0)
    dq_ref[:, 896:] = jnp.zeros((TOK, 256), f32)
    for i in range(HK):
        kg = kvs[:, HD * i : HD * i + HD]
        vg = kvs[:, KW + HD * i : KW + HD * i + HD]
        q3 = heads_of(qkv, 2 * KW, i)
        do3 = jnp.concatenate([datt[:, HD * (3 * i + h) : HD * (3 * i + h + 1)] for h in range(3)], axis=0)
        probs = softmax_terms(q3, kg, allowed3)
        d_probs = nt(do3, vg)
        inner = jnp.sum(probs * d_probs, axis=1, keepdims=True)
        d_scores = (probs * (d_probs - inner)).astype(bf16)
        dq3 = nn(d_scores, kg) * 0.125
        for h in range(3):
            lane = HD * (3 * i + h)
            dq_ref[:, lane : lane + HD] = dq3[TOK * h : TOK * h + TOK, :]
        dkv[:, HD * i : HD * i + HD] = tn(d_scores, q3) * 0.125
        dkv[:, KW + HD * i : KW + HD * i + HD] = tn(probs.astype(bf16), do3)
    dkv_ref[...] = dkv[3 * TOK :, :]
    for k, part in enumerate((d3, d2, d1)):
        part[...] = dkv[TOK * k : TOK * k + TOK, :].astype(bf16)


def split3(v):
    hi = v.astype(bf16)
    rest = v - hi.astype(f32)
    middle = rest.astype(bf16)
    return hi, middle, (rest - middle.astype(f32)).astype(bf16)


def project_back_kernel(
    sel, own_a, own_b, recv_a, recv_b, dq, dkv, e1, e2, e3, cosw, sinw, norm_ref, x_ref, gain_ref, dmid_ref, pba, attb,
    dproj, gg, core, dx_ref, keep, send, buf, sems,
):
    pick(sel, (own_a, own_b), (recv_a, recv_b), buf, sems)
    kv = dkv[...] + e1[...].astype(f32) + e2[...].astype(f32) + e3[...].astype(f32)
    d = jnp.concatenate([kv, dq[...]], axis=1)
    low = lane_in_head(d.shape) < HD // 2
    scaled = d * sinw[...]
    turned = jnp.where(low, pltpu.roll(scaled, QKVW - 32, 1), -pltpu.roll(scaled, 32, 1))
    dp = (d * cosw[...] + turned).astype(bf16)
    arrived((own_a, own_b), buf, sems)
    dn_b = None
    for j in range(7):
        a = nt(dp[:, 256 * j : 256 * j + 256], chunk_of(buf, j))
        dn_b = a if j == 0 else dn_b + a
    hi, middle, lo = split3(dn_b)
    dn = nn(hi, pba[...]) + nn(middle, pba[...]) + nn(lo, pba[...])
    x = x_ref[...].astype(f32)
    rstd = rstd_of(x)
    z = x * rstd
    g1 = jnp.sum(dn * z, axis=0, keepdims=True)
    dx_ref[...] = (dmid_ref[...] + norm_back(dn * gain_ref[0:1, :], z, rstd)).astype(bf16)
    row = lax.broadcasted_iota(jnp.int32, (256, WA), 0)
    gains = jnp.where(row == 64, g1, jnp.where(row == 65, gg[0:1, :], 0.0)).astype(bf16)
    norm_t = norm_ref[...].T
    att_t = attb[...].T

    def put(target, j, g):
        target[:, 16 * (j % 6) : 16 * (j % 6) + 16, :] = g.astype(bf16).reshape(64, 16, 256)

    for j in range(12):
        if j < 7:
            g = nn(norm_t, dp[:, 256 * j : 256 * j + 256])
        elif j < 11:
            g = nn(att_t, dproj[:, 256 * (j - 7) : 256 * (j - 6)])
        else:
            g = jnp.zeros((WA, 256), f32)
        if j == 6:
            g = g + nt(pba[...], gains)
        pl.when(core[0] == j // 6)(functools.partial(put, keep, j, g))
        pl.when(core[0] != j // 6)(functools.partial(put, send, j, g))


VM = pl.BlockSpec(memory_space=pltpu.VMEM)
ANY = pl.BlockSpec(memory_space=pl.ANY)
SM = pl.BlockSpec(memory_space=pltpu.SMEM)


def weight_scratch(rows):
    return pltpu.VMEM((64, rows, 256), bf16)


def project(sel, own, recv, pab, pba, cosw, sinw, x=None, parts=None):
    outs = [sds((TOK, WA), bf16), sds((TOK, QKVW), bf16), sds((TOK, 2 * KW), bf16), sds((8, WA), f32)]
    ins = [sel, *own[:2], *recv[:2], pab, pba, cosw, sinw] + ([x] if parts is None else list(parts))
    if parts is not None:
        outs = [sds((TOK, WA), bf16)] + outs
    res = call(
        functools.partial(project_kernel, parts is None),
        outs, ins, [SM] + [ANY] * 4 + [VM] * (len(ins) - 5),
        [weight_scratch(112), pltpu.SemaphoreType.DMA((2,))], name="project",
    )
    return ([x] + list(res)) if parts is None else res


def attend(sel, own, recv, qkv, chunks, mask, x, gains, pnb):
    ins = [sel, own[2], recv[2], qkv, *chunks, mask, x, gains, pnb]
    return call(
        attend_kernel,
        [sds((TOK, WA), bf16), sds((TOK, WA), f32), sds((TOK, WA), bf16)],
        ins, [SM, ANY, ANY] + [VM] * (len(ins) - 3),
        [weight_scratch(64), pltpu.VMEM((LEN, 2 * KW), bf16), pltpu.VMEM((TOK, QW), bf16), pltpu.SemaphoreType.DMA((1,))],
        name="attend",
    )


def weight_specs(section):
    return [pl.BlockSpec((4, 4, 80, 256), lambda j, m=m: (0, j, 3 * section + m, 0)) for m in range(3)]


def whole(shape):
    return pl.BlockSpec(shape, lambda j: (0,) * len(shape))


def ffn(section, xo, xr, packed):
    row = whole((TOK, WA))
    return call(
        ffn_kernel, [sds((TOK, WA), f32)] * 2, [xo, xr, packed, packed, packed],
        [row, row] + weight_specs(section), grid=(4,), out_specs=[row, row], name="ffn",
    )


def ffn_back(section, xo, xr, do, dr, packed):
    row = whole((TOK, WA))
    return call(
        ffn_back_kernel, [sds((16, 4, 240, 256), bf16)] + [sds((TOK, WA), f32)] * 2,
        [xo, xr, do, dr, packed, packed, packed],
        [row] * 4 + weight_specs(section), grid=(4,),
        out_specs=[pl.BlockSpec((4, 4, 240, 256), lambda j: (j, 0, 0, 0)), row, row], name="ffn_back",
    )


def attend_back(sel, own, recv, no, nr, mid, gains, dy, qkv, chunks, mask, pnb):
    ins = [sel, own[2], recv[2], no, nr, mid, gains, dy, qkv, *chunks, mask, pnb]
    small = sds((TOK, 2 * KW), bf16)
    return call(
        attend_back_kernel,
        [sds((TOK, WA), f32), sds((TOK, WA), bf16), sds((8, WA), f32), sds((TOK, 1152), f32), sds((TOK, 2 * KW), f32), small, small, small],
        ins, [SM, ANY, ANY] + [VM] * (len(ins) - 3),
        [weight_scratch(64), pltpu.VMEM((LEN, 2 * KW), bf16), pltpu.VMEM((LEN, 2 * KW), f32), pltpu.SemaphoreType.DMA((1,))],
        name="attend_back",
    )


def project_back(sel, own, recv, core, *rest):
    ins = [sel, *own[:2], *recv[:2], *rest, core]
    return call(
        project_back_kernel, [sds((TOK, WA), bf16)] + [sds((64, 96, 256), bf16)] * 2,
        ins, [SM] + [ANY] * 4 + [VM] * (len(ins) - 6) + [SM],
        [weight_scratch(112), pltpu.SemaphoreType.DMA((2,))], name="project_back",
    )


def other_core(v):
    return lax.ppermute(v, "section", [(0, 1), (1, 0)])


def shift_perm(name, k):
    if name == "x":
        return "gx", [(i, (i + k) % 4) for i in range(4)]
    if name == "z":
        return "gy", [(i, (i + 4 * k) % 16) for i in range(16)]
    return "gy", [(i, (i // 4) * 4 + (i % 4 + k) % 4) for i in range(16)]


def permuted(v, name, k):
    axis, perm = shift_perm(name, k)
    return lax.ppermute(v, axis, perm)


ORDERS = (("x", "y", "z"), ("y", "z", "x"), ("z", "x", "y"))
GROUPS = (((0, 1), (0, 3), (1, 1), (1, 3), (2, 2)), ((0, 2), (1, 2), (2, 1), (2, 3)))


def exchange(pieces, names, grouped, beside=()):
    keys = list(pieces)
    pieces = dict(zip(keys, lax.optimization_barrier([pieces[key] for key in keys])))
    if not grouped:
        return {key: permuted(pieces[key], names[key[0]], key[1]) for key in keys}, beside
    got = {key: permuted(pieces[key], names[key[0]], key[1]) for key in GROUPS[0]}
    tied = lax.optimization_barrier([[got[key] for key in GROUPS[0]], [pieces[key] for key in GROUPS[1]], list(beside)])
    got = dict(zip(GROUPS[0], tied[0]))
    for key, piece in zip(GROUPS[1], tied[1]):
        got[key] = permuted(piece, names[key[0]], key[1])
    return got, tied[2]


def gather_chunks(chunks, beside):
    state = [(c, ()) for c in chunks]
    for step in range(3):
        names = [order[step] for order in ORDERS]
        pieces = {(c, k): state[c][0] for c in range(3) for k in (1, 2, 3)}
        got, tied = exchange(pieces, names, step == 2, beside)
        if step == 2:
            beside = tied
        after = []
        for c in range(3):
            v, have = state[c]
            have = tuple(n for n in ("z", "y", "x") if n in have or n == names[c])
            v = jnp.stack([v, got[(c, 3)], got[(c, 2)], got[(c, 1)]], axis=have.index(names[c]))
            after.append((v, have))
        state = after
    return [v.reshape((64,) + v.shape[3:]) for v, _ in state], beside


def reduce_bundles(bundles, place, last):
    left = [("z", "y", "x")] * 3
    for step in range(3):
        names = [order[step] for order in ORDERS]
        if step == 2:
            bundles[1] = bundles[1] + [last]
        pieces, mine = {}, []
        for c in range(3):
            dim = left[c].index(names[c])
            me = place[names[c]]

            def part(v, own_first, k):
                if own_first:
                    return lax.index_in_dim(v, k, dim, keepdims=False)
                return lax.dynamic_index_in_dim(v, (me + k) % 4, dim, keepdims=False)

            mine.append([part(v, own_first, 0) for v, own_first in bundles[c]])
            for k in (1, 2, 3):
                pieces[(c, k)] = jnp.concatenate([part(v, own_first, k) for v, own_first in bundles[c]], axis=-2)
        got, _ = exchange(pieces, names, step == 0)
        for c in range(3):
            row, summed = 0, []
            for v, (_, own_first) in zip(mine[c], bundles[c]):
                rows = v.shape[-2]
                total = v.astype(f32)
                for k in (1, 2, 3):
                    total = total + got[(c, k)][..., row : row + rows, :].astype(f32)
                row += rows
                summed.append((total.astype(bf16), own_first))
            bundles[c] = summed
            left[c] = tuple(n for n in left[c] if n != names[c])
    return [[v for v, _ in bundle] for bundle in bundles]


def rope_tables(positions):
    frequency = rope_base ** (-(jnp.arange(HD // 2, dtype=f32) * 2.0) / HD)
    angles = positions.astype(f32)[:, None] * frequency[None, :]
    cosine, sine = jnp.cos(angles), jnp.sin(angles)
    cosine, sine = jnp.concatenate([cosine, cosine], 1), jnp.concatenate([sine, sine], 1)

    def wide(table, plain):
        rest = jnp.full((TOK, KW), plain, f32)
        return jnp.concatenate([jnp.tile(table, (1, HK)), rest, jnp.tile(table, (1, HQ)), jnp.full((TOK, 192), plain, f32)], 1)

    return wide(cosine, 1.0), wide(sine, 0.0)


def to_a(v):
    rows = v.shape[0]
    return jnp.pad(v.reshape(rows, 4, 240), ((0, 0), (0, 0), (0, 16))).reshape(rows, WA)


def from_a(v):
    return v.reshape(v.shape[:-1] + (4, 256))[..., :240].reshape(v.shape[:-1] + (D,))


def place_matrices(place):
    a = jnp.arange(WA, dtype=jnp.int32)
    in_a = jnp.where(a % 256 < 240, (a // 256) * 240 + a % 256, -1)
    shard = a // 16
    x, z, y = (place["x"] + shard) % 4, (place["z"] + shard // 16) % 4, (place["y"] + shard // 4) % 4
    in_b = jnp.where(a % 16 < 15, (x * 16 + z * 4 + y) * 15 + a % 16, -2)
    pab = (in_a[:, None] == in_b[None, :]).astype(bf16)
    pba = (in_b[:, None] == in_a[None, :]).astype(bf16)
    pnb = (jnp.arange(QW, dtype=jnp.int32)[:, None] == in_b[None, :]).astype(bf16)
    return pab, pba, pnb


def per_device(inputs, cotangent, segment_ids, gain_attn, w_qkv, w_out, gain_ffn, w_gate, w_up, w_down):
    core = lax.axis_index("section")
    gx = lax.axis_index("gx")
    gy = lax.axis_index("gy")
    first = core == 0
    place = {"x": gx, "z": gy // 4, "y": gy % 4}

    pieces = jnp.stack([w_gate[0].T, w_up[0].T, w_down[0]]).reshape(3, 2, 80, 240)
    keep = jnp.where(first, pieces[:, 0], pieces[:, 1])
    got = other_core(jnp.where(first, pieces[:, 1], pieces[:, 0]))
    halves = jnp.concatenate([jnp.where(first, keep, got), jnp.where(first, got, keep)], 0)
    halves = jnp.pad(halves.reshape(FROWS, 240), ((0, 0), (0, 16)))
    attn = jnp.concatenate(
        [
            w_qkv[0][:, QW:],
            w_qkv[0][:, :QW],
            gain_attn[0][:, None],
            gain_ffn[0][:, None],
            jnp.zeros((15, 190), bf16),
            to_a(w_out[0]),
        ],
        1,
    )
    attn = jnp.pad(attn, ((0, 1), (0, 0))).reshape(16, 11, 256).transpose(1, 0, 2).reshape(AROWS, 256)
    packed = lax.all_gather(halves[None], ("gx", "gy"), axis=0, tiled=True).reshape(4, 16, FROWS, 256)

    own_in = to_a(jnp.where(first, inputs[0, 0], inputs[1, 0]))
    cot0, cot1 = to_a(cotangent[0, 0]), to_a(cotangent[1, 0])
    cot_own, cot_other = jnp.where(first, cot0, cot1), jnp.where(first, cot1, cot0)
    segments = jnp.where(first, segment_ids[0, 0], segment_ids[1, 0])
    local_ids = lax.dynamic_slice_in_dim(segments, gx * TOK, TOK, 0)
    own_index = gx * TOK + jnp.arange(TOK, dtype=jnp.int32)
    doc_start = jnp.sum((segments[None, :] < local_ids[:, None]).astype(jnp.int32), axis=1)
    key_index = (gx - 3) * TOK + jnp.arange(LEN, dtype=jnp.int32)
    key_ids = lax.dynamic_slice_in_dim(jnp.pad(segments, (3 * TOK, 0), constant_values=-1), gx * TOK, LEN, 0)
    mask = ((local_ids[:, None] == key_ids[None, :]) & (key_index[None, :] <= own_index[:, None])).astype(f32)
    cosw, sinw = rope_tables(own_index - doc_start)
    beside = [cosw, sinw, mask, own_in, cot_own, cot_other, *place_matrices(place)]
    own, beside = gather_chunks([attn[:64], attn[64:112], attn[112:]], beside)
    cosw, sinw, mask, own_in, cot_own, cot_other, pab, pba, pnb = beside
    recv = [other_core(w) for w in own]

    def ahead(v, k):
        return lax.ppermute(v, "gx", [(i, i + k) for i in range(4 - k)])

    def back(v, k):
        return lax.ppermute(v, "gx", [(i + k, i) for i in range(4 - k)])

    sels = [core[None].astype(jnp.int32), (1 - core)[None].astype(jnp.int32)]
    kept = []
    x, parts = own_in, None
    for section in range(2):
        sel = sels[section]
        x, norm_b, qkv, kv, gains = project(sel, own, recv, pab, pba, cosw, sinw, x, parts)
        chunks = [ahead(kv, 1), ahead(kv, 2), ahead(kv, 3)]
        attb, mid, n2 = attend(sel, own, recv, qkv, chunks, mask, x, gains, pnb)
        n2_other = other_core(n2)
        yo, yr = ffn(section, n2, n2_other, packed)
        parts = (mid, yo, other_core(yr))
        kept.append((x, norm_b, qkv, gains, chunks, attb, mid, n2, n2_other))
    outs = [kept[1][0], (parts[0] + parts[1] + parts[2]).astype(bf16)]

    dy, dy_other = cot_own, cot_other
    grads_in, ffn_grads, attn_grads = [None, None], [None, None], [None, None]
    for section in (1, 0):
        sel = sels[section]
        x, norm_b, qkv, gains, chunks, attb, mid, n2, n2_other = kept[section]
        ffn_grads[section], no, nr = ffn_back(section, n2, n2_other, dy, dy_other, packed)
        dmid, dproj, gg, dq, dkv, d1, d2, d3 = attend_back(
            sel, own, recv, no, other_core(nr), mid, gains, dy, qkv, chunks, mask, pnb
        )
        dy, keep, send = project_back(
            sel, own, recv, sels[0], dq, dkv, back(d1, 1), back(d2, 2), back(d3, 3),
            cosw, sinw, norm_b, x, gains, dmid, pba, attb, dproj, gg,
        )
        grads_in[section] = dy
        attn_grads[section] = (keep, other_core(send))
        if section == 1:
            dy_other = other_core(dy)

    late = lax.psum_scatter(ffn_grads[1].reshape(16, 960, 256), "gy", scatter_dimension=0, tiled=True).reshape(4, 240, 256)
    halved = []
    for keep, got in attn_grads:
        halved.append((keep.astype(f32) + got.astype(f32)).astype(bf16).reshape(4, 4, 4, 96, 256))
    early = ffn_grads[0].reshape(4, 4, 4, 240, 256)
    bundles = [
        [(early[..., :144, :], False)],
        [(early[..., 144:, :], False), (halved[0][..., :48, :], True)],
        [(halved[0][..., 48:, :], True), (halved[1], True)],
    ]
    (e0,), (e1, a0, late), (a1, b) = reduce_bundles(bundles, place, (late, False))
    half = [jnp.concatenate([e0, e1, a0, a1], 0), jnp.concatenate([late, b], 0)]
    mine = jnp.where(first, half[0], half[1])
    theirs = other_core(jnp.where(first, half[1], half[0]))
    low, high = jnp.where(first, mine, theirs), jnp.where(first, theirs, mine)
    ff = jnp.concatenate([low[:240].reshape(3, 80, 256), high[:240].reshape(3, 80, 256)], 1)[:, :, :240].astype(f32)
    at = jnp.concatenate([low[240:], high[240:]], 0).reshape(12, 16, 256)[:, :15].astype(f32)
    qkv_grad = at[:7].transpose(1, 0, 2).reshape(15, QKVW)
    out_grad = at[7:11].transpose(1, 0, 2)[:, :, :240].reshape(15, D)
    grad_qkv = jnp.concatenate([qkv_grad[:, 2 * KW : 1600], qkv_grad[:, : 2 * KW]], 1)

    def placed(pair):
        a = jnp.where(first, pair[0], pair[1])
        b = other_core(jnp.where(first, pair[1], pair[0]))
        both = jnp.stack([jnp.where(first, a, b), jnp.where(first, b, a)])
        return from_a(both)[None, :, None]

    return (
        placed(outs),
        placed(grads_in),
        qkv_grad[:, 1600][None],
        grad_qkv[None],
        out_grad[None],
        qkv_grad[:, 1601][None],
        ff[0].T[None],
        ff[1].T[None],
        ff[2][None],
    )


def solution(mesh):
    return jax.shard_map(
        per_device,
        mesh=mesh,
        in_specs=(
            P(None, "gy", "gx", None),
            P(None, "gy", "gx", None),
            P(None, "gy", None),
            P("section", ("gx", "gy")),
            P("section", ("gx", "gy"), None),
            P("section", ("gx", "gy"), None),
            P("section", ("gx", "gy")),
            P("section", "gx", "gy"),
            P("section", "gx", "gy"),
            P("section", "gy", "gx"),
        ),
        out_specs=(
            P("section", None, "gy", "gx", None),
            P("section", None, "gy", "gx", None),
            P("section", ("gx", "gy")),
            P("section", ("gx", "gy"), None),
            P("section", ("gx", "gy"), None),
            P("section", ("gx", "gy")),
            P("section", "gx", "gy"),
            P("section", "gx", "gy"),
            P("section", "gy", "gx"),
        ),
        check_vma=False,
    )
```

```python
import functools

import jax
import jax.numpy as jnp
from jax import lax
from jax.experimental import pallas as pl
from jax.experimental.pallas import tpu as pltpu
from jax.sharding import PartitionSpec as P

HQ, HK, HD = 15, 5, 64
D, QW, KW = 960, 960, 320
TOK, LEN = 128, 512
WA = 1024
QKVW = 1792
FROWS, AROWS = 480, 176
epsilon = 1e-05
rope_base = 100000.0
masked_score = -1e30
VMEM = 60 * 2**20
bf16, f32 = jnp.bfloat16, jnp.float32


def nn(a, b):
    return jnp.dot(a, b, preferred_element_type=f32)


def nt(a, b):
    return lax.dot_general(a, b, (((1,), (1,)), ((), ())), preferred_element_type=f32)


def tn(a, b):
    return lax.dot_general(a, b, (((0,), (0,)), ((), ())), preferred_element_type=f32)


def call(kernel, outs, ins, specs=None, scratch=(), grid=None, out_specs=None, name=None):
    vm = pl.BlockSpec(memory_space=pltpu.VMEM)
    kwargs = {}
    if grid is not None:
        kwargs["grid"] = grid
    return pl.pallas_call(
        kernel,
        out_shape=outs,
        in_specs=specs if specs is not None else [vm] * len(ins),
        out_specs=out_specs if out_specs is not None else [vm] * len(outs),
        scratch_shapes=list(scratch),
        compiler_params=pltpu.CompilerParams(vmem_limit_bytes=VMEM),
        name=name,
        **kwargs,
    )(*ins)


def sds(shape, dt):
    return jax.ShapeDtypeStruct(shape, dt)


def weight_copies(source, first, buf, sems):
    rows = buf.shape[2]
    return [
        pltpu.make_async_copy(source.at[pl.ds(16 * x, 16), pl.ds(first, rows), :], buf.at[:, x], sems.at[x])
        for x in range(4)
    ]


def pick(sel_ref, own, recv, first, buf, sems):
    @pl.when(sel_ref[0] == 0)
    def _():
        for copy in weight_copies(own, first, buf, sems):
            copy.start()

    @pl.when(sel_ref[0] != 0)
    def _():
        for copy in weight_copies(recv, first, buf, sems):
            copy.start()


def arrived(own, first, buf, sems):
    for copy in weight_copies(own, first, buf, sems):
        copy.wait()


def chunk_of(buf, j):
    return buf[:, :, 16 * j : 16 * j + 16, :].reshape(WA, 256)


def rstd_of(v):
    return lax.rsqrt(jnp.sum(v * v, axis=1, keepdims=True) * (1.0 / D) + epsilon)


def lane_in_head(shape):
    return lax.broadcasted_iota(jnp.int32, shape, 1) % HD


def rotated(v, cosw, sinw):
    low = lane_in_head(v.shape) < HD // 2
    turned = jnp.where(low, -pltpu.roll(v, v.shape[1] - 32, 1), pltpu.roll(v, 32, 1))
    return v * cosw[...] + turned * sinw[...]


def rotated_back(v, cosw, sinw):
    low = lane_in_head(v.shape) < HD // 2
    scaled = v * sinw[...]
    turned = jnp.where(low, pltpu.roll(scaled, v.shape[1] - 32, 1), -pltpu.roll(scaled, 32, 1))
    return v * cosw[...] + turned


def key_value_kernel(has_x, sel, own, recv, pab, pba, cosw, sinw, *rest):
    if has_x:
        x_ref, norm_ref, kv_ref, gain_ref, buf, sems = rest
    else:
        mid_ref, yo_ref, yr_ref, x_out, norm_ref, kv_ref, gain_ref, buf, sems = rest
    pick(sel, own, recv, 0, buf, sems)
    if has_x:
        x = x_ref[...].astype(f32)
    else:
        xb = (mid_ref[...] + yo_ref[...] + yr_ref[...]).astype(bf16)
        x_out[...] = xb
        x = xb.astype(f32)
    rstd = rstd_of(x)
    arrived(own, 0, buf, sems)
    gains = nn(chunk_of(buf, 2).astype(f32).T.astype(bf16), pba[...])[128:136, :]
    gain_ref[...] = gains
    normed = (x * rstd * gains[0:1, :]).astype(bf16)
    norm_b = nn(normed, pab[...]).astype(bf16)
    norm_ref[...] = norm_b
    proj = jnp.concatenate([nn(norm_b, chunk_of(buf, j)) for j in range(3)], axis=1)
    kv_ref[...] = rotated(proj, cosw, sinw).astype(bf16)[:, : 2 * KW]


def query_kernel(sel, own, recv, norm_ref, cosw, sinw, q_ref, buf, sems):
    pick(sel, own, recv, 48, buf, sems)
    arrived(own, 48, buf, sems)
    proj = jnp.concatenate([nn(norm_ref[...], chunk_of(buf, j)) for j in range(4)], axis=1)
    q_ref[...] = rotated(proj, cosw, sinw).astype(bf16)


def heads_of(ref, i):
    return jnp.concatenate([ref[:, HD * (3 * i + h) : HD * (3 * i + h + 1)] for h in range(3)], axis=0)


def softmax_terms(q3, kg, allowed3):
    scores = nt(q3, kg) * 0.125
    scores = jnp.where(allowed3, scores, masked_score)
    highest = jnp.max(scores, axis=1, keepdims=True)
    terms = jnp.exp(scores - highest)
    return terms / jnp.sum(terms, axis=1, keepdims=True)


def attend_kernel(sel, own, recv, q, kv, r1, r2, r3, mask, x_ref, gain_ref, pnb, attb_ref, mid_ref, n2_ref, buf, kvs, att, sems):
    pick(sel, own, recv, 112, buf, sems)
    for k, part in enumerate((r3, r2, r1)):
        kvs[TOK * k : TOK * k + TOK, :] = part[...]
    kvs[3 * TOK :, :] = kv[...]
    allowed = mask[...] > 0.5
    allowed3 = jnp.concatenate([allowed] * 3, axis=0)
    for i in range(HK):
        kg = kvs[:, HD * i : HD * i + HD]
        vg = kvs[:, KW + HD * i : KW + HD * i + HD]
        probs = softmax_terms(heads_of(q, i), kg, allowed3).astype(bf16)
        o3 = nn(probs, vg).astype(bf16)
        for h in range(3):
            lane = HD * (3 * i + h)
            att[:, lane : lane + HD] = o3[TOK * h : TOK * h + TOK, :]
    attb = nn(att[...], pnb[...]).astype(bf16)
    attb_ref[...] = attb
    arrived(own, 112, buf, sems)
    out = jnp.concatenate([nn(attb, chunk_of(buf, j)) for j in range(4)], axis=1)
    mid = x_ref[...].astype(f32) + out
    mid_ref[...] = mid
    n2_ref[...] = (mid * rstd_of(mid) * gain_ref[1:2, :]).astype(bf16)


def tile_of(w, g, section):
    return (w[:, g] if section == 0 else w[g]).reshape(320, 256)


def hidden_parts(xs, wg, wu, section):
    gate = up = None
    for g in range(4):
        xg = xs[:, 256 * g : 256 * g + 256]
        a, b = nt(xg, tile_of(wg, g, section)), nt(xg, tile_of(wu, g, section))
        gate, up = (a, b) if g == 0 else (gate + a, up + b)
    return gate, up, 1.0 / (1.0 + jnp.exp(-gate))


def ffn_kernel(section, xo, xr, wg, wu, wd, yo, yr):
    j = pl.program_id(0)

    @pl.when(j == 0)
    def _():
        yo[...] = jnp.zeros_like(yo)
        yr[...] = jnp.zeros_like(yr)

    xs = jnp.concatenate([xo[...], xr[...]], axis=0)
    gate, up, sigma = hidden_parts(xs, wg, wu, section)
    hidden = (gate * sigma * up).astype(bf16)
    for g in range(4):
        y = nn(hidden, tile_of(wd, g, section))
        yo[:, 256 * g : 256 * g + 256] += y[:TOK]
        yr[:, 256 * g : 256 * g + 256] += y[TOK:]


def ffn_back_kernel(section, xo, xr, do, dr, wg, wu, wd, *outs):
    *grads, no, nr = outs
    places = [(grads[0], 80 * m) for m in range(3)] if len(grads) == 1 else [(g, 0) for g in grads]
    j = pl.program_id(0)

    @pl.when(j == 0)
    def _():
        no[...] = jnp.zeros_like(no)
        nr[...] = jnp.zeros_like(nr)

    xs = jnp.concatenate([xo[...], xr[...]], axis=0)
    ds = jnp.concatenate([do[...], dr[...]], axis=0)
    gate, up, sigma = hidden_parts(xs, wg, wu, section)
    hidden = gate * sigma * up
    d_hidden = None
    for g in range(4):
        a = nt(ds[:, 256 * g : 256 * g + 256], tile_of(wd, g, section))
        d_hidden = a if g == 0 else d_hidden + a
    d_gate = (d_hidden * up * sigma * (1.0 + gate * (1.0 - sigma))).astype(bf16)
    d_up = (d_hidden * gate * sigma).astype(bf16)
    hid_t = hidden.astype(bf16).T
    dg_t = d_gate.T
    du_t = d_up.T
    for g in range(4):
        xg = xs[:, 256 * g : 256 * g + 256]
        values = (nn(dg_t, xg), nn(du_t, xg), nn(hid_t, ds[:, 256 * g : 256 * g + 256]))
        for (target, row), value in zip(places, values):
            target[:, g, row : row + 80, :] = value.astype(bf16).reshape(4, 80, 256)
        dn = nn(d_gate, tile_of(wg, g, section)) + nn(d_up, tile_of(wu, g, section))
        no[:, 256 * g : 256 * g + 256] += dn[:TOK]
        nr[:, 256 * g : 256 * g + 256] += dn[TOK:]


def norm_back(e, z, rstd):
    return rstd * (e - z * (jnp.sum(e * z, axis=1, keepdims=True) * (1.0 / D)))


def attend_back_kernel(
    sel, own, recv, no, nr, mid_ref, gain_ref, dy_ref, q, kv, r1, r2, r3, mask, pnb,
    dmid_ref, dproj_ref, gg_ref, dq_ref, dkv_ref, d1, d2, d3, buf, kvs, dkv, sems,
):
    pick(sel, own, recv, 112, buf, sems)
    for k, part in enumerate((r3, r2, r1)):
        kvs[TOK * k : TOK * k + TOK, :] = part[...]
    kvs[3 * TOK :, :] = kv[...]
    mid = mid_ref[...]
    rstd = rstd_of(mid)
    z = mid * rstd
    dn = no[...] + nr[...]
    gg_ref[...] = jnp.broadcast_to(jnp.sum(dn * z, axis=0, keepdims=True), gg_ref.shape)
    dmid = dy_ref[...].astype(f32) + norm_back(dn * gain_ref[1:2, :], z, rstd)
    dmid_ref[...] = dmid
    dproj = dmid.astype(bf16)
    dproj_ref[...] = dproj
    arrived(own, 112, buf, sems)
    datt = None
    for j in range(4):
        a = nt(dproj[:, 256 * j : 256 * j + 256], chunk_of(buf, j))
        datt = a if j == 0 else datt + a
    datt = nt(datt.astype(bf16), pnb[...]).astype(bf16)
    allowed = mask[...] > 0.5
    allowed3 = jnp.concatenate([allowed] * 3, axis=0)
    dq_ref[:, 896:] = jnp.zeros((TOK, 128), f32)
    for i in range(HK):
        kg = kvs[:, HD * i : HD * i + HD]
        vg = kvs[:, KW + HD * i : KW + HD * i + HD]
        q3 = heads_of(q, i)
        do3 = heads_of(datt, i)
        probs = softmax_terms(q3, kg, allowed3)
        d_probs = nt(do3, vg)
        inner = jnp.sum(probs * d_probs, axis=1, keepdims=True)
        d_scores = (probs * (d_probs - inner)).astype(bf16)
        dq3 = nn(d_scores, kg) * 0.125
        for h in range(3):
            lane = HD * (3 * i + h)
            dq_ref[:, lane : lane + HD] = dq3[TOK * h : TOK * h + TOK, :]
        dkv[:, HD * i : HD * i + HD] = tn(d_scores, q3) * 0.125
        dkv[:, KW + HD * i : KW + HD * i + HD] = tn(probs.astype(bf16), do3)
    dkv_ref[...] = dkv[3 * TOK :, :]
    for k, part in enumerate((d3, d2, d1)):
        part[...] = dkv[TOK * k : TOK * k + TOK, :].astype(bf16)


def split3(v):
    hi = v.astype(bf16)
    rest = v - hi.astype(f32)
    middle = rest.astype(bf16)
    return hi, middle, (rest - middle.astype(f32)).astype(bf16)


def query_back_kernel(
    sel, core, own, recv, dq, cosw, sinw, norm_ref, attb, dproj, dn_ref, keep, send, buf, left, right, sems,
):
    pick(sel, own, recv, 48, buf, sems)
    dp = rotated_back(dq[...], cosw, sinw).astype(bf16)
    left[0] = norm_ref[...].T
    left[1] = attb[...].T
    for j in range(4):
        right[j] = dp[:, 256 * j : 256 * j + 256]
        right[4 + j] = dproj[:, 256 * j : 256 * j + 256]
    for target, half in ((keep, core[0]), (send, 1 - core[0])):
        for j in range(4):
            target[:, 16 * j : 16 * j + 16, :] = nn(left[half], right[4 * half + j]).astype(bf16).reshape(64, 16, 256)
    arrived(own, 48, buf, sems)
    dn = None
    for j in range(4):
        a = nt(dp[:, 256 * j : 256 * j + 256], chunk_of(buf, j))
        dn = a if j == 0 else dn + a
    dn_ref[...] = dn


def key_value_back_kernel(
    sel, core, own, recv, dkv, e1, e2, e3, cosw, sinw, norm_ref, x_ref, gain_ref, dmid_ref, pba, dnq, gg,
    dx_ref, keep, send, buf, right, sems,
):
    pick(sel, own, recv, 0, buf, sems)
    kv = dkv[...] + e1[...].astype(f32) + e2[...].astype(f32) + e3[...].astype(f32)
    d = jnp.concatenate([kv, jnp.zeros((TOK, 128), f32)], axis=1)
    dp = rotated_back(d, cosw, sinw).astype(bf16)
    arrived(own, 0, buf, sems)
    dn_b = dnq[...]
    for j in range(3):
        dn_b = dn_b + nt(dp[:, 256 * j : 256 * j + 256], chunk_of(buf, j))
        right[j] = dp[:, 256 * j : 256 * j + 256]
    right[3] = jnp.zeros((TOK, 256), bf16)
    hi, middle, lo = split3(dn_b)
    dn = nn(hi, pba[...]) + nn(middle, pba[...]) + nn(lo, pba[...])
    x = x_ref[...].astype(f32)
    rstd = rstd_of(x)
    z = x * rstd
    g1 = jnp.sum(dn * z, axis=0, keepdims=True)
    dx_ref[...] = (dmid_ref[...] + norm_back(dn * gain_ref[0:1, :], z, rstd)).astype(bf16)
    row = lax.broadcasted_iota(jnp.int32, (256, WA), 0)
    gains = jnp.where(row == 128, g1, jnp.where(row == 129, gg[0:1, :], 0.0)).astype(bf16)
    gains = nt(pba[...], gains)
    norm_t = norm_ref[...].T
    for target, half in ((keep, core[0]), (send, 1 - core[0])):
        for j in range(2):
            g = nn(norm_t, right[2 * half + j])
            if j == 0:
                g = g + gains * half.astype(f32)
            target[:, 16 * j : 16 * j + 16, :] = g.astype(bf16).reshape(64, 16, 256)


VM = pl.BlockSpec(memory_space=pltpu.VMEM)
ANY = pl.BlockSpec(memory_space=pl.ANY)
SM = pl.BlockSpec(memory_space=pltpu.SMEM)


def weight_scratch(rows):
    return pltpu.VMEM((16, 4, rows, 256), bf16)


def key_value(sel, own, recv, pab, pba, cosw, sinw, x=None, parts=None):
    outs = [sds((TOK, WA), bf16), sds((TOK, 2 * KW), bf16), sds((8, WA), f32)]
    ins = [sel, own, recv, pab, pba, cosw, sinw] + ([x] if parts is None else list(parts))
    if parts is not None:
        outs = [sds((TOK, WA), bf16)] + outs
    res = call(
        functools.partial(key_value_kernel, parts is None),
        outs, ins, [SM, ANY, ANY] + [VM] * (len(ins) - 3),
        [weight_scratch(48), pltpu.SemaphoreType.DMA((4,))], name="key_value",
    )
    return ([x] + list(res)) if parts is None else res


def query(sel, own, recv, *rest):
    return call(
        query_kernel, [sds((TOK, WA), bf16)], [sel, own, recv, *rest], [SM, ANY, ANY] + [VM] * len(rest),
        [weight_scratch(64), pltpu.SemaphoreType.DMA((4,))], name="query",
    )[0]


def attend(sel, own, recv, q, kv, chunks, mask, x, gains, pnb):
    ins = [sel, own, recv, q, kv, *chunks, mask, x, gains, pnb]
    return call(
        attend_kernel,
        [sds((TOK, WA), bf16), sds((TOK, WA), f32), sds((TOK, WA), bf16)],
        ins, [SM, ANY, ANY] + [VM] * (len(ins) - 3),
        [weight_scratch(64), pltpu.VMEM((LEN, 2 * KW), bf16), pltpu.VMEM((TOK, QW), bf16), pltpu.SemaphoreType.DMA((4,))],
        name="attend",
    )


def weight_specs(section):
    if section == 0:
        return [pl.BlockSpec((4, 4, 80, 256), lambda j: (j, 0, 0, 0)) for _ in range(3)]
    return [pl.BlockSpec((4, 4, 80, 256), lambda j, m=m: (0, j, m, 0)) for m in range(3)]


def whole(shape):
    return pl.BlockSpec(shape, lambda j: (0,) * len(shape))


def ffn(section, xo, xr, packed):
    row = whole((TOK, WA))
    return call(
        functools.partial(ffn_kernel, section), [sds((TOK, WA), f32)] * 2, [xo, xr, *packed],
        [row, row] + weight_specs(section), grid=(4,), out_specs=[row, row], name="ffn",
    )


def ffn_back(section, xo, xr, do, dr, packed):
    row = whole((TOK, WA))
    sizes = [240] if section == 1 else [80] * 3
    return call(
        functools.partial(ffn_back_kernel, section), [sds((16, 4, n, 256), bf16) for n in sizes] + [sds((TOK, WA), f32)] * 2,
        [xo, xr, do, dr, *packed],
        [row] * 4 + weight_specs(section), grid=(4,),
        out_specs=[pl.BlockSpec((4, 4, n, 256), lambda j: (j, 0, 0, 0)) for n in sizes] + [row, row], name="ffn_back",
    )


def attend_back(sel, own, recv, no, nr, mid, gains, dy, q, kv, chunks, mask, pnb):
    ins = [sel, own, recv, no, nr, mid, gains, dy, q, kv, *chunks, mask, pnb]
    small = sds((TOK, 2 * KW), bf16)
    return call(
        attend_back_kernel,
        [sds((TOK, WA), f32), sds((TOK, WA), bf16), sds((8, WA), f32), sds((TOK, WA), f32), sds((TOK, 2 * KW), f32), small, small, small],
        ins, [SM, ANY, ANY] + [VM] * (len(ins) - 3),
        [weight_scratch(64), pltpu.VMEM((LEN, 2 * KW), bf16), pltpu.VMEM((LEN, 2 * KW), f32), pltpu.SemaphoreType.DMA((4,))],
        name="attend_back",
    )


def query_back(sel, core, own, recv, *rest):
    return call(
        query_back_kernel, [sds((TOK, WA), f32)] + [sds((64, 64, 256), bf16)] * 2,
        [sel, core, own, recv, *rest], [SM, SM, ANY, ANY] + [VM] * len(rest),
        [weight_scratch(64), pltpu.VMEM((2, WA, TOK), bf16), pltpu.VMEM((8, TOK, 256), bf16), pltpu.SemaphoreType.DMA((4,))],
        name="query_back",
    )


def key_value_back(sel, core, own, recv, *rest):
    return call(
        key_value_back_kernel, [sds((TOK, WA), bf16)] + [sds((64, 32, 256), bf16)] * 2,
        [sel, core, own, recv, *rest], [SM, SM, ANY, ANY] + [VM] * len(rest),
        [weight_scratch(48), pltpu.VMEM((4, TOK, 256), bf16), pltpu.SemaphoreType.DMA((4,))],
        name="key_value_back",
    )


def other_core(v):
    return lax.ppermute(v, "section", [(0, 1), (1, 0)])


def shift_perm(name, k):
    if name == "x":
        return "gx", [(i, (i + k) % 4) for i in range(4)]
    if name == "z":
        return "gy", [(i, (i + 4 * k) % 16) for i in range(16)]
    return "gy", [(i, (i // 4) * 4 + (i % 4 + k) % 4) for i in range(16)]


def permuted(v, name, k):
    axis, perm = shift_perm(name, k)
    return lax.ppermute(v, axis, perm)


ORDERS = (("x", "y", "z"), ("y", "z", "x"), ("z", "x", "y"))
GROUPS = (((0, 1), (0, 3), (1, 1), (1, 3), (2, 2)), ((0, 2), (1, 2), (2, 1), (2, 3)))


def exchange(pieces, names, grouped, beside=()):
    keys = list(pieces)
    pieces = dict(zip(keys, lax.optimization_barrier([pieces[key] for key in keys])))
    if not grouped:
        return {key: permuted(pieces[key], names[key[0]], key[1]) for key in keys}, beside
    got = {key: permuted(pieces[key], names[key[0]], key[1]) for key in GROUPS[0]}
    tied = lax.optimization_barrier([[got[key] for key in GROUPS[0]], [pieces[key] for key in GROUPS[1]], list(beside)])
    got = dict(zip(GROUPS[0], tied[0]))
    for key, piece in zip(GROUPS[1], tied[1]):
        got[key] = permuted(piece, names[key[0]], key[1])
    return got, tied[2]


def gather_chunks(chunks, place, beside, after_first):
    state = [(c, ()) for c in chunks]

    def joined(got, names):
        after = []
        for c in range(3):
            v, have = state[c]
            have = tuple(n for n in ("z", "y", "x") if n in have or n == names[c])
            steps = [(place[names[c]] - i) % 4 for i in range(4)]
            others = [jnp.where(k == 1, got[(c, 1)], jnp.where(k == 2, got[(c, 2)], got[(c, 3)])) for k in steps]
            v = jnp.stack([jnp.where(k == 0, v, w) for k, w in zip(steps, others)], axis=have.index(names[c]))
            after.append((v, have))
        return after

    for step in range(3):
        names = [order[step] for order in ORDERS]
        pieces = {(c, k): state[c][0] for c in range(3) for k in (1, 2, 3)}
        got, tied = exchange(pieces, names, step >= 1, ((), beside, after_first)[step])
        if step < 2:
            state = joined(got, names)
        beside, after_first = (tied if step == 1 else beside), (tied if step == 2 else after_first)

    def finish(value):
        keys = list(got)
        value, parts = lax.optimization_barrier((value, [got[key] for key in keys]))
        return value, [v for v, _ in joined(dict(zip(keys, parts)), names)]

    return beside, after_first, finish


def reduce_bundles(bundles, place, last):
    left = [("z", "y", "x")] * 3
    for step in range(3):
        names = [order[step] for order in ORDERS]
        if step == 2:
            bundles[1] = bundles[1] + last
        pieces, mine = {}, []
        for c in range(3):
            dim = left[c].index(names[c])
            me = place[names[c]]
            mine.append([lax.dynamic_index_in_dim(v, me, dim, keepdims=False) for v in bundles[c]])
            for k in (1, 2, 3):
                parts = [lax.dynamic_index_in_dim(v, (me + k) % 4, dim, keepdims=False) for v in bundles[c]]
                pieces[(c, k)] = jnp.concatenate(parts, axis=-2)
            left[c] = tuple(n for n in left[c] if n != names[c])
        got, _ = exchange(pieces, names, step == 0)
        for c in range(3):
            total = jnp.concatenate(mine[c], axis=-2).astype(f32)
            for k in (1, 2, 3):
                total = total + got[(c, k)].astype(f32)
            bundles[c] = [total.astype(bf16)]
    return [bundle[0] for bundle in bundles]


def rope_tables(positions):
    frequency = rope_base ** (-(jnp.arange(HD // 2, dtype=f32) * 2.0) / HD)
    angles = positions.astype(f32)[:, None] * frequency[None, :]
    cosine, sine = jnp.cos(angles), jnp.sin(angles)
    cosine, sine = jnp.concatenate([cosine, cosine], 1), jnp.concatenate([sine, sine], 1)

    def wide(table, plain):
        key = jnp.concatenate([jnp.tile(table, (1, HK)), jnp.full((TOK, 448), plain, f32)], 1)
        return key, jnp.concatenate([jnp.tile(table, (1, HQ)), jnp.full((TOK, 64), plain, f32)], 1)

    return wide(cosine, 1.0) + wide(sine, 0.0)


def to_a(v):
    rows = v.shape[0]
    return jnp.pad(v.reshape(rows, 4, 240), ((0, 0), (0, 0), (0, 16))).reshape(rows, WA)


def from_a(v):
    return v.reshape(v.shape[:-1] + (4, 256))[..., :240].reshape(v.shape[:-1] + (D,))


def place_matrices():
    a = jnp.arange(WA, dtype=jnp.int32)
    in_a = jnp.where(a % 256 < 240, (a // 256) * 240 + a % 256, -1)
    shard = (a // 16 % 4) * 16 + a // 64
    in_b = jnp.where(a % 16 < 15, shard * 15 + a % 16, -2)
    pab = (in_a[:, None] == in_b[None, :]).astype(bf16)
    pba = (in_b[:, None] == in_a[None, :]).astype(bf16)
    pnb = (jnp.arange(QW, dtype=jnp.int32)[:, None] == in_b[None, :]).astype(bf16)
    return pab, pba, pnb


def per_device(inputs, cotangent, segment_ids, gain_attn, w_qkv, w_out, gain_ffn, w_gate, w_up, w_down):
    core = lax.axis_index("section")
    gx = lax.axis_index("gx")
    gy = lax.axis_index("gy")
    first = core == 0
    place = {"x": gx, "z": gy // 4, "y": gy % 4}

    pieces = jnp.stack([w_gate[0].T, w_up[0].T, w_down[0]]).reshape(3, 2, 80, 240)
    keep = jnp.where(first, pieces[:, 0], pieces[:, 1])
    got = other_core(jnp.where(first, pieces[:, 1], pieces[:, 0]))
    halves = jnp.concatenate([jnp.where(first, keep, got), jnp.where(first, got, keep)], 0)
    halves = jnp.pad(halves.reshape(FROWS, 240), ((0, 0), (0, 16)))
    attn = jnp.concatenate(
        [
            w_qkv[0][:, QW:],
            gain_attn[0][:, None],
            gain_ffn[0][:, None],
            jnp.zeros((15, 126), bf16),
            w_qkv[0][:, :QW],
            jnp.zeros((15, 64), bf16),
            to_a(w_out[0]),
        ],
        1,
    )
    attn = jnp.pad(attn, ((0, 1), (0, 0))).reshape(16, 11, 256).transpose(1, 0, 2).reshape(AROWS, 256)
    own = lax.all_gather(attn[None], ("gx", "gy"), axis=0, tiled=True)
    own_in = to_a(jnp.where(first, inputs[0, 0], inputs[1, 0]))
    cot0, cot1 = to_a(cotangent[0, 0]), to_a(cotangent[1, 0])
    cot_own, cot_other = jnp.where(first, cot0, cot1), jnp.where(first, cot1, cot0)
    segments = jnp.where(first, segment_ids[0, 0], segment_ids[1, 0])
    local_ids = lax.dynamic_slice_in_dim(segments, gx * TOK, TOK, 0)
    own_index = gx * TOK + jnp.arange(TOK, dtype=jnp.int32)
    doc_start = jnp.sum((segments[None, :] < local_ids[:, None]).astype(jnp.int32), axis=1)
    key_index = (gx - 3) * TOK + jnp.arange(LEN, dtype=jnp.int32)
    key_ids = lax.dynamic_slice_in_dim(jnp.pad(segments, (3 * TOK, 0), constant_values=-1), gx * TOK, LEN, 0)
    mask = ((local_ids[:, None] == key_ids[None, :]) & (key_index[None, :] <= own_index[:, None])).astype(f32)
    cos_kv, cos_q, sin_kv, sin_q = rope_tables(own_index - doc_start)
    beside = [cos_kv, cos_q, sin_kv, sin_q, mask, own_in, cot_own, cot_other, *place_matrices()]
    early = [halves[:80], halves[80:160], halves[160:240]]
    beside, (own, second), finish = gather_chunks(early, place, beside, (own, halves[240:]))
    recv = other_core(own)
    packed = lax.all_gather(second[None], ("gx", "gy"), axis=0, tiled=True).reshape(4, 16, 240, 256)
    cos_kv, cos_q, sin_kv, sin_q, mask, own_in, cot_own, cot_other, pab, pba, pnb = beside
    ffn_weights = [None, [packed] * 3]

    def ahead(v, k):
        return lax.ppermute(v, "gx", [(i, i + k) for i in range(4 - k)])

    def back(v, k):
        return lax.ppermute(v, "gx", [(i + k, i) for i in range(4 - k)])

    def added(a, b):
        return (a.astype(f32) + b.astype(f32)).astype(bf16)

    def over_gy(v):
        rows = v.shape[-2]
        return lax.psum_scatter(v.reshape(16, 4 * rows, 256), "gy", scatter_dimension=0, tiled=True).reshape(4, rows, 256)

    sels = [core[None].astype(jnp.int32), (1 - core)[None].astype(jnp.int32)]
    kept = []
    x, parts = own_in, None
    for section in range(2):
        sel = sels[section]
        x, norm_b, kv, gains = key_value(sel, own, recv, pab, pba, cos_kv, sin_kv, x, parts)
        chunks = [ahead(kv, 1), ahead(kv, 2), ahead(kv, 3)]
        q = query(sel, own, recv, norm_b, cos_q, sin_q)
        if section == 0:
            q, first_ffn = finish(q)
            ffn_weights[0] = [w.reshape(16, 4, 80, 256) for w in first_ffn]
        attb, mid, n2 = attend(sel, own, recv, q, kv, chunks, mask, x, gains, pnb)
        n2_other = other_core(n2)
        yo, yr = ffn(section, n2, n2_other, ffn_weights[section])
        parts = (mid, yo, other_core(yr))
        kept.append((x, norm_b, q, kv, gains, chunks, attb, mid, n2, n2_other))
    outs = [kept[1][0], (parts[0] + parts[1] + parts[2]).astype(bf16)]

    dy, dy_other = cot_own, cot_other
    grads_in, ffn_grads, attn_grads = [None, None], [None, None], [None, None]
    for section in (1, 0):
        sel = sels[section]
        x, norm_b, q, kv, gains, chunks, attb, mid, n2, n2_other = kept[section]
        *ffn_grads[section], no, nr = ffn_back(section, n2, n2_other, dy, dy_other, ffn_weights[section])
        if section == 1:
            late0 = over_gy(ffn_grads[1][0])
        dmid, dproj, gg, dq, dkv, d1, d2, d3 = attend_back(
            sel, own, recv, no, other_core(nr), mid, gains, dy, q, kv, chunks, mask, pnb
        )
        back_chunks = [back(d1, 1), back(d2, 2), back(d3, 3)]
        dnq, keep_q, send_q = query_back(sel, sels[0], own, recv, dq, cos_q, sin_q, norm_b, attb, dproj)
        if section == 0:
            dnq, late0, cat1 = lax.optimization_barrier((dnq, late0, cat1))
            late = [late0, over_gy(cat1)]
        dy, keep_kv, send_kv = key_value_back(
            sel, sels[0], own, recv, dkv, *back_chunks, cos_kv, sin_kv, norm_b, x, gains, dmid, pba, dnq, gg
        )
        send_q, send_kv = lax.optimization_barrier((send_q, send_kv))
        got_q, got_kv = other_core(send_q), other_core(send_kv)
        grads_in[section] = dy
        attn_grads[section] = (added(keep_q, got_q), added(keep_kv, got_kv))
        if section == 1:
            dy_other = other_core(dy)
            cat1 = jnp.concatenate(attn_grads[1], 1)

    grid = (4, 4, 4)
    ffn0 = [v.reshape(grid + (80, 256)) for v in ffn_grads[0]]
    q0, kv0 = [v.reshape(grid + v.shape[1:]) for v in attn_grads[0]]
    bundles = [[ffn0[0], q0[..., :32, :]], [ffn0[1], q0[..., 32:, :]], [ffn0[2], kv0]]
    r0, r1, r2 = reduce_bundles(bundles, place, late)
    half = [jnp.concatenate([r0[:80], r1[:80], r2[:80], r0[80:], r1[80:112], r2[80:]], 0), r1[112:]]
    mine = jnp.where(first, half[0], half[1])
    theirs = other_core(jnp.where(first, half[1], half[0]))
    low, high = jnp.where(first, mine, theirs), jnp.where(first, theirs, mine)
    ff = jnp.concatenate([low[:240].reshape(3, 80, 256), high[:240].reshape(3, 80, 256)], 1)[:, :, :240].astype(f32)
    def columns(v):
        chunks = v.reshape(v.shape[0] // 16, 16, 256)[:, :15].astype(f32)
        return chunks.transpose(1, 0, 2).reshape(15, v.shape[0] * 16)

    q_grad, kv_grad = columns(low[240:304]), columns(jnp.concatenate([low[304:336], high[304:320]], 0))
    out_grad = from_a(columns(high[240:304]))
    grad_qkv = jnp.concatenate([q_grad[:, :QW], kv_grad[:, : 2 * KW]], 1)

    def placed(pair):
        a = jnp.where(first, pair[0], pair[1])
        b = other_core(jnp.where(first, pair[1], pair[0]))
        both = jnp.stack([jnp.where(first, a, b), jnp.where(first, b, a)])
        return from_a(both)[None, :, None]

    return (
        placed(outs),
        placed(grads_in),
        kv_grad[:, 640][None],
        grad_qkv[None],
        out_grad[None],
        kv_grad[:, 641][None],
        ff[0].T[None],
        ff[1].T[None],
        ff[2][None],
    )


def solution(mesh):
    return jax.shard_map(
        per_device,
        mesh=mesh,
        in_specs=(
            P(None, "gy", "gx", None),
            P(None, "gy", "gx", None),
            P(None, "gy", None),
            P("section", ("gx", "gy")),
            P("section", ("gx", "gy"), None),
            P("section", ("gx", "gy"), None),
            P("section", ("gx", "gy")),
            P("section", "gx", "gy"),
            P("section", "gx", "gy"),
            P("section", "gy", "gx"),
        ),
        out_specs=(
            P("section", None, "gy", "gx", None),
            P("section", None, "gy", "gx", None),
            P("section", ("gx", "gy")),
            P("section", ("gx", "gy"), None),
            P("section", ("gx", "gy"), None),
            P("section", ("gx", "gy")),
            P("section", "gx", "gy"),
            P("section", "gx", "gy"),
            P("section", "gy", "gx"),
        ),
        check_vma=False,
    )
```

```python
import functools

import jax
import jax.numpy as jnp
from jax import lax
from jax.experimental import pallas as pl
from jax.experimental.pallas import tpu as pltpu
from jax.sharding import PartitionSpec as P

HQ, HK, HD = 15, 5, 64
D, QW, KW = 960, 960, 320
TOK, LEN = 128, 512
WA = 1024
QKVW = 1792
FROWS, AROWS = 480, 176
epsilon = 1e-05
rope_base = 100000.0
masked_score = -1e30
VMEM = 60 * 2**20
bf16, f32 = jnp.bfloat16, jnp.float32


def nn(a, b):
    return jnp.dot(a, b, preferred_element_type=f32)


def nt(a, b):
    return lax.dot_general(a, b, (((1,), (1,)), ((), ())), preferred_element_type=f32)


def tn(a, b):
    return lax.dot_general(a, b, (((0,), (0,)), ((), ())), preferred_element_type=f32)


def call(kernel, outs, ins, specs, scratch=(), name=None):
    vm = pl.BlockSpec(memory_space=pltpu.VMEM)
    return pl.pallas_call(
        kernel,
        out_shape=outs,
        in_specs=specs,
        out_specs=[vm] * len(outs),
        scratch_shapes=list(scratch),
        compiler_params=pltpu.CompilerParams(vmem_limit_bytes=VMEM),
        name=name,
    )(*ins)


def stepped(kernel, place, outs, ins, specs, out_specs, scratch, name):
    return pl.pallas_call(
        kernel,
        out_shape=outs,
        grid_spec=pltpu.PrefetchScalarGridSpec(
            num_scalar_prefetch=1, grid=(4,), in_specs=specs, out_specs=out_specs, scratch_shapes=scratch
        ),
        compiler_params=pltpu.CompilerParams(vmem_limit_bytes=VMEM),
        name=name,
    )(place, *ins)


def sds(shape, dt):
    return jax.ShapeDtypeStruct(shape, dt)


def weight_copies(source, first, buf, sems):
    rows = buf.shape[2]
    return [
        pltpu.make_async_copy(source.at[pl.ds(16 * x, 16), pl.ds(first, rows), :], buf.at[:, x], sems.at[x])
        for x in range(4)
    ]


def pick(sel_ref, own, recv, first, buf, sems):
    @pl.when(sel_ref[0] == 0)
    def _():
        for copy in weight_copies(own, first, buf, sems):
            copy.start()

    @pl.when(sel_ref[0] != 0)
    def _():
        for copy in weight_copies(recv, first, buf, sems):
            copy.start()


def arrived(own, first, buf, sems):
    for copy in weight_copies(own, first, buf, sems):
        copy.wait()


def chunk_of(buf, j):
    return buf[:, :, 16 * j : 16 * j + 16, :].reshape(WA, 256)


def rstd_of(v):
    return lax.rsqrt(jnp.sum(v * v, axis=1, keepdims=True) * (1.0 / D) + epsilon)


def lane_in_head(shape):
    return lax.broadcasted_iota(jnp.int32, shape, 1) % HD


def rotated(v, cosw, sinw):
    low = lane_in_head(v.shape) < HD // 2
    turned = jnp.where(low, -pltpu.roll(v, v.shape[1] - 32, 1), pltpu.roll(v, 32, 1))
    return v * cosw[...] + turned * sinw[...]


def rotated_back(v, cosw, sinw):
    low = lane_in_head(v.shape) < HD // 2
    scaled = v * sinw[...]
    turned = jnp.where(low, pltpu.roll(scaled, v.shape[1] - 32, 1), -pltpu.roll(scaled, 32, 1))
    return v * cosw[...] + turned


def key_value_kernel(has_x, sel, own, recv, pab, pba, cosw, sinw, *rest):
    if has_x:
        x_ref, norm_ref, kv_ref, gain_ref, buf, sems = rest
    else:
        mid_ref, yo_ref, yr_ref, x_out, norm_ref, kv_ref, gain_ref, buf, sems = rest
    pick(sel, own, recv, 0, buf, sems)
    if has_x:
        x = x_ref[...].astype(f32)
    else:
        xb = (mid_ref[...] + yo_ref[...] + yr_ref[...]).astype(bf16)
        x_out[...] = xb
        x = xb.astype(f32)
    rstd = rstd_of(x)
    arrived(own, 0, buf, sems)
    gains = nn(chunk_of(buf, 2).astype(f32).T.astype(bf16), pba[...])[128:136, :]
    gain_ref[...] = gains
    normed = (x * rstd * gains[0:1, :]).astype(bf16)
    norm_b = nn(normed, pab[...]).astype(bf16)
    norm_ref[...] = norm_b
    proj = jnp.concatenate([nn(norm_b, chunk_of(buf, j)) for j in range(3)], axis=1)
    kv_ref[...] = rotated(proj, cosw, sinw).astype(bf16)[:, : 2 * KW]


def query_kernel(sel, own, recv, norm_ref, cosw, sinw, q_ref, buf, sems):
    pick(sel, own, recv, 48, buf, sems)
    arrived(own, 48, buf, sems)
    proj = jnp.concatenate([nn(norm_ref[...], chunk_of(buf, j)) for j in range(4)], axis=1)
    q_ref[...] = rotated(proj, cosw, sinw).astype(bf16)


def heads_of(ref, i):
    return jnp.concatenate([ref[:, HD * (3 * i + h) : HD * (3 * i + h + 1)] for h in range(3)], axis=0)


def softmax_terms(q3, kg, allowed3):
    scores = nt(q3, kg) * 0.125
    scores = jnp.where(allowed3, scores, masked_score)
    highest = jnp.max(scores, axis=1, keepdims=True)
    terms = jnp.exp(scores - highest)
    return terms / jnp.sum(terms, axis=1, keepdims=True)


def attend_kernel(sel, own, recv, q, kv, r1, r2, r3, mask, x_ref, gain_ref, pnb, attb_ref, mid_ref, n2_ref, buf, kvs, att, sems):
    pick(sel, own, recv, 112, buf, sems)
    for k, part in enumerate((r3, r2, r1)):
        kvs[TOK * k : TOK * k + TOK, :] = part[...]
    kvs[3 * TOK :, :] = kv[...]
    allowed = mask[...] > 0.5
    allowed3 = jnp.concatenate([allowed] * 3, axis=0)
    for i in range(HK):
        kg = kvs[:, HD * i : HD * i + HD]
        vg = kvs[:, KW + HD * i : KW + HD * i + HD]
        probs = softmax_terms(heads_of(q, i), kg, allowed3).astype(bf16)
        o3 = nn(probs, vg).astype(bf16)
        for h in range(3):
            lane = HD * (3 * i + h)
            att[:, lane : lane + HD] = o3[TOK * h : TOK * h + TOK, :]
    attb = nn(att[...], pnb[...]).astype(bf16)
    attb_ref[...] = attb
    arrived(own, 112, buf, sems)
    out = jnp.concatenate([nn(attb, chunk_of(buf, j)) for j in range(4)], axis=1)
    mid = x_ref[...].astype(f32) + out
    mid_ref[...] = mid
    n2_ref[...] = (mid * rstd_of(mid) * gain_ref[1:2, :]).astype(bf16)


def tile_of(w, g, section):
    if section == 1:
        return w[g].reshape(320, 256)
    if len(w) == 1:
        return w[0][:, 0, g].reshape(320, 256)
    if w[0].shape[0] == 1:
        return jnp.concatenate([part[0, g] for part in w], axis=0)
    return w[g][:, 0].reshape(320, 256)


def weight_refs(section, refs):
    if section == 1:
        return refs[0], refs[1], refs[2], refs[3:]
    return refs[:4], refs[4:8], refs[8:9], refs[9:]


def lanes(gx, g, section):
    if section == 0:
        return pl.ds(pl.multiple_of((gx[0] + g) % 4 * 256, 256), 256)
    return pl.ds(256 * g, 256)


def hidden_parts(gx, xs, wg, wu, section):
    gate = up = None
    for g in range(4):
        xg = xs[:, lanes(gx, g, section)]
        a, b = nt(xg, tile_of(wg, g, section)), nt(xg, tile_of(wu, g, section))
        gate, up = (a, b) if g == 0 else (gate + a, up + b)
    return gate, up, 1.0 / (1.0 + jnp.exp(-gate))


def ffn_kernel(section, gx, xo, xr, *refs):
    wg, wu, wd, (yo, yr, xs) = weight_refs(section, refs)
    j = pl.program_id(0)

    @pl.when(j == 0)
    def _():
        yo[...] = jnp.zeros_like(yo)
        yr[...] = jnp.zeros_like(yr)
        xs[:TOK] = xo[...]
        xs[TOK:] = xr[...]

    gate, up, sigma = hidden_parts(gx, xs, wg, wu, section)
    hidden = (gate * sigma * up).astype(bf16)
    for g in range(4):
        y = nn(hidden, tile_of(wd, g, section))
        yo[:, lanes(gx, g, section)] += y[:TOK]
        yr[:, lanes(gx, g, section)] += y[TOK:]


def ffn_back_kernel(section, gx, xo, xr, do, dr, *refs):
    wg, wu, wd, rest = weight_refs(section, refs)
    *attn, grads, no, nr, xs, ds = rest
    if section == 0:
        row = 240
        for mine, other in ((attn[0], attn[1]), (attn[2], attn[3])):
            rows = mine.shape[3]
            grads[:, :, :, row : row + rows, :] = (mine[...].astype(f32) + other[...].astype(f32)).astype(bf16)
            row += rows
    j = pl.program_id(0)

    @pl.when(j == 0)
    def _():
        no[...] = jnp.zeros_like(no)
        nr[...] = jnp.zeros_like(nr)
        xs[:TOK] = xo[...]
        xs[TOK:] = xr[...]
        ds[:TOK] = do[...]
        ds[TOK:] = dr[...]

    gate, up, sigma = hidden_parts(gx, xs, wg, wu, section)
    hidden = gate * sigma * up
    d_hidden = None
    for g in range(4):
        a = nt(ds[:, lanes(gx, g, section)], tile_of(wd, g, section))
        d_hidden = a if g == 0 else d_hidden + a
    d_gate = (d_hidden * up * sigma * (1.0 + gate * (1.0 - sigma))).astype(bf16)
    d_up = (d_hidden * gate * sigma).astype(bf16)
    hid_t = hidden.astype(bf16).T
    dg_t = d_gate.T
    du_t = d_up.T
    for g in range(4):
        xg, dg = xs[:, lanes(gx, g, section)], ds[:, lanes(gx, g, section)]
        values = (nn(dg_t, xg), nn(du_t, xg), nn(hid_t, dg))
        for m, value in enumerate(values):
            value = value.astype(bf16).reshape(4, 80, 256)
            if section == 0:
                for i in range(4):
                    grads[(gx[1] + i) % 4, 0, (gx[0] + g) % 4, 80 * m : 80 * m + 80, :] = value[i]
            else:
                grads[:, g, 80 * m : 80 * m + 80, :] = value
        dn = nn(d_gate, tile_of(wg, g, section)) + nn(d_up, tile_of(wu, g, section))
        no[:, lanes(gx, g, section)] += dn[:TOK]
        nr[:, lanes(gx, g, section)] += dn[TOK:]


def norm_back(e, z, rstd):
    return rstd * (e - z * (jnp.sum(e * z, axis=1, keepdims=True) * (1.0 / D)))


def attend_back_kernel(
    sel, own, recv, no, nr, mid_ref, gain_ref, dy_ref, q, kv, r1, r2, r3, mask, pnb,
    dmid_ref, dproj_ref, gg_ref, dq_ref, dkv_ref, d1, d2, d3, buf, kvs, dkv, sems,
):
    pick(sel, own, recv, 112, buf, sems)
    for k, part in enumerate((r3, r2, r1)):
        kvs[TOK * k : TOK * k + TOK, :] = part[...]
    kvs[3 * TOK :, :] = kv[...]
    mid = mid_ref[...]
    rstd = rstd_of(mid)
    z = mid * rstd
    dn = no[...] + nr[...]
    gg_ref[...] = jnp.broadcast_to(jnp.sum(dn * z, axis=0, keepdims=True), gg_ref.shape)
    dmid = dy_ref[...].astype(f32) + norm_back(dn * gain_ref[1:2, :], z, rstd)
    dmid_ref[...] = dmid
    dproj = dmid.astype(bf16)
    dproj_ref[...] = dproj
    arrived(own, 112, buf, sems)
    datt = None
    for j in range(4):
        a = nt(dproj[:, 256 * j : 256 * j + 256], chunk_of(buf, j))
        datt = a if j == 0 else datt + a
    datt = nt(datt.astype(bf16), pnb[...]).astype(bf16)
    allowed = mask[...] > 0.5
    allowed3 = jnp.concatenate([allowed] * 3, axis=0)
    dq_ref[:, 896:] = jnp.zeros((TOK, 128), f32)
    for i in range(HK):
        kg = kvs[:, HD * i : HD * i + HD]
        vg = kvs[:, KW + HD * i : KW + HD * i + HD]
        q3 = heads_of(q, i)
        do3 = heads_of(datt, i)
        probs = softmax_terms(q3, kg, allowed3)
        d_probs = nt(do3, vg)
        inner = jnp.sum(probs * d_probs, axis=1, keepdims=True)
        d_scores = (probs * (d_probs - inner)).astype(bf16)
        dq3 = nn(d_scores, kg) * 0.125
        for h in range(3):
            lane = HD * (3 * i + h)
            dq_ref[:, lane : lane + HD] = dq3[TOK * h : TOK * h + TOK, :]
        dkv[:, HD * i : HD * i + HD] = tn(d_scores, q3) * 0.125
        dkv[:, KW + HD * i : KW + HD * i + HD] = tn(probs.astype(bf16), do3)
    dkv_ref[...] = dkv[3 * TOK :, :]
    for k, part in enumerate((d3, d2, d1)):
        part[...] = dkv[TOK * k : TOK * k + TOK, :].astype(bf16)


def split3(v):
    hi = v.astype(bf16)
    rest = v - hi.astype(f32)
    middle = rest.astype(bf16)
    return hi, middle, (rest - middle.astype(f32)).astype(bf16)


def query_back_kernel(
    sel, core, own, recv, dq, cosw, sinw, norm_ref, attb, dproj, dn_ref, keep, send, buf, left, right, sems,
):
    pick(sel, own, recv, 48, buf, sems)
    dp = rotated_back(dq[...], cosw, sinw).astype(bf16)
    left[0] = norm_ref[...].T
    left[1] = attb[...].T
    for j in range(4):
        right[j] = dp[:, 256 * j : 256 * j + 256]
        right[4 + j] = dproj[:, 256 * j : 256 * j + 256]
    for target, half in ((keep, core[0]), (send, 1 - core[0])):
        for j in range(4):
            target[:, 16 * j : 16 * j + 16, :] = nn(left[half], right[4 * half + j]).astype(bf16).reshape(64, 16, 256)
    arrived(own, 48, buf, sems)
    dn = None
    for j in range(4):
        a = nt(dp[:, 256 * j : 256 * j + 256], chunk_of(buf, j))
        dn = a if j == 0 else dn + a
    dn_ref[...] = dn


def key_value_back_kernel(
    sel, core, own, recv, dkv, e1, e2, e3, cosw, sinw, norm_ref, x_ref, gain_ref, dmid_ref, pba, dnq, gg,
    dx_ref, keep, send, buf, right, sems,
):
    pick(sel, own, recv, 0, buf, sems)
    kv = dkv[...] + e1[...].astype(f32) + e2[...].astype(f32) + e3[...].astype(f32)
    d = jnp.concatenate([kv, jnp.zeros((TOK, 128), f32)], axis=1)
    dp = rotated_back(d, cosw, sinw).astype(bf16)
    arrived(own, 0, buf, sems)
    dn_b = dnq[...]
    for j in range(3):
        dn_b = dn_b + nt(dp[:, 256 * j : 256 * j + 256], chunk_of(buf, j))
        right[j] = dp[:, 256 * j : 256 * j + 256]
    right[3] = jnp.zeros((TOK, 256), bf16)
    hi, middle, lo = split3(dn_b)
    dn = nn(hi, pba[...]) + nn(middle, pba[...]) + nn(lo, pba[...])
    x = x_ref[...].astype(f32)
    rstd = rstd_of(x)
    z = x * rstd
    g1 = jnp.sum(dn * z, axis=0, keepdims=True)
    dx_ref[...] = (dmid_ref[...] + norm_back(dn * gain_ref[0:1, :], z, rstd)).astype(bf16)
    row = lax.broadcasted_iota(jnp.int32, (256, WA), 0)
    gains = jnp.where(row == 128, g1, jnp.where(row == 129, gg[0:1, :], 0.0)).astype(bf16)
    gains = nt(pba[...], gains)
    norm_t = norm_ref[...].T
    for target, half in ((keep, core[0]), (send, 1 - core[0])):
        for j in range(2):
            g = nn(norm_t, right[2 * half + j])
            if j == 0:
                g = g + gains * half.astype(f32)
            target[:, 16 * j : 16 * j + 16, :] = g.astype(bf16).reshape(64, 16, 256)


VM = pl.BlockSpec(memory_space=pltpu.VMEM)
ANY = pl.BlockSpec(memory_space=pl.ANY)
SM = pl.BlockSpec(memory_space=pltpu.SMEM)


def weight_scratch(rows):
    return pltpu.VMEM((16, 4, rows, 256), bf16)


def key_value(sel, own, recv, pab, pba, cosw, sinw, x=None, parts=None):
    outs = [sds((TOK, WA), bf16), sds((TOK, 2 * KW), bf16), sds((8, WA), f32)]
    ins = [sel, own, recv, pab, pba, cosw, sinw] + ([x] if parts is None else list(parts))
    if parts is not None:
        outs = [sds((TOK, WA), bf16)] + outs
    res = call(
        functools.partial(key_value_kernel, parts is None),
        outs, ins, [SM, ANY, ANY] + [VM] * (len(ins) - 3),
        [weight_scratch(48), pltpu.SemaphoreType.DMA((4,))], name="key_value",
    )
    return ([x] + list(res)) if parts is None else res


def query(sel, own, recv, *rest):
    return call(
        query_kernel, [sds((TOK, WA), bf16)], [sel, own, recv, *rest], [SM, ANY, ANY] + [VM] * len(rest),
        [weight_scratch(64), pltpu.SemaphoreType.DMA((4,))], name="query",
    )[0]


def attend(sel, own, recv, q, kv, chunks, mask, x, gains, pnb):
    ins = [sel, own, recv, q, kv, *chunks, mask, x, gains, pnb]
    return call(
        attend_kernel,
        [sds((TOK, WA), bf16), sds((TOK, WA), f32), sds((TOK, WA), bf16)],
        ins, [SM, ANY, ANY] + [VM] * (len(ins) - 3),
        [weight_scratch(64), pltpu.VMEM((LEN, 2 * KW), bf16), pltpu.VMEM((TOK, QW), bf16), pltpu.SemaphoreType.DMA((4,))],
        name="attend",
    )


def weight_specs(section):
    if section == 0:
        by_z = [pl.BlockSpec((1, 4, 80, 256), lambda j, p: (j, 0, 0, 0)) for _ in range(4)]
        by_x = [pl.BlockSpec((4, 1, 80, 256), lambda j, p: (0, j, 0, 0)) for _ in range(4)]
        return by_z + by_x + [pl.BlockSpec((4, 1, 4, 80, 256), lambda j, p: (0, j, 0, 0, 0))]
    return [pl.BlockSpec((4, 4, 80, 256), lambda j, p, m=m: (0, j, m, 0)) for m in range(3)]


def whole(shape):
    return pl.BlockSpec(shape, lambda j, p: (0,) * len(shape))


def ffn(section, place, xo, xr, packed):
    row = whole((TOK, WA))
    return stepped(
        functools.partial(ffn_kernel, section), place, [sds((TOK, WA), f32)] * 2, [xo, xr, *packed],
        [row, row] + weight_specs(section), [row, row], [pltpu.VMEM((2 * TOK, WA), bf16)], "ffn",
    )


def ffn_back(section, place, xo, xr, do, dr, packed, attn=()):
    row = whole((TOK, WA))
    if section == 1:
        grads, block = sds((16, 4, 240, 256), bf16), pl.BlockSpec((4, 4, 240, 256), lambda j, p: (j, 0, 0, 0))
    else:
        grads = sds((4, 4, 4, 336, 256), bf16)
        block = pl.BlockSpec((4, 1, 4, 336, 256), lambda j, p: (0, (p[2] + j) % 4, 0, 0, 0))
    attn_specs = [pl.BlockSpec((4, 1) + v.shape[2:], lambda j, p: (0, (p[2] + j) % 4, 0, 0, 0)) for v in attn]
    return stepped(
        functools.partial(ffn_back_kernel, section), place, [grads] + [sds((TOK, WA), f32)] * 2,
        [xo, xr, do, dr, *packed, *attn],
        [row] * 4 + weight_specs(section) + attn_specs, [block, row, row],
        [pltpu.VMEM((2 * TOK, WA), bf16)] * 2, "ffn_back",
    )


def attend_back(sel, own, recv, no, nr, mid, gains, dy, q, kv, chunks, mask, pnb):
    ins = [sel, own, recv, no, nr, mid, gains, dy, q, kv, *chunks, mask, pnb]
    small = sds((TOK, 2 * KW), bf16)
    return call(
        attend_back_kernel,
        [sds((TOK, WA), f32), sds((TOK, WA), bf16), sds((8, WA), f32), sds((TOK, WA), f32), sds((TOK, 2 * KW), f32), small, small, small],
        ins, [SM, ANY, ANY] + [VM] * (len(ins) - 3),
        [weight_scratch(64), pltpu.VMEM((LEN, 2 * KW), bf16), pltpu.VMEM((LEN, 2 * KW), f32), pltpu.SemaphoreType.DMA((4,))],
        name="attend_back",
    )


def query_back(sel, core, own, recv, *rest):
    return call(
        query_back_kernel, [sds((TOK, WA), f32)] + [sds((64, 64, 256), bf16)] * 2,
        [sel, core, own, recv, *rest], [SM, SM, ANY, ANY] + [VM] * len(rest),
        [weight_scratch(64), pltpu.VMEM((2, WA, TOK), bf16), pltpu.VMEM((8, TOK, 256), bf16), pltpu.SemaphoreType.DMA((4,))],
        name="query_back",
    )


def key_value_back(sel, core, own, recv, *rest):
    return call(
        key_value_back_kernel, [sds((TOK, WA), bf16)] + [sds((64, 32, 256), bf16)] * 2,
        [sel, core, own, recv, *rest], [SM, SM, ANY, ANY] + [VM] * len(rest),
        [weight_scratch(48), pltpu.VMEM((4, TOK, 256), bf16), pltpu.SemaphoreType.DMA((4,))],
        name="key_value_back",
    )


def other_core(v):
    return lax.ppermute(v, "section", [(0, 1), (1, 0)])


def shift_perm(name, k):
    if name == "x":
        return "gx", [(i, (i + k) % 4) for i in range(4)]
    if name == "z":
        return "gy", [(i, (i + 4 * k) % 16) for i in range(16)]
    return "gy", [(i, (i // 4) * 4 + (i % 4 + k) % 4) for i in range(16)]


def permuted(v, name, k):
    axis, perm = shift_perm(name, k)
    return lax.ppermute(v, axis, perm)


ORDERS = (("x", "y", "z"), ("y", "z", "x"), ("z", "x", "y"))
GROUPS = (((0, 1), (0, 3), (1, 1), (1, 3), (2, 2)), ((0, 2), (1, 2), (2, 1), (2, 3)))


def exchange(pieces, names, grouped, beside=()):
    keys = list(pieces)
    pieces = dict(zip(keys, lax.optimization_barrier([pieces[key] for key in keys])))
    if not grouped:
        return {key: permuted(pieces[key], names[key[0]], key[1]) for key in keys}, beside
    got = {key: permuted(pieces[key], names[key[0]], key[1]) for key in GROUPS[0]}
    tied = lax.optimization_barrier([[got[key] for key in GROUPS[0]], [pieces[key] for key in GROUPS[1]], list(beside)])
    got = dict(zip(GROUPS[0], tied[0]))
    for key, piece in zip(GROUPS[1], tied[1]):
        got[key] = permuted(piece, names[key[0]], key[1])
    return got, tied[2]


def gather_chunks(chunks, beside, after_first):
    state = [(c, ()) for c in chunks]

    def joined(got, names):
        after = []
        for c in range(3):
            v, have = state[c]
            have = tuple(n for n in ("z", "y", "x") if n in have or n == names[c])
            v = jnp.stack([v, got[(c, 3)], got[(c, 2)], got[(c, 1)]], axis=have.index(names[c]))
            after.append((v, have))
        return after

    for step in range(3):
        names = [order[step] for order in ORDERS]
        pieces = {(c, k): state[c][0] for c in range(3) for k in (1, 2, 3)}
        got, tied = exchange(pieces, names, step >= 1, ((), beside, after_first)[step])
        if step < 2:
            state = joined(got, names)
        beside, after_first = (tied if step == 1 else beside), (tied if step == 2 else after_first)

    def finish(value):
        keys = list(got)
        value, parts = lax.optimization_barrier((value, [got[key] for key in keys]))
        parts = dict(zip(keys, parts))
        apart = [[state[c][0], parts[(c, 3)], parts[(c, 2)], parts[(c, 1)]] for c in range(3)]
        return value, apart[0] + apart[1] + [jnp.stack(apart[2], axis=1)]

    return beside, after_first, finish


def reduce_axis(v, dim, name, place):
    me = place[name]
    pieces = [lax.dynamic_index_in_dim(v, (me + k) % 4, dim, keepdims=False) for k in (1, 3, 2)]
    pieces = lax.optimization_barrier(pieces)
    total = lax.dynamic_index_in_dim(v, me, dim, keepdims=False).astype(f32)
    for piece, k in zip(pieces, (1, 3, 2)):
        total = total + permuted(piece, name, k).astype(f32)
    return total.astype(bf16)


def rope_tables(positions):
    frequency = rope_base ** (-(jnp.arange(HD // 2, dtype=f32) * 2.0) / HD)
    angles = positions.astype(f32)[:, None] * frequency[None, :]
    cosine, sine = jnp.cos(angles), jnp.sin(angles)
    cosine, sine = jnp.concatenate([cosine, cosine], 1), jnp.concatenate([sine, sine], 1)

    def wide(table, plain):
        key = jnp.concatenate([jnp.tile(table, (1, HK)), jnp.full((TOK, 448), plain, f32)], 1)
        return key, jnp.concatenate([jnp.tile(table, (1, HQ)), jnp.full((TOK, 64), plain, f32)], 1)

    return wide(cosine, 1.0) + wide(sine, 0.0)


def to_a(v):
    rows = v.shape[0]
    return jnp.pad(v.reshape(rows, 4, 240), ((0, 0), (0, 0), (0, 16))).reshape(rows, WA)


def from_a(v):
    return v.reshape(v.shape[:-1] + (4, 256))[..., :240].reshape(v.shape[:-1] + (D,))


def place_matrices():
    a = jnp.arange(WA, dtype=jnp.int32)
    in_a = jnp.where(a % 256 < 240, (a // 256) * 240 + a % 256, -1)
    shard = (a // 16 % 4) * 16 + a // 64
    in_b = jnp.where(a % 16 < 15, shard * 15 + a % 16, -2)
    pab = (in_a[:, None] == in_b[None, :]).astype(bf16)
    pba = (in_b[:, None] == in_a[None, :]).astype(bf16)
    pnb = (jnp.arange(QW, dtype=jnp.int32)[:, None] == in_b[None, :]).astype(bf16)
    return pab, pba, pnb


def per_device(inputs, cotangent, segment_ids, gain_attn, w_qkv, w_out, gain_ffn, w_gate, w_up, w_down):
    core = lax.axis_index("section")
    gx = lax.axis_index("gx")
    gy = lax.axis_index("gy")
    first = core == 0
    place = {"x": gx, "z": gy // 4, "y": gy % 4}

    pieces = jnp.stack([w_gate[0].T, w_up[0].T, w_down[0]]).reshape(3, 2, 80, 240)
    keep = jnp.where(first, pieces[:, 0], pieces[:, 1])
    got = other_core(jnp.where(first, pieces[:, 1], pieces[:, 0]))
    halves = jnp.concatenate([jnp.where(first, keep, got), jnp.where(first, got, keep)], 0)
    halves = jnp.pad(halves.reshape(FROWS, 240), ((0, 0), (0, 16)))
    attn = jnp.concatenate(
        [
            w_qkv[0][:, QW:],
            gain_attn[0][:, None],
            gain_ffn[0][:, None],
            jnp.zeros((15, 126), bf16),
            w_qkv[0][:, :QW],
            jnp.zeros((15, 64), bf16),
            to_a(w_out[0]),
        ],
        1,
    )
    attn = jnp.pad(attn, ((0, 1), (0, 0))).reshape(16, 11, 256).transpose(1, 0, 2).reshape(AROWS, 256)
    own = lax.all_gather(attn[None], ("gx", "gy"), axis=0, tiled=True)
    own_in = to_a(jnp.where(first, inputs[0, 0], inputs[1, 0]))
    cot0, cot1 = to_a(cotangent[0, 0]), to_a(cotangent[1, 0])
    cot_own, cot_other = jnp.where(first, cot0, cot1), jnp.where(first, cot1, cot0)
    segments = jnp.where(first, segment_ids[0, 0], segment_ids[1, 0])
    local_ids = lax.dynamic_slice_in_dim(segments, gx * TOK, TOK, 0)
    own_index = gx * TOK + jnp.arange(TOK, dtype=jnp.int32)
    doc_start = jnp.sum((segments[None, :] < local_ids[:, None]).astype(jnp.int32), axis=1)
    key_index = (gx - 3) * TOK + jnp.arange(LEN, dtype=jnp.int32)
    key_ids = lax.dynamic_slice_in_dim(jnp.pad(segments, (3 * TOK, 0), constant_values=-1), gx * TOK, LEN, 0)
    mask = ((local_ids[:, None] == key_ids[None, :]) & (key_index[None, :] <= own_index[:, None])).astype(f32)
    cos_kv, cos_q, sin_kv, sin_q = rope_tables(own_index - doc_start)
    beside = [cos_kv, cos_q, sin_kv, sin_q, mask, own_in, cot_own, cot_other, *place_matrices()]
    early = [halves[:80], halves[80:160], halves[160:240]]
    beside, (own, second), finish = gather_chunks(early, beside, (own, halves[240:]))
    recv = other_core(own)
    packed = lax.all_gather(second[None], ("gx", "gy"), axis=0, tiled=True).reshape(4, 16, 240, 256)
    cos_kv, cos_q, sin_kv, sin_q, mask, own_in, cot_own, cot_other, pab, pba, pnb = beside
    ffn_weights = [None, [packed] * 3]

    def ahead(v, k):
        return lax.ppermute(v, "gx", [(i, i + k) for i in range(4 - k)])

    def back(v, k):
        return lax.ppermute(v, "gx", [(i + k, i) for i in range(4 - k)])

    def added(a, b):
        return (a.astype(f32) + b.astype(f32)).astype(bf16)

    def over_gy(v):
        rows = v.shape[-2]
        return lax.psum_scatter(v.reshape(16, 4 * rows, 256), "gy", scatter_dimension=0, tiled=True).reshape(4, rows, 256)

    grid = (4, 4, 4)
    gx_now = jnp.stack([gx, gy // 4, gy % 4]).astype(jnp.int32)
    sels = [core[None].astype(jnp.int32), (1 - core)[None].astype(jnp.int32)]
    kept = []
    x, parts = own_in, None
    for section in range(2):
        sel = sels[section]
        x, norm_b, kv, gains = key_value(sel, own, recv, pab, pba, cos_kv, sin_kv, x, parts)
        chunks = [ahead(kv, 1), ahead(kv, 2), ahead(kv, 3)]
        q = query(sel, own, recv, norm_b, cos_q, sin_q)
        if section == 0:
            q, first_ffn = finish(q)
            ffn_weights[0] = first_ffn
        attb, mid, n2 = attend(sel, own, recv, q, kv, chunks, mask, x, gains, pnb)
        n2_other = other_core(n2)
        if section == 0:
            yo, yr = ffn(section, gx_now, n2, n2_other, ffn_weights[section])
            parts = (mid, yo, other_core(yr))
        kept.append((x, norm_b, q, kv, gains, chunks, attb, mid, n2, n2_other))

    dy, dy_other = cot_own, cot_other
    grads_in, attn = [None, None], ()
    for section in (1, 0):
        sel = sels[section]
        x, norm_b, q, kv, gains, chunks, attb, mid, n2, n2_other = kept[section]
        grads, no, nr = ffn_back(section, gx_now, n2, n2_other, dy, dy_other, ffn_weights[section], attn)
        nr = other_core(nr)
        if section == 1:
            late1 = over_gy(grads)
        dmid, dproj, gg, dq, dkv, d1, d2, d3 = attend_back(
            sel, own, recv, no, nr, mid, gains, dy, q, kv, chunks, mask, pnb
        )
        back_chunks = [back(d1, 1), back(d2, 2), back(d3, 3)]
        dnq, keep_q, send_q = query_back(sel, sels[0], own, recv, dq, cos_q, sin_q, norm_b, attb, dproj)
        if section == 0:
            late1, grads, *back_chunks = lax.optimization_barrier((late1, grads, *back_chunks))
            late2 = over_gy(grads)
        send_q, *back_chunks = lax.optimization_barrier((send_q, *back_chunks))
        got_q = other_core(send_q)
        dy, keep_kv, send_kv = key_value_back(
            sel, sels[0], own, recv, dkv, *back_chunks, cos_kv, sin_kv, norm_b, x, gains, dmid, pba, dnq, gg
        )
        got_kv = other_core(send_kv)
        grads_in[section] = dy
        if section == 1:
            pairs = (keep_q, got_q, keep_kv, got_kv)
            dy, dy_other, *attn = lax.optimization_barrier((dy, other_core(dy), *pairs))
            attn = [v.reshape(grid + v.shape[1:]) for v in attn]

    _, n2, n2_other = lax.optimization_barrier((grads_in[0], *kept[1][-2:]))
    yo, yr = ffn(1, gx_now, n2, n2_other, ffn_weights[1])
    outs = [kept[1][0], (kept[1][7] + yo + other_core(yr)).astype(bf16)]

    attn0 = jnp.concatenate([added(keep_q, got_q), added(keep_kv, got_kv)], 1).reshape(grid + (96, 256))
    attn0 = reduce_axis(attn0, 2, "x", place)
    attn0 = reduce_axis(attn0, 0, "z", place)
    attn0 = reduce_axis(attn0, 0, "y", place)
    late = reduce_axis(jnp.concatenate([late1, late2], 1), 0, "x", place)
    half = [jnp.concatenate([late[240:480], attn0], 0), jnp.concatenate([late[:240], late[480:]], 0)]
    mine = jnp.where(first, half[0], half[1])
    theirs = other_core(jnp.where(first, half[1], half[0]))
    low, high = jnp.where(first, mine, theirs), jnp.where(first, theirs, mine)
    ff = jnp.concatenate([low[:240].reshape(3, 80, 256), high[:240].reshape(3, 80, 256)], 1)[:, :, :240].astype(f32)
    def columns(v):
        chunks = v.reshape(v.shape[0] // 16, 16, 256)[:, :15].astype(f32)
        return chunks.transpose(1, 0, 2).reshape(15, v.shape[0] * 16)

    q_grad, kv_grad = columns(low[240:304]), columns(jnp.concatenate([low[304:336], high[304:320]], 0))
    out_grad = from_a(columns(high[240:304]))
    grad_qkv = jnp.concatenate([q_grad[:, :QW], kv_grad[:, : 2 * KW]], 1)

    def placed(pair):
        a = jnp.where(first, pair[0], pair[1])
        b = other_core(jnp.where(first, pair[1], pair[0]))
        both = jnp.stack([jnp.where(first, a, b), jnp.where(first, b, a)])
        return from_a(both)[None, :, None]

    return (
        placed(outs),
        placed(grads_in),
        kv_grad[:, 640][None],
        grad_qkv[None],
        out_grad[None],
        kv_grad[:, 641][None],
        ff[0].T[None],
        ff[1].T[None],
        ff[2][None],
    )


def solution(mesh):
    return jax.shard_map(
        per_device,
        mesh=mesh,
        in_specs=(
            P(None, "gy", "gx", None),
            P(None, "gy", "gx", None),
            P(None, "gy", None),
            P("section", ("gx", "gy")),
            P("section", ("gx", "gy"), None),
            P("section", ("gx", "gy"), None),
            P("section", ("gx", "gy")),
            P("section", "gx", "gy"),
            P("section", "gx", "gy"),
            P("section", "gy", "gx"),
        ),
        out_specs=(
            P("section", None, "gy", "gx", None),
            P("section", None, "gy", "gx", None),
            P("section", ("gx", "gy")),
            P("section", ("gx", "gy"), None),
            P("section", ("gx", "gy"), None),
            P("section", ("gx", "gy")),
            P("section", "gx", "gy"),
            P("section", "gx", "gy"),
            P("section", "gy", "gx"),
        ),
        check_vma=False,
    )
```

```python
import functools

import jax
import jax.numpy as jnp
from jax import lax
from jax.experimental import pallas as pl
from jax.experimental.pallas import tpu as pltpu
from jax.sharding import PartitionSpec as P

HQ, HK, HD = 15, 5, 64
D, QW, KW = 960, 960, 320
TOK, LEN = 128, 512
WA = 1024
QKVW = 1792
FROWS, AROWS = 480, 176
epsilon = 1e-05
rope_base = 100000.0
masked_score = -1e30
VMEM = 60 * 2**20
bf16, f32 = jnp.bfloat16, jnp.float32


def nn(a, b):
    return jnp.dot(a, b, preferred_element_type=f32)


def nt(a, b):
    return lax.dot_general(a, b, (((1,), (1,)), ((), ())), preferred_element_type=f32)


def tn(a, b):
    return lax.dot_general(a, b, (((0,), (0,)), ((), ())), preferred_element_type=f32)


def call(kernel, outs, ins, specs, scratch=(), name=None):
    vm = pl.BlockSpec(memory_space=pltpu.VMEM)
    return pl.pallas_call(
        kernel,
        out_shape=outs,
        in_specs=specs,
        out_specs=[vm] * len(outs),
        scratch_shapes=list(scratch),
        compiler_params=pltpu.CompilerParams(vmem_limit_bytes=VMEM),
        name=name,
    )(*ins)


def stepped(kernel, place, outs, ins, specs, out_specs, scratch, name):
    return pl.pallas_call(
        kernel,
        out_shape=outs,
        grid_spec=pltpu.PrefetchScalarGridSpec(
            num_scalar_prefetch=1, grid=(4,), in_specs=specs, out_specs=out_specs, scratch_shapes=scratch
        ),
        compiler_params=pltpu.CompilerParams(vmem_limit_bytes=VMEM),
        name=name,
    )(place, *ins)


def sds(shape, dt):
    return jax.ShapeDtypeStruct(shape, dt)


def weight_copies(source, first, buf, sems):
    rows = buf.shape[2]
    return [
        pltpu.make_async_copy(source.at[pl.ds(16 * x, 16), pl.ds(first, rows), :], buf.at[:, x], sems.at[x])
        for x in range(4)
    ]


def pick(sel_ref, own, recv, first, buf, sems):
    @pl.when(sel_ref[0] == 0)
    def _():
        for copy in weight_copies(own, first, buf, sems):
            copy.start()

    @pl.when(sel_ref[0] != 0)
    def _():
        for copy in weight_copies(recv, first, buf, sems):
            copy.start()


def arrived(own, first, buf, sems):
    for copy in weight_copies(own, first, buf, sems):
        copy.wait()


def chunk_of(buf, j):
    return buf[:, :, 16 * j : 16 * j + 16, :].reshape(WA, 256)


def rstd_of(v):
    return lax.rsqrt(jnp.sum(v * v, axis=1, keepdims=True) * (1.0 / D) + epsilon)


def lane_in_head(shape):
    return lax.broadcasted_iota(jnp.int32, shape, 1) % HD


def rotated(v, cosw, sinw):
    low = lane_in_head(v.shape) < HD // 2
    turned = jnp.where(low, -pltpu.roll(v, v.shape[1] - 32, 1), pltpu.roll(v, 32, 1))
    return v * cosw[...] + turned * sinw[...]


def rotated_back(v, cosw, sinw):
    low = lane_in_head(v.shape) < HD // 2
    scaled = v * sinw[...]
    turned = jnp.where(low, pltpu.roll(scaled, v.shape[1] - 32, 1), -pltpu.roll(scaled, 32, 1))
    return v * cosw[...] + turned


def key_value_kernel(has_x, sel, own, recv, pab, cosw, sinw, *rest):
    if has_x:
        x_ref, norm_ref, kv_ref, gain_ref, buf, sems = rest
    else:
        mid_ref, yo_ref, yr_ref, x_out, norm_ref, kv_ref, gain_ref, buf, sems = rest
    pick(sel, own, recv, 0, buf, sems)
    if has_x:
        x = x_ref[...].astype(f32)
    else:
        xb = (mid_ref[...] + yo_ref[...] + yr_ref[...]).astype(bf16)
        x_out[...] = xb
        x = xb.astype(f32)
    rstd = rstd_of(x)
    arrived(own, 0, buf, sems)
    gains = nt(chunk_of(buf, 2)[:, 128:].astype(f32).T.astype(bf16), pab[...])[0:8, :]
    gain_ref[...] = gains
    normed = (x * rstd * gains[0:1, :]).astype(bf16)
    norm_b = nn(normed, pab[...]).astype(bf16)
    norm_ref[...] = norm_b
    proj = jnp.concatenate([nn(norm_b, chunk_of(buf, j)) for j in range(3)], axis=1)
    kv_ref[...] = rotated(proj, cosw, sinw).astype(bf16)[:, : 2 * KW]


def query_kernel(sel, own, recv, norm_ref, cosw, sinw, q_ref, buf, sems):
    pick(sel, own, recv, 48, buf, sems)
    arrived(own, 48, buf, sems)
    proj = jnp.concatenate([nn(norm_ref[...], chunk_of(buf, j)) for j in range(4)], axis=1)
    q_ref[...] = rotated(proj, cosw, sinw).astype(bf16)


def heads_of(ref, i):
    return jnp.concatenate([ref[:, HD * (3 * i + h) : HD * (3 * i + h + 1)] for h in range(3)], axis=0)


def softmax_terms(q3, kg, allowed3):
    scores = nt(q3, kg) * 0.125
    scores = jnp.where(allowed3, scores, masked_score)
    highest = jnp.max(scores, axis=1, keepdims=True)
    terms = jnp.exp(scores - highest)
    return terms / jnp.sum(terms, axis=1, keepdims=True)


def attend_kernel(sel, own, recv, q, kv, r1, r2, r3, mask, x_ref, gain_ref, pnb, attb_ref, mid_ref, n2_ref, buf, kvs, att, sems):
    pick(sel, own, recv, 112, buf, sems)
    for k, part in enumerate((r3, r2, r1)):
        kvs[TOK * k : TOK * k + TOK, :] = part[...]
    kvs[3 * TOK :, :] = kv[...]
    allowed = mask[...] > 0.5
    allowed3 = jnp.concatenate([allowed] * 3, axis=0)
    for i in range(HK):
        kg = kvs[:, HD * i : HD * i + HD]
        vg = kvs[:, KW + HD * i : KW + HD * i + HD]
        probs = softmax_terms(heads_of(q, i), kg, allowed3).astype(bf16)
        o3 = nn(probs, vg).astype(bf16)
        for h in range(3):
            lane = HD * (3 * i + h)
            att[:, lane : lane + HD] = o3[TOK * h : TOK * h + TOK, :]
    attb = nn(att[...], pnb[...]).astype(bf16)
    attb_ref[...] = attb
    arrived(own, 112, buf, sems)
    out = jnp.concatenate([nn(attb, chunk_of(buf, j)) for j in range(4)], axis=1)
    mid = x_ref[...].astype(f32) + out
    mid_ref[...] = mid
    n2_ref[...] = (mid * rstd_of(mid) * gain_ref[1:2, :]).astype(bf16)


def tile_of(w, g, section):
    if section == 1:
        return w[g].reshape(320, 256)
    if not isinstance(w, tuple):
        return w[:, g].reshape(320, 256)
    if w[0].shape[0] == 1:
        return jnp.concatenate([part[0, g] for part in w], axis=0)
    return w[g][:, 0].reshape(320, 256)


def weight_refs(section, refs):
    if section == 1:
        return refs[0], refs[1], refs[2], refs[3:]
    *refs, down = refs
    for i in range(4):

        @pl.when(pl.program_id(0) == i)
        def _(i=i):
            down[...] = refs[8 + i][...]

    return tuple(refs[:4]), tuple(refs[4:8]), down, refs[12:]


def lanes(gx, g, section):
    if section == 0:
        return pl.ds(pl.multiple_of((gx[0] + g) % 4 * 256, 256), 256)
    return pl.ds(256 * g, 256)


def hidden_parts(gx, xs, wg, wu, section):
    gate = up = None
    for g in range(4):
        xg = xs[:, lanes(gx, g, section)]
        a, b = nt(xg, tile_of(wg, g, section)), nt(xg, tile_of(wu, g, section))
        gate, up = (a, b) if g == 0 else (gate + a, up + b)
    return gate, up, 1.0 / (1.0 + jnp.exp(-gate))


def ffn_kernel(section, gx, xo, xr, *refs):
    wg, wu, wd, (yo, yr, xs) = weight_refs(section, refs)
    j = pl.program_id(0)

    @pl.when(j == 0)
    def _():
        yo[...] = jnp.zeros_like(yo)
        yr[...] = jnp.zeros_like(yr)
        xs[:TOK] = xo[...]
        xs[TOK:] = xr[...]

    gate, up, sigma = hidden_parts(gx, xs, wg, wu, section)
    hidden = (gate * sigma * up).astype(bf16)
    for g in range(4):
        y = nn(hidden, tile_of(wd, g, section))
        yo[:, lanes(gx, g, section)] += y[:TOK]
        yr[:, lanes(gx, g, section)] += y[TOK:]


def ffn_back_kernel(section, gx, xo, xr, do, dr, *refs):
    wg, wu, wd, rest = weight_refs(section, refs)
    *attn, grads, no, nr, xs, ds = rest
    if section == 0:
        row = 240
        for mine, other in ((attn[0], attn[1]), (attn[2], attn[3])):
            rows = mine.shape[3]
            grads[:, :, :, row : row + rows, :] = (mine[...].astype(f32) + other[...].astype(f32)).astype(bf16)
            row += rows
    j = pl.program_id(0)

    @pl.when(j == 0)
    def _():
        no[...] = jnp.zeros_like(no)
        nr[...] = jnp.zeros_like(nr)
        xs[:TOK] = xo[...]
        xs[TOK:] = xr[...]
        ds[:TOK] = do[...]
        ds[TOK:] = dr[...]

    gate, up, sigma = hidden_parts(gx, xs, wg, wu, section)
    hidden = gate * sigma * up
    d_hidden = None
    for g in range(4):
        a = nt(ds[:, lanes(gx, g, section)], tile_of(wd, g, section))
        d_hidden = a if g == 0 else d_hidden + a
    d_gate = (d_hidden * up * sigma * (1.0 + gate * (1.0 - sigma))).astype(bf16)
    d_up = (d_hidden * gate * sigma).astype(bf16)
    hid_t = hidden.astype(bf16).T
    dg_t = d_gate.T
    du_t = d_up.T
    for g in range(4):
        xg, dg = xs[:, lanes(gx, g, section)], ds[:, lanes(gx, g, section)]
        values = (nn(dg_t, xg), nn(du_t, xg), nn(hid_t, dg))
        for m, value in enumerate(values):
            value = value.astype(bf16).reshape(4, 80, 256)
            if section == 0:
                for i in range(4):
                    grads[(gx[1] + i) % 4, 0, (gx[0] + g) % 4, 80 * m : 80 * m + 80, :] = value[i]
            else:
                grads[:, g, 80 * m : 80 * m + 80, :] = value
        dn = nn(d_gate, tile_of(wg, g, section)) + nn(d_up, tile_of(wu, g, section))
        no[:, lanes(gx, g, section)] += dn[:TOK]
        nr[:, lanes(gx, g, section)] += dn[TOK:]


def norm_back(e, z, rstd):
    return rstd * (e - z * (jnp.sum(e * z, axis=1, keepdims=True) * (1.0 / D)))


def attend_back_kernel(
    sel, own, recv, no, nr, mid_ref, gain_ref, dy_ref, q, kv, r1, r2, r3, mask, pnb,
    dmid_ref, dproj_ref, gg_ref, dq_ref, dkv_ref, d1, d2, d3, buf, kvs, dkv, sems,
):
    pick(sel, own, recv, 112, buf, sems)
    for k, part in enumerate((r3, r2, r1)):
        kvs[TOK * k : TOK * k + TOK, :] = part[...]
    kvs[3 * TOK :, :] = kv[...]
    mid = mid_ref[...]
    rstd = rstd_of(mid)
    z = mid * rstd
    dn = no[...] + nr[...]
    gg_ref[...] = jnp.broadcast_to(jnp.sum(dn * z, axis=0, keepdims=True), gg_ref.shape)
    dmid = dy_ref[...].astype(f32) + norm_back(dn * gain_ref[1:2, :], z, rstd)
    dmid_ref[...] = dmid
    dproj = dmid.astype(bf16)
    dproj_ref[...] = dproj
    arrived(own, 112, buf, sems)
    datt = None
    for j in range(4):
        a = nt(dproj[:, 256 * j : 256 * j + 256], chunk_of(buf, j))
        datt = a if j == 0 else datt + a
    datt = nt(datt.astype(bf16), pnb[...]).astype(bf16)
    allowed = mask[...] > 0.5
    allowed3 = jnp.concatenate([allowed] * 3, axis=0)
    dq_ref[:, 896:] = jnp.zeros((TOK, 128), f32)
    for i in range(HK):
        kg = kvs[:, HD * i : HD * i + HD]
        vg = kvs[:, KW + HD * i : KW + HD * i + HD]
        q3 = heads_of(q, i)
        do3 = heads_of(datt, i)
        probs = softmax_terms(q3, kg, allowed3)
        d_probs = nt(do3, vg)
        inner = jnp.sum(probs * d_probs, axis=1, keepdims=True)
        d_scores = (probs * (d_probs - inner)).astype(bf16)
        dq3 = nn(d_scores, kg) * 0.125
        for h in range(3):
            lane = HD * (3 * i + h)
            dq_ref[:, lane : lane + HD] = dq3[TOK * h : TOK * h + TOK, :]
        dkv[:, HD * i : HD * i + HD] = tn(d_scores, q3) * 0.125
        dkv[:, KW + HD * i : KW + HD * i + HD] = tn(probs.astype(bf16), do3)
    dkv_ref[...] = dkv[3 * TOK :, :]
    for k, part in enumerate((d3, d2, d1)):
        part[...] = dkv[TOK * k : TOK * k + TOK, :].astype(bf16)


def split3(v):
    hi = v.astype(bf16)
    rest = v - hi.astype(f32)
    middle = rest.astype(bf16)
    return hi, middle, (rest - middle.astype(f32)).astype(bf16)


def query_back_kernel(
    sel, core, own, recv, dq, cosw, sinw, norm_ref, attb, dproj, dn_ref, keep, send, buf, left, right, sems,
):
    pick(sel, own, recv, 48, buf, sems)
    dp = rotated_back(dq[...], cosw, sinw).astype(bf16)
    left[0] = norm_ref[...].T
    left[1] = attb[...].T
    for j in range(4):
        right[j] = dp[:, 256 * j : 256 * j + 256]
        right[4 + j] = dproj[:, 256 * j : 256 * j + 256]
    for target, half in ((keep, core[0]), (send, 1 - core[0])):
        for j in range(4):
            target[:, 16 * j : 16 * j + 16, :] = nn(left[half], right[4 * half + j]).astype(bf16).reshape(64, 16, 256)
    arrived(own, 48, buf, sems)
    dn = None
    for j in range(4):
        a = nt(dp[:, 256 * j : 256 * j + 256], chunk_of(buf, j))
        dn = a if j == 0 else dn + a
    dn_ref[...] = dn


def key_value_back_kernel(
    sel, core, own, recv, dkv, e1, e2, e3, cosw, sinw, norm_ref, x_ref, gain_ref, dmid_ref, pba, dnq, gg,
    dx_ref, keep, send, buf, right, sems,
):
    pick(sel, own, recv, 0, buf, sems)
    kv = dkv[...] + e1[...].astype(f32) + e2[...].astype(f32) + e3[...].astype(f32)
    d = jnp.concatenate([kv, jnp.zeros((TOK, 128), f32)], axis=1)
    dp = rotated_back(d, cosw, sinw).astype(bf16)
    arrived(own, 0, buf, sems)
    dn_b = dnq[...]
    for j in range(3):
        dn_b = dn_b + nt(dp[:, 256 * j : 256 * j + 256], chunk_of(buf, j))
        right[j] = dp[:, 256 * j : 256 * j + 256]
    right[3] = jnp.zeros((TOK, 256), bf16)
    hi, middle, lo = split3(dn_b)
    dn = nn(hi, pba[...]) + nn(middle, pba[...]) + nn(lo, pba[...])
    x = x_ref[...].astype(f32)
    rstd = rstd_of(x)
    z = x * rstd
    g1 = jnp.sum(dn * z, axis=0, keepdims=True)
    dx_ref[...] = (dmid_ref[...] + norm_back(dn * gain_ref[0:1, :], z, rstd)).astype(bf16)
    row = lax.broadcasted_iota(jnp.int32, (256, WA), 0)
    gains = jnp.where(row == 128, g1, jnp.where(row == 129, gg[0:1, :], 0.0)).astype(bf16)
    gains = nt(pba[...], gains)
    norm_t = norm_ref[...].T
    for target, half in ((keep, core[0]), (send, 1 - core[0])):
        for j in range(2):
            g = nn(norm_t, right[2 * half + j])
            if j == 0:
                g = g + gains * half.astype(f32)
            target[:, 16 * j : 16 * j + 16, :] = g.astype(bf16).reshape(64, 16, 256)


VM = pl.BlockSpec(memory_space=pltpu.VMEM)
ANY = pl.BlockSpec(memory_space=pl.ANY)
SM = pl.BlockSpec(memory_space=pltpu.SMEM)


def weight_scratch(rows):
    return pltpu.VMEM((16, 4, rows, 256), bf16)


def key_value(sel, own, recv, pab, cosw, sinw, x=None, parts=None):
    outs = [sds((TOK, WA), bf16), sds((TOK, 2 * KW), bf16), sds((8, WA), f32)]
    ins = [sel, own, recv, pab, cosw, sinw] + ([x] if parts is None else list(parts))
    if parts is not None:
        outs = [sds((TOK, WA), bf16)] + outs
    res = call(
        functools.partial(key_value_kernel, parts is None),
        outs, ins, [SM, ANY, ANY] + [VM] * (len(ins) - 3),
        [weight_scratch(48), pltpu.SemaphoreType.DMA((4,))], name="key_value",
    )
    return ([x] + list(res)) if parts is None else res


def query(sel, own, recv, *rest):
    return call(
        query_kernel, [sds((TOK, WA), bf16)], [sel, own, recv, *rest], [SM, ANY, ANY] + [VM] * len(rest),
        [weight_scratch(64), pltpu.SemaphoreType.DMA((4,))], name="query",
    )[0]


def attend(sel, own, recv, q, kv, chunks, mask, x, gains, pnb):
    ins = [sel, own, recv, q, kv, *chunks, mask, x, gains, pnb]
    return call(
        attend_kernel,
        [sds((TOK, WA), bf16), sds((TOK, WA), f32), sds((TOK, WA), bf16)],
        ins, [SM, ANY, ANY] + [VM] * (len(ins) - 3),
        [weight_scratch(64), pltpu.VMEM((LEN, 2 * KW), bf16), pltpu.VMEM((TOK, QW), bf16), pltpu.SemaphoreType.DMA((4,))],
        name="attend",
    )


def weight_specs(section):
    if section == 0:
        by_z = [pl.BlockSpec((1, 4, 80, 256), lambda j, p: (j, 0, 0, 0)) for _ in range(4)]
        by_x = [pl.BlockSpec((4, 1, 80, 256), lambda j, p: (0, j, 0, 0)) for _ in range(4)]
        return by_z + by_x + [whole((4, 4, 80, 256)) for _ in range(4)]
    return [pl.BlockSpec((4, 4, 80, 256), lambda j, p, m=m: (0, j, m, 0)) for m in range(3)]


def down_scratch(section):
    return [pltpu.VMEM((4, 4, 80, 256), bf16)] if section == 0 else []


def whole(shape):
    return pl.BlockSpec(shape, lambda j, p: (0,) * len(shape))


def ffn(section, place, xo, xr, packed):
    row = whole((TOK, WA))
    return stepped(
        functools.partial(ffn_kernel, section), place, [sds((TOK, WA), f32)] * 2, [xo, xr, *packed],
        [row, row] + weight_specs(section), [row, row], [pltpu.VMEM((2 * TOK, WA), bf16)] + down_scratch(section), "ffn",
    )


def ffn_back(section, place, xo, xr, do, dr, packed, attn=()):
    row = whole((TOK, WA))
    if section == 1:
        grads, block = sds((16, 4, 240, 256), bf16), pl.BlockSpec((4, 4, 240, 256), lambda j, p: (j, 0, 0, 0))
    else:
        grads = sds((4, 4, 4, 336, 256), bf16)
        block = pl.BlockSpec((4, 1, 4, 336, 256), lambda j, p: (0, (p[2] + j) % 4, 0, 0, 0))
    attn_specs = [pl.BlockSpec((4, 1) + v.shape[2:], lambda j, p: (0, (p[2] + j) % 4, 0, 0, 0)) for v in attn]
    return stepped(
        functools.partial(ffn_back_kernel, section), place, [grads] + [sds((TOK, WA), f32)] * 2,
        [xo, xr, do, dr, *packed, *attn],
        [row] * 4 + weight_specs(section) + attn_specs, [block, row, row],
        [pltpu.VMEM((2 * TOK, WA), bf16)] * 2 + down_scratch(section), "ffn_back",
    )


def attend_back(sel, own, recv, no, nr, mid, gains, dy, q, kv, chunks, mask, pnb):
    ins = [sel, own, recv, no, nr, mid, gains, dy, q, kv, *chunks, mask, pnb]
    small = sds((TOK, 2 * KW), bf16)
    return call(
        attend_back_kernel,
        [sds((TOK, WA), f32), sds((TOK, WA), bf16), sds((8, WA), f32), sds((TOK, WA), f32), sds((TOK, 2 * KW), f32), small, small, small],
        ins, [SM, ANY, ANY] + [VM] * (len(ins) - 3),
        [weight_scratch(64), pltpu.VMEM((LEN, 2 * KW), bf16), pltpu.VMEM((LEN, 2 * KW), f32), pltpu.SemaphoreType.DMA((4,))],
        name="attend_back",
    )


def query_back(sel, core, own, recv, *rest):
    return call(
        query_back_kernel, [sds((TOK, WA), f32)] + [sds((64, 64, 256), bf16)] * 2,
        [sel, core, own, recv, *rest], [SM, SM, ANY, ANY] + [VM] * len(rest),
        [weight_scratch(64), pltpu.VMEM((2, WA, TOK), bf16), pltpu.VMEM((8, TOK, 256), bf16), pltpu.SemaphoreType.DMA((4,))],
        name="query_back",
    )


def key_value_back(sel, core, own, recv, *rest):
    return call(
        key_value_back_kernel, [sds((TOK, WA), bf16)] + [sds((64, 32, 256), bf16)] * 2,
        [sel, core, own, recv, *rest], [SM, SM, ANY, ANY] + [VM] * len(rest),
        [weight_scratch(48), pltpu.VMEM((4, TOK, 256), bf16), pltpu.SemaphoreType.DMA((4,))],
        name="key_value_back",
    )


def other_core(v):
    return lax.ppermute(v, "section", [(0, 1), (1, 0)])


def shift_perm(name, k):
    if name == "x":
        return "gx", [(i, (i + k) % 4) for i in range(4)]
    if name == "z":
        return "gy", [(i, (i + 4 * k) % 16) for i in range(16)]
    return "gy", [(i, (i // 4) * 4 + (i % 4 + k) % 4) for i in range(16)]


def permuted(v, name, k):
    axis, perm = shift_perm(name, k)
    return lax.ppermute(v, axis, perm)


ORDERS = (("x", "y", "z"), ("y", "z", "x"), ("z", "x", "y"))
GROUPS = (((0, 1), (0, 3), (1, 1), (1, 3), (2, 2)), ((0, 2), (1, 2), (2, 1), (2, 3)))


def exchange(pieces, names, grouped, beside=()):
    keys = list(pieces)
    pieces = dict(zip(keys, lax.optimization_barrier([pieces[key] for key in keys])))
    if not grouped:
        return {key: permuted(pieces[key], names[key[0]], key[1]) for key in keys}, beside
    got = {key: permuted(pieces[key], names[key[0]], key[1]) for key in GROUPS[0]}
    tied = lax.optimization_barrier([[got[key] for key in GROUPS[0]], [pieces[key] for key in GROUPS[1]], list(beside)])
    got = dict(zip(GROUPS[0], tied[0]))
    for key, piece in zip(GROUPS[1], tied[1]):
        got[key] = permuted(piece, names[key[0]], key[1])
    return got, tied[2]


def gather_chunks(chunks, beside, after_first):
    state = [(c, ()) for c in chunks]

    def joined(got, names):
        after = []
        for c in range(3):
            v, have = state[c]
            have = tuple(n for n in ("z", "y", "x") if n in have or n == names[c])
            v = jnp.stack([v, got[(c, 3)], got[(c, 2)], got[(c, 1)]], axis=have.index(names[c]))
            after.append((v, have))
        return after

    for step in range(3):
        names = [order[step] for order in ORDERS]
        pieces = {(c, k): state[c][0] for c in range(3) for k in (1, 2, 3)}
        got, tied = exchange(pieces, names, step >= 1, ((), beside, after_first)[step])
        if step < 2:
            state = joined(got, names)
        beside, after_first = (tied if step == 1 else beside), (tied if step == 2 else after_first)

    def finish(value):
        keys = list(got)
        value, parts = lax.optimization_barrier((value, [got[key] for key in keys]))
        parts = dict(zip(keys, parts))
        apart = [[state[c][0], parts[(c, 3)], parts[(c, 2)], parts[(c, 1)]] for c in range(3)]
        return value, apart[0] + apart[1] + apart[2]

    return beside, after_first, finish


def reduce_axis(v, dim, name, place):
    me = place[name]
    pieces = [lax.dynamic_index_in_dim(v, (me + k) % 4, dim, keepdims=False) for k in (1, 3, 2)]
    pieces = lax.optimization_barrier(pieces)
    total = lax.dynamic_index_in_dim(v, me, dim, keepdims=False).astype(f32)
    for piece, k in zip(pieces, (1, 3, 2)):
        total = total + permuted(piece, name, k).astype(f32)
    return total.astype(bf16)


def rope_tables(positions):
    frequency = rope_base ** (-(jnp.arange(HD // 2, dtype=f32) * 2.0) / HD)
    angles = positions.astype(f32)[:, None] * frequency[None, :]
    cosine, sine = jnp.cos(angles), jnp.sin(angles)
    cosine, sine = jnp.concatenate([cosine, cosine], 1), jnp.concatenate([sine, sine], 1)

    def wide(table, plain):
        key = jnp.concatenate([jnp.tile(table, (1, HK)), jnp.full((TOK, 448), plain, f32)], 1)
        return key, jnp.concatenate([jnp.tile(table, (1, HQ)), jnp.full((TOK, 64), plain, f32)], 1)

    return wide(cosine, 1.0) + wide(sine, 0.0)


def to_a(v):
    rows = v.shape[0]
    return jnp.pad(v.reshape(rows, 4, 240), ((0, 0), (0, 0), (0, 16))).reshape(rows, WA)


def from_a(v):
    return v.reshape(v.shape[:-1] + (4, 256))[..., :240].reshape(v.shape[:-1] + (D,))


def place_matrices():
    a = jnp.arange(WA, dtype=jnp.int32)
    in_a = jnp.where(a % 256 < 240, (a // 256) * 240 + a % 256, -1)
    shard = (a // 16 % 4) * 16 + a // 64
    in_b = jnp.where(a % 16 < 15, shard * 15 + a % 16, -2)
    pab = (in_a[:, None] == in_b[None, :]).astype(bf16)
    pba = (in_b[:, None] == in_a[None, :]).astype(bf16)
    pnb = (jnp.arange(QW, dtype=jnp.int32)[:, None] == in_b[None, :]).astype(bf16)
    return pab, pba, pnb


def per_device(inputs, cotangent, segment_ids, gain_attn, w_qkv, w_out, gain_ffn, w_gate, w_up, w_down):
    core = lax.axis_index("section")
    gx = lax.axis_index("gx")
    gy = lax.axis_index("gy")
    first = core == 0
    place = {"x": gx, "z": gy // 4, "y": gy % 4}

    pieces = jnp.stack([w_gate[0].T, w_up[0].T, w_down[0]]).reshape(3, 2, 80, 240)
    keep = jnp.where(first, pieces[:, 0], pieces[:, 1])
    got = other_core(jnp.where(first, pieces[:, 1], pieces[:, 0]))
    halves = jnp.concatenate([jnp.where(first, keep, got), jnp.where(first, got, keep)], 0)
    halves = jnp.pad(halves.reshape(FROWS, 240), ((0, 0), (0, 16)))
    attn = jnp.concatenate(
        [
            w_qkv[0][:, QW:],
            gain_attn[0][:, None],
            gain_ffn[0][:, None],
            jnp.zeros((15, 126), bf16),
            w_qkv[0][:, :QW],
            jnp.zeros((15, 64), bf16),
            to_a(w_out[0]),
        ],
        1,
    )
    attn = jnp.pad(attn, ((0, 1), (0, 0))).reshape(16, 11, 256).transpose(1, 0, 2).reshape(AROWS, 256)
    own = lax.all_gather(attn[None], ("gx", "gy"), axis=0, tiled=True)
    own_in = to_a(jnp.where(first, inputs[0, 0], inputs[1, 0]))
    cot0, cot1 = to_a(cotangent[0, 0]), to_a(cotangent[1, 0])
    cot_own, cot_other = jnp.where(first, cot0, cot1), jnp.where(first, cot1, cot0)
    segments = jnp.where(first, segment_ids[0, 0], segment_ids[1, 0])
    local_ids = lax.dynamic_slice_in_dim(segments, gx * TOK, TOK, 0)
    own_index = gx * TOK + jnp.arange(TOK, dtype=jnp.int32)
    doc_start = jnp.sum((segments[None, :] < local_ids[:, None]).astype(jnp.int32), axis=1)
    key_index = (gx - 3) * TOK + jnp.arange(LEN, dtype=jnp.int32)
    key_ids = lax.dynamic_slice_in_dim(jnp.pad(segments, (3 * TOK, 0), constant_values=-1), gx * TOK, LEN, 0)
    mask = ((local_ids[:, None] == key_ids[None, :]) & (key_index[None, :] <= own_index[:, None])).astype(f32)
    cos_kv, cos_q, sin_kv, sin_q = rope_tables(own_index - doc_start)
    beside = [cos_kv, cos_q, sin_kv, sin_q, mask, own_in, cot_own, cot_other, *place_matrices()]
    early = [halves[:80], halves[80:160], halves[160:240]]
    beside, (own, second), finish = gather_chunks(early, beside, (own, halves[240:]))
    recv = other_core(own)
    packed = lax.all_gather(second[None], ("gx", "gy"), axis=0, tiled=True).reshape(4, 16, 240, 256)
    cos_kv, cos_q, sin_kv, sin_q, mask, own_in, cot_own, cot_other, pab, pba, pnb = beside
    ffn_weights = [None, [packed] * 3]

    def ahead(v, k):
        return lax.ppermute(v, "gx", [(i, i + k) for i in range(4 - k)])

    def back(v, k):
        return lax.ppermute(v, "gx", [(i + k, i) for i in range(4 - k)])

    def added(a, b):
        return (a.astype(f32) + b.astype(f32)).astype(bf16)

    def over_gy(v):
        rows = v.shape[-2]
        return lax.psum_scatter(v.reshape(16, 4 * rows, 256), "gy", scatter_dimension=0, tiled=True).reshape(4, rows, 256)

    grid = (4, 4, 4)
    gx_now = jnp.stack([gx, gy // 4, gy % 4]).astype(jnp.int32)
    sels = [core[None].astype(jnp.int32), (1 - core)[None].astype(jnp.int32)]
    kept = []
    x, parts = own_in, None
    for section in range(2):
        sel = sels[section]
        x, norm_b, kv, gains = key_value(sel, own, recv, pab, cos_kv, sin_kv, x, parts)
        chunks = [ahead(kv, 1), ahead(kv, 2), ahead(kv, 3)]
        q = query(sel, own, recv, norm_b, cos_q, sin_q)
        if section == 0:
            q, first_ffn = finish(q)
            ffn_weights[0] = first_ffn
        attb, mid, n2 = attend(sel, own, recv, q, kv, chunks, mask, x, gains, pnb)
        n2_other = other_core(n2)
        if section == 0:
            yo, yr = ffn(section, gx_now, n2, n2_other, ffn_weights[section])
            parts = (mid, yo, other_core(yr))
        kept.append((x, norm_b, q, kv, gains, chunks, attb, mid, n2, n2_other))

    dy, dy_other = cot_own, cot_other
    grads_in, attn = [None, None], ()
    for section in (1, 0):
        sel = sels[section]
        x, norm_b, q, kv, gains, chunks, attb, mid, n2, n2_other = kept[section]
        grads, no, nr = ffn_back(section, gx_now, n2, n2_other, dy, dy_other, ffn_weights[section], attn)
        nr = other_core(nr)
        if section == 1:
            late1 = over_gy(grads)
        dmid, dproj, gg, dq, dkv, d1, d2, d3 = attend_back(
            sel, own, recv, no, nr, mid, gains, dy, q, kv, chunks, mask, pnb
        )
        back_chunks = [back(d1, 1), back(d2, 2), back(d3, 3)]
        dnq, keep_q, send_q = query_back(sel, sels[0], own, recv, dq, cos_q, sin_q, norm_b, attb, dproj)
        if section == 0:
            late1, grads, *back_chunks = lax.optimization_barrier((late1, grads, *back_chunks))
            late2 = over_gy(grads)
        send_q, *back_chunks = lax.optimization_barrier((send_q, *back_chunks))
        got_q = other_core(send_q)
        dy, keep_kv, send_kv = key_value_back(
            sel, sels[0], own, recv, dkv, *back_chunks, cos_kv, sin_kv, norm_b, x, gains, dmid, pba, dnq, gg
        )
        got_kv = other_core(send_kv)
        grads_in[section] = dy
        if section == 1:
            pairs = (keep_q, got_q, keep_kv, got_kv)
            dy, dy_other, *attn = lax.optimization_barrier((dy, other_core(dy), *pairs))
            attn = [v.reshape(grid + v.shape[1:]) for v in attn]

    _, n2, n2_other = lax.optimization_barrier((grads_in[0], *kept[1][-2:]))
    yo, yr = ffn(1, gx_now, n2, n2_other, ffn_weights[1])
    outs = [kept[1][0], (kept[1][7] + yo + other_core(yr)).astype(bf16)]

    attn0 = jnp.concatenate([added(keep_q, got_q), added(keep_kv, got_kv)], 1).reshape(grid + (96, 256))
    attn0 = reduce_axis(attn0, 2, "x", place)
    attn0, late1 = lax.optimization_barrier((attn0, reduce_axis(late1, 0, "x", place)))
    attn0 = reduce_axis(attn0, 0, "z", place)
    attn0 = reduce_axis(attn0, 0, "y", place)
    late2 = reduce_axis(late2, 0, "x", place)
    half = [jnp.concatenate([late2[:240], attn0], 0), jnp.concatenate([late1, late2[240:]], 0)]
    mine = jnp.where(first, half[0], half[1])
    theirs = other_core(jnp.where(first, half[1], half[0]))
    low, high = jnp.where(first, mine, theirs), jnp.where(first, theirs, mine)
    ff = jnp.concatenate([low[:240].reshape(3, 80, 256), high[:240].reshape(3, 80, 256)], 1)[:, :, :240].astype(f32)
    def columns(v):
        chunks = v.reshape(v.shape[0] // 16, 16, 256)[:, :15].astype(f32)
        return chunks.transpose(1, 0, 2).reshape(15, v.shape[0] * 16)

    q_grad, kv_grad = columns(low[240:304]), columns(jnp.concatenate([low[304:336], high[304:320]], 0))
    out_grad = from_a(columns(high[240:304]))
    grad_qkv = jnp.concatenate([q_grad[:, :QW], kv_grad[:, : 2 * KW]], 1)

    def placed(pair):
        a = jnp.where(first, pair[0], pair[1])
        b = other_core(jnp.where(first, pair[1], pair[0]))
        both = jnp.stack([jnp.where(first, a, b), jnp.where(first, b, a)])
        return from_a(both)[None, :, None]

    return (
        placed(outs),
        placed(grads_in),
        kv_grad[:, 640][None],
        grad_qkv[None],
        out_grad[None],
        kv_grad[:, 641][None],
        ff[0].T[None],
        ff[1].T[None],
        ff[2][None],
    )


def solution(mesh):
    return jax.shard_map(
        per_device,
        mesh=mesh,
        in_specs=(
            P(None, "gy", "gx", None),
            P(None, "gy", "gx", None),
            P(None, "gy", None),
            P("section", ("gx", "gy")),
            P("section", ("gx", "gy"), None),
            P("section", ("gx", "gy"), None),
            P("section", ("gx", "gy")),
            P("section", "gx", "gy"),
            P("section", "gx", "gy"),
            P("section", "gy", "gx"),
        ),
        out_specs=(
            P("section", None, "gy", "gx", None),
            P("section", None, "gy", "gx", None),
            P("section", ("gx", "gy")),
            P("section", ("gx", "gy"), None),
            P("section", ("gx", "gy"), None),
            P("section", ("gx", "gy")),
            P("section", "gx", "gy"),
            P("section", "gx", "gy"),
            P("section", "gy", "gx"),
        ),
        check_vma=False,
    )
```

```python
import functools

import jax
import jax.numpy as jnp
from jax import lax
from jax.experimental import pallas as pl
from jax.experimental.pallas import tpu as pltpu
from jax.sharding import PartitionSpec as P

HQ, HK, HD = 15, 5, 64
D, QW, KW = 960, 960, 320
TOK, LEN = 128, 512
WA = 1024
QKVW = 1792
FROWS, AROWS = 480, 176
epsilon = 1e-05
rope_base = 100000.0
masked_score = -1e30
VMEM = 60 * 2**20
bf16, f32 = jnp.bfloat16, jnp.float32


def nn(a, b):
    return jnp.dot(a, b, preferred_element_type=f32)


def nt(a, b):
    return lax.dot_general(a, b, (((1,), (1,)), ((), ())), preferred_element_type=f32)


def tn(a, b):
    return lax.dot_general(a, b, (((0,), (0,)), ((), ())), preferred_element_type=f32)


def call(kernel, outs, ins, specs, scratch=(), name=None):
    vm = pl.BlockSpec(memory_space=pltpu.VMEM)
    return pl.pallas_call(
        kernel,
        out_shape=outs,
        in_specs=specs,
        out_specs=[vm] * len(outs),
        scratch_shapes=list(scratch),
        compiler_params=pltpu.CompilerParams(vmem_limit_bytes=VMEM),
        name=name,
    )(*ins)


def stepped(kernel, place, outs, ins, specs, out_specs, scratch, name):
    return pl.pallas_call(
        kernel,
        out_shape=outs,
        grid_spec=pltpu.PrefetchScalarGridSpec(
            num_scalar_prefetch=1, grid=(4,), in_specs=specs, out_specs=out_specs, scratch_shapes=scratch
        ),
        compiler_params=pltpu.CompilerParams(vmem_limit_bytes=VMEM),
        name=name,
    )(place, *ins)


def sds(shape, dt):
    return jax.ShapeDtypeStruct(shape, dt)


def weight_copies(source, first, buf, sems):
    rows = buf.shape[2]
    return [
        pltpu.make_async_copy(source.at[pl.ds(16 * x, 16), pl.ds(first, rows), :], buf.at[:, x], sems.at[x])
        for x in range(4)
    ]


def pick(sel_ref, own, recv, first, buf, sems):
    @pl.when(sel_ref[0] == 0)
    def _():
        for copy in weight_copies(own, first, buf, sems):
            copy.start()

    @pl.when(sel_ref[0] != 0)
    def _():
        for copy in weight_copies(recv, first, buf, sems):
            copy.start()


def arrived(own, first, buf, sems):
    for copy in weight_copies(own, first, buf, sems):
        copy.wait()


def chunk_of(buf, j):
    return buf[:, :, 16 * j : 16 * j + 16, :].reshape(WA, 256)


def rstd_of(v):
    return lax.rsqrt(jnp.sum(v * v, axis=1, keepdims=True) * (1.0 / D) + epsilon)


def lane_in_head(shape):
    return lax.broadcasted_iota(jnp.int32, shape, 1) % HD


def rotated(v, cosw, sinw):
    low = lane_in_head(v.shape) < HD // 2
    turned = jnp.where(low, -pltpu.roll(v, v.shape[1] - 32, 1), pltpu.roll(v, 32, 1))
    return v * cosw[...] + turned * sinw[...]


def rotated_back(v, cosw, sinw):
    low = lane_in_head(v.shape) < HD // 2
    scaled = v * sinw[...]
    turned = jnp.where(low, pltpu.roll(scaled, v.shape[1] - 32, 1), -pltpu.roll(scaled, 32, 1))
    return v * cosw[...] + turned


def key_value_kernel(has_x, sel, own, recv, pab, cosw, sinw, *rest):
    if has_x:
        x_ref, norm_ref, kv_ref, gain_ref, buf, sems = rest
    else:
        mid_ref, yo_ref, yr_ref, x_out, norm_ref, kv_ref, gain_ref, buf, sems = rest
    pick(sel, own, recv, 0, buf, sems)
    if has_x:
        x = x_ref[...].astype(f32)
    else:
        xb = (mid_ref[...] + yo_ref[...] + yr_ref[...]).astype(bf16)
        x_out[...] = xb
        x = xb.astype(f32)
    rstd = rstd_of(x)
    arrived(own, 0, buf, sems)
    gains = nt(chunk_of(buf, 2)[:, 128:].astype(f32).T.astype(bf16), pab[...])[0:8, :]
    gain_ref[...] = gains
    normed = (x * rstd * gains[0:1, :]).astype(bf16)
    norm_b = nn(normed, pab[...]).astype(bf16)
    norm_ref[...] = norm_b
    proj = jnp.concatenate([nn(norm_b, chunk_of(buf, j)) for j in range(3)], axis=1)
    kv_ref[...] = rotated(proj, cosw, sinw).astype(bf16)[:, : 2 * KW]


def query_kernel(sel, own, recv, norm_ref, cosw, sinw, q_ref, buf, sems):
    pick(sel, own, recv, 48, buf, sems)
    arrived(own, 48, buf, sems)
    proj = jnp.concatenate([nn(norm_ref[...], chunk_of(buf, j)) for j in range(4)], axis=1)
    q_ref[...] = rotated(proj, cosw, sinw).astype(bf16)


def heads_of(ref, i):
    return jnp.concatenate([ref[:, HD * (3 * i + h) : HD * (3 * i + h + 1)] for h in range(3)], axis=0)


def softmax_terms(q3, kg, allowed3):
    scores = nt(q3, kg) * 0.125
    scores = jnp.where(allowed3, scores, masked_score)
    highest = jnp.max(scores, axis=1, keepdims=True)
    terms = jnp.exp(scores - highest)
    return terms / jnp.sum(terms, axis=1, keepdims=True)


def attend_kernel(sel, own, recv, q, kv, r1, r2, r3, mask, x_ref, gain_ref, pnb, attb_ref, mid_ref, n2_ref, buf, kvs, att, sems):
    pick(sel, own, recv, 112, buf, sems)
    for k, part in enumerate((r3, r2, r1)):
        kvs[TOK * k : TOK * k + TOK, :] = part[...]
    kvs[3 * TOK :, :] = kv[...]
    allowed = mask[...] > 0.5
    allowed3 = jnp.concatenate([allowed] * 3, axis=0)
    for i in range(HK):
        kg = kvs[:, HD * i : HD * i + HD]
        vg = kvs[:, KW + HD * i : KW + HD * i + HD]
        probs = softmax_terms(heads_of(q, i), kg, allowed3).astype(bf16)
        o3 = nn(probs, vg).astype(bf16)
        for h in range(3):
            lane = HD * (3 * i + h)
            att[:, lane : lane + HD] = o3[TOK * h : TOK * h + TOK, :]
    attb = nn(att[...], pnb[...]).astype(bf16)
    attb_ref[...] = attb
    arrived(own, 112, buf, sems)
    out = jnp.concatenate([nn(attb, chunk_of(buf, j)) for j in range(4)], axis=1)
    mid = x_ref[...].astype(f32) + out
    mid_ref[...] = mid
    n2_ref[...] = (mid * rstd_of(mid) * gain_ref[1:2, :]).astype(bf16)


def tile_of(w, g, section):
    if section == 1:
        return w[g].reshape(320, 256)
    if not isinstance(w, tuple):
        return w[:, g].reshape(320, 256)
    if w[0].shape[0] == 1:
        return jnp.concatenate([part[0, g] for part in w], axis=0)
    return w[g][:, 0].reshape(320, 256)


def weight_refs(section, refs):
    if section == 1:
        return refs[0], refs[1], refs[2], refs[3:]
    *refs, down = refs
    for i in range(4):

        @pl.when(pl.program_id(0) == i)
        def _(i=i):
            down[...] = refs[8 + i][...]

    return tuple(refs[:4]), tuple(refs[4:8]), down, refs[12:]


def lanes(gx, g, section):
    if section == 0:
        return pl.ds(pl.multiple_of((gx[0] + g) % 4 * 256, 256), 256)
    return pl.ds(256 * g, 256)


def hidden_parts(gx, xs, wg, wu, section):
    gate = up = None
    for g in range(4):
        xg = xs[:, lanes(gx, g, section)]
        a, b = nt(xg, tile_of(wg, g, section)), nt(xg, tile_of(wu, g, section))
        gate, up = (a, b) if g == 0 else (gate + a, up + b)
    return gate, up, 1.0 / (1.0 + jnp.exp(-gate))


def ffn_kernel(section, gx, xo, xr, *refs):
    wg, wu, wd, (yo, yr, xs) = weight_refs(section, refs)
    j = pl.program_id(0)

    @pl.when(j == 0)
    def _():
        yo[...] = jnp.zeros_like(yo)
        yr[...] = jnp.zeros_like(yr)
        xs[:TOK] = xo[...]
        xs[TOK:] = xr[...]

    gate, up, sigma = hidden_parts(gx, xs, wg, wu, section)
    hidden = (gate * sigma * up).astype(bf16)
    for g in range(4):
        y = nn(hidden, tile_of(wd, g, section))
        yo[:, lanes(gx, g, section)] += y[:TOK]
        yr[:, lanes(gx, g, section)] += y[TOK:]


def ffn_back_kernel(section, gx, xo, xr, do, dr, *refs):
    wg, wu, wd, rest = weight_refs(section, refs)
    *attn, grads, no, nr, xs, ds = rest
    if section == 0:
        row = 240
        for mine, other in ((attn[0], attn[1]), (attn[2], attn[3])):
            rows = mine.shape[3]
            grads[:, :, :, row : row + rows, :] = (mine[...].astype(f32) + other[...].astype(f32)).astype(bf16)
            row += rows
    j = pl.program_id(0)

    @pl.when(j == 0)
    def _():
        no[...] = jnp.zeros_like(no)
        nr[...] = jnp.zeros_like(nr)
        xs[:TOK] = xo[...]
        xs[TOK:] = xr[...]
        ds[:TOK] = do[...]
        ds[TOK:] = dr[...]

    gate, up, sigma = hidden_parts(gx, xs, wg, wu, section)
    hidden = gate * sigma * up
    d_hidden = None
    for g in range(4):
        a = nt(ds[:, lanes(gx, g, section)], tile_of(wd, g, section))
        d_hidden = a if g == 0 else d_hidden + a
    d_gate = (d_hidden * up * sigma * (1.0 + gate * (1.0 - sigma))).astype(bf16)
    d_up = (d_hidden * gate * sigma).astype(bf16)
    hid_t = hidden.astype(bf16).T
    dg_t = d_gate.T
    du_t = d_up.T
    for g in range(4):
        xg, dg = xs[:, lanes(gx, g, section)], ds[:, lanes(gx, g, section)]
        values = (nn(dg_t, xg), nn(du_t, xg), nn(hid_t, dg))
        for m, value in enumerate(values):
            value = value.astype(bf16).reshape(4, 80, 256)
            if section == 0:
                for i in range(4):
                    grads[(gx[1] + i) % 4, 0, (gx[0] + g) % 4, 80 * m : 80 * m + 80, :] = value[i]
            else:
                grads[:, g, 80 * m : 80 * m + 80, :] = value
        dn = nn(d_gate, tile_of(wg, g, section)) + nn(d_up, tile_of(wu, g, section))
        no[:, lanes(gx, g, section)] += dn[:TOK]
        nr[:, lanes(gx, g, section)] += dn[TOK:]


def norm_back(e, z, rstd):
    return rstd * (e - z * (jnp.sum(e * z, axis=1, keepdims=True) * (1.0 / D)))


def attend_back_kernel(
    sel, own, recv, no, nr, mid_ref, gain_ref, dy_ref, q, kv, r1, r2, r3, mask, pnb,
    dmid_ref, dproj_ref, gg_ref, dq_ref, dkv_ref, d1, d2, d3, buf, kvs, dkv, sems,
):
    pick(sel, own, recv, 112, buf, sems)
    for k, part in enumerate((r3, r2, r1)):
        kvs[TOK * k : TOK * k + TOK, :] = part[...]
    kvs[3 * TOK :, :] = kv[...]
    mid = mid_ref[...]
    rstd = rstd_of(mid)
    z = mid * rstd
    dn = no[...] + nr[...]
    gg_ref[...] = jnp.broadcast_to(jnp.sum(dn * z, axis=0, keepdims=True), gg_ref.shape)
    dmid = dy_ref[...].astype(f32) + norm_back(dn * gain_ref[1:2, :], z, rstd)
    dmid_ref[...] = dmid
    dproj = dmid.astype(bf16)
    dproj_ref[...] = dproj
    arrived(own, 112, buf, sems)
    datt = None
    for j in range(4):
        a = nt(dproj[:, 256 * j : 256 * j + 256], chunk_of(buf, j))
        datt = a if j == 0 else datt + a
    datt = nt(datt.astype(bf16), pnb[...]).astype(bf16)
    allowed = mask[...] > 0.5
    allowed3 = jnp.concatenate([allowed] * 3, axis=0)
    dq_ref[:, 896:] = jnp.zeros((TOK, 128), f32)
    for i in range(HK):
        kg = kvs[:, HD * i : HD * i + HD]
        vg = kvs[:, KW + HD * i : KW + HD * i + HD]
        q3 = heads_of(q, i)
        do3 = heads_of(datt, i)
        probs = softmax_terms(q3, kg, allowed3)
        d_probs = nt(do3, vg)
        inner = jnp.sum(probs * d_probs, axis=1, keepdims=True)
        d_scores = (probs * (d_probs - inner)).astype(bf16)
        dq3 = nn(d_scores, kg) * 0.125
        for h in range(3):
            lane = HD * (3 * i + h)
            dq_ref[:, lane : lane + HD] = dq3[TOK * h : TOK * h + TOK, :]
        dkv[:, HD * i : HD * i + HD] = tn(d_scores, q3) * 0.125
        dkv[:, KW + HD * i : KW + HD * i + HD] = tn(probs.astype(bf16), do3)
    dkv_ref[...] = dkv[3 * TOK :, :]
    for k, part in enumerate((d3, d2, d1)):
        part[...] = dkv[TOK * k : TOK * k + TOK, :].astype(bf16)


def split3(v):
    hi = v.astype(bf16)
    rest = v - hi.astype(f32)
    middle = rest.astype(bf16)
    return hi, middle, (rest - middle.astype(f32)).astype(bf16)


def query_back_kernel(
    sel, core, own, recv, dq, cosw, sinw, norm_ref, attb, dproj, dn_ref, keep, send, buf, left, right, sems,
):
    pick(sel, own, recv, 48, buf, sems)
    dp = rotated_back(dq[...], cosw, sinw).astype(bf16)
    left[0] = norm_ref[...].T
    left[1] = attb[...].T
    for j in range(4):
        right[j] = dp[:, 256 * j : 256 * j + 256]
        right[4 + j] = dproj[:, 256 * j : 256 * j + 256]
    for target, half in ((keep, core[0]), (send, 1 - core[0])):
        for j in range(4):
            target[:, 16 * j : 16 * j + 16, :] = nn(left[half], right[4 * half + j]).astype(bf16).reshape(64, 16, 256)
    arrived(own, 48, buf, sems)
    dn = None
    for j in range(4):
        a = nt(dp[:, 256 * j : 256 * j + 256], chunk_of(buf, j))
        dn = a if j == 0 else dn + a
    dn_ref[...] = dn


def key_value_back_kernel(
    sel, core, own, recv, dkv, e1, e2, e3, cosw, sinw, norm_ref, x_ref, gain_ref, dmid_ref, pba, dnq, gg,
    dx_ref, keep, send, buf, right, sems,
):
    pick(sel, own, recv, 0, buf, sems)
    kv = dkv[...] + e1[...].astype(f32) + e2[...].astype(f32) + e3[...].astype(f32)
    d = jnp.concatenate([kv, jnp.zeros((TOK, 128), f32)], axis=1)
    dp = rotated_back(d, cosw, sinw).astype(bf16)
    arrived(own, 0, buf, sems)
    dn_b = dnq[...]
    for j in range(3):
        dn_b = dn_b + nt(dp[:, 256 * j : 256 * j + 256], chunk_of(buf, j))
        right[j] = dp[:, 256 * j : 256 * j + 256]
    right[3] = jnp.zeros((TOK, 256), bf16)
    hi, middle, lo = split3(dn_b)
    dn = nn(hi, pba[...]) + nn(middle, pba[...]) + nn(lo, pba[...])
    x = x_ref[...].astype(f32)
    rstd = rstd_of(x)
    z = x * rstd
    g1 = jnp.sum(dn * z, axis=0, keepdims=True)
    dx_ref[...] = (dmid_ref[...] + norm_back(dn * gain_ref[0:1, :], z, rstd)).astype(bf16)
    row = lax.broadcasted_iota(jnp.int32, (256, WA), 0)
    gains = jnp.where(row == 128, g1, jnp.where(row == 129, gg[0:1, :], 0.0)).astype(bf16)
    gains = nt(pba[...], gains)
    norm_t = norm_ref[...].T
    for target, half in ((keep, core[0]), (send, 1 - core[0])):
        for j in range(2):
            g = nn(norm_t, right[2 * half + j])
            if j == 0:
                g = g + gains * half.astype(f32)
            target[:, 16 * j : 16 * j + 16, :] = g.astype(bf16).reshape(64, 16, 256)


VM = pl.BlockSpec(memory_space=pltpu.VMEM)
ANY = pl.BlockSpec(memory_space=pl.ANY)
SM = pl.BlockSpec(memory_space=pltpu.SMEM)


def weight_scratch(rows):
    return pltpu.VMEM((16, 4, rows, 256), bf16)


def key_value(sel, own, recv, pab, cosw, sinw, x=None, parts=None):
    outs = [sds((TOK, WA), bf16), sds((TOK, 2 * KW), bf16), sds((8, WA), f32)]
    ins = [sel, own, recv, pab, cosw, sinw] + ([x] if parts is None else list(parts))
    if parts is not None:
        outs = [sds((TOK, WA), bf16)] + outs
    res = call(
        functools.partial(key_value_kernel, parts is None),
        outs, ins, [SM, ANY, ANY] + [VM] * (len(ins) - 3),
        [weight_scratch(48), pltpu.SemaphoreType.DMA((4,))], name="key_value",
    )
    return ([x] + list(res)) if parts is None else res


def query(sel, own, recv, *rest):
    return call(
        query_kernel, [sds((TOK, WA), bf16)], [sel, own, recv, *rest], [SM, ANY, ANY] + [VM] * len(rest),
        [weight_scratch(64), pltpu.SemaphoreType.DMA((4,))], name="query",
    )[0]


def attend(sel, own, recv, q, kv, chunks, mask, x, gains, pnb):
    ins = [sel, own, recv, q, kv, *chunks, mask, x, gains, pnb]
    return call(
        attend_kernel,
        [sds((TOK, WA), bf16), sds((TOK, WA), f32), sds((TOK, WA), bf16)],
        ins, [SM, ANY, ANY] + [VM] * (len(ins) - 3),
        [weight_scratch(64), pltpu.VMEM((LEN, 2 * KW), bf16), pltpu.VMEM((TOK, QW), bf16), pltpu.SemaphoreType.DMA((4,))],
        name="attend",
    )


def weight_specs(section):
    if section == 0:
        by_z = [pl.BlockSpec((1, 4, 80, 256), lambda j, p: (j, 0, 0, 0)) for _ in range(4)]
        by_x = [pl.BlockSpec((4, 1, 80, 256), lambda j, p: (0, j, 0, 0)) for _ in range(4)]
        return by_z + by_x + [whole((4, 4, 80, 256)) for _ in range(4)]
    return [pl.BlockSpec((4, 4, 80, 256), lambda j, p, m=m: (0, j, m, 0)) for m in range(3)]


def down_scratch(section):
    return [pltpu.VMEM((4, 4, 80, 256), bf16)] if section == 0 else []


def whole(shape):
    return pl.BlockSpec(shape, lambda j, p: (0,) * len(shape))


def ffn(section, place, xo, xr, packed):
    row = whole((TOK, WA))
    return stepped(
        functools.partial(ffn_kernel, section), place, [sds((TOK, WA), f32)] * 2, [xo, xr, *packed],
        [row, row] + weight_specs(section), [row, row], [pltpu.VMEM((2 * TOK, WA), bf16)] + down_scratch(section), "ffn",
    )


def ffn_back(section, place, xo, xr, do, dr, packed, attn=()):
    row = whole((TOK, WA))
    if section == 1:
        grads, block = sds((16, 4, 240, 256), bf16), pl.BlockSpec((4, 4, 240, 256), lambda j, p: (j, 0, 0, 0))
    else:
        grads = sds((4, 4, 4, 336, 256), bf16)
        block = pl.BlockSpec((4, 1, 4, 336, 256), lambda j, p: (0, (p[2] + j) % 4, 0, 0, 0))
    attn_specs = [pl.BlockSpec((4, 1) + v.shape[2:], lambda j, p: (0, (p[2] + j) % 4, 0, 0, 0)) for v in attn]
    return stepped(
        functools.partial(ffn_back_kernel, section), place, [grads] + [sds((TOK, WA), f32)] * 2,
        [xo, xr, do, dr, *packed, *attn],
        [row] * 4 + weight_specs(section) + attn_specs, [block, row, row],
        [pltpu.VMEM((2 * TOK, WA), bf16)] * 2 + down_scratch(section), "ffn_back",
    )


def attend_back(sel, own, recv, no, nr, mid, gains, dy, q, kv, chunks, mask, pnb):
    ins = [sel, own, recv, no, nr, mid, gains, dy, q, kv, *chunks, mask, pnb]
    small = sds((TOK, 2 * KW), bf16)
    return call(
        attend_back_kernel,
        [sds((TOK, WA), f32), sds((TOK, WA), bf16), sds((8, WA), f32), sds((TOK, WA), f32), sds((TOK, 2 * KW), f32), small, small, small],
        ins, [SM, ANY, ANY] + [VM] * (len(ins) - 3),
        [weight_scratch(64), pltpu.VMEM((LEN, 2 * KW), bf16), pltpu.VMEM((LEN, 2 * KW), f32), pltpu.SemaphoreType.DMA((4,))],
        name="attend_back",
    )


def query_back(sel, core, own, recv, *rest):
    return call(
        query_back_kernel, [sds((TOK, WA), f32)] + [sds((64, 64, 256), bf16)] * 2,
        [sel, core, own, recv, *rest], [SM, SM, ANY, ANY] + [VM] * len(rest),
        [weight_scratch(64), pltpu.VMEM((2, WA, TOK), bf16), pltpu.VMEM((8, TOK, 256), bf16), pltpu.SemaphoreType.DMA((4,))],
        name="query_back",
    )


def key_value_back(sel, core, own, recv, *rest):
    return call(
        key_value_back_kernel, [sds((TOK, WA), bf16)] + [sds((64, 32, 256), bf16)] * 2,
        [sel, core, own, recv, *rest], [SM, SM, ANY, ANY] + [VM] * len(rest),
        [weight_scratch(48), pltpu.VMEM((4, TOK, 256), bf16), pltpu.SemaphoreType.DMA((4,))],
        name="key_value_back",
    )


def other_core(v):
    return lax.ppermute(v, "section", [(0, 1), (1, 0)])


def shift_perm(name, k):
    if name == "x":
        return "gx", [(i, (i + k) % 4) for i in range(4)]
    if name == "z":
        return "gy", [(i, (i + 4 * k) % 16) for i in range(16)]
    return "gy", [(i, (i // 4) * 4 + (i % 4 + k) % 4) for i in range(16)]


def permuted(v, name, k):
    axis, perm = shift_perm(name, k)
    return lax.ppermute(v, axis, perm)


ORDERS = (("x", "y", "z"), ("y", "z", "x"), ("z", "x", "y"))
GROUPS = (((0, 1), (0, 3), (1, 1), (1, 3), (2, 2)), ((0, 2), (1, 2), (2, 1), (2, 3)))


def exchange(pieces, names, grouped, beside=()):
    keys = list(pieces)
    pieces = dict(zip(keys, lax.optimization_barrier([pieces[key] for key in keys])))
    if not grouped:
        return {key: permuted(pieces[key], names[key[0]], key[1]) for key in keys}, beside
    got = {key: permuted(pieces[key], names[key[0]], key[1]) for key in GROUPS[0]}
    tied = lax.optimization_barrier([[got[key] for key in GROUPS[0]], [pieces[key] for key in GROUPS[1]], list(beside)])
    got = dict(zip(GROUPS[0], tied[0]))
    for key, piece in zip(GROUPS[1], tied[1]):
        got[key] = permuted(piece, names[key[0]], key[1])
    return got, tied[2]


def gather_chunks(chunks, beside, after_first):
    state = [(c, ()) for c in chunks]

    def joined(got, names):
        after = []
        for c in range(3):
            v, have = state[c]
            have = tuple(n for n in ("z", "y", "x") if n in have or n == names[c])
            v = jnp.stack([v, got[(c, 3)], got[(c, 2)], got[(c, 1)]], axis=have.index(names[c]))
            after.append((v, have))
        return after

    for step in range(3):
        names = [order[step] for order in ORDERS]
        pieces = {(c, k): state[c][0] for c in range(3) for k in (1, 2, 3)}
        if step == 1:
            index, _ = lax.optimization_barrier((jnp.arange(WA, dtype=jnp.int32), [v for v, _ in state]))
            beside = [*beside, *place_matrices(index)]
        got, tied = exchange(pieces, names, step >= 1, ((), beside, after_first)[step])
        if step < 2:
            state = joined(got, names)
        beside, after_first = (tied if step == 1 else beside), (tied if step == 2 else after_first)

    def finish(value):
        keys = list(got)
        value, parts = lax.optimization_barrier((value, [got[key] for key in keys]))
        parts = dict(zip(keys, parts))
        apart = [[state[c][0], parts[(c, 3)], parts[(c, 2)], parts[(c, 1)]] for c in range(3)]
        return value, apart[0] + apart[1] + apart[2]

    return beside, after_first, finish


def reduce_axis(v, dim, name, place):
    me = place[name]
    pieces = [lax.dynamic_index_in_dim(v, (me + k) % 4, dim, keepdims=False) for k in (1, 3, 2)]
    pieces = lax.optimization_barrier(pieces)
    total = lax.dynamic_index_in_dim(v, me, dim, keepdims=False).astype(f32)
    for piece, k in zip(pieces, (1, 3, 2)):
        total = total + permuted(piece, name, k).astype(f32)
    return total.astype(bf16)


def rope_tables(positions):
    frequency = rope_base ** (-(jnp.arange(HD // 2, dtype=f32) * 2.0) / HD)
    angles = positions.astype(f32)[:, None] * frequency[None, :]
    cosine, sine = jnp.cos(angles), jnp.sin(angles)
    cosine, sine = jnp.concatenate([cosine, cosine], 1), jnp.concatenate([sine, sine], 1)

    def wide(table, plain):
        key = jnp.concatenate([jnp.tile(table, (1, HK)), jnp.full((TOK, 448), plain, f32)], 1)
        return key, jnp.concatenate([jnp.tile(table, (1, HQ)), jnp.full((TOK, 64), plain, f32)], 1)

    return wide(cosine, 1.0) + wide(sine, 0.0)


def to_a(v):
    rows = v.shape[0]
    return jnp.pad(v.reshape(rows, 4, 240), ((0, 0), (0, 0), (0, 16))).reshape(rows, WA)


def from_a(v):
    return v.reshape(v.shape[:-1] + (4, 256))[..., :240].reshape(v.shape[:-1] + (D,))


def place_matrices(a):
    in_a = jnp.where(a % 256 < 240, (a // 256) * 240 + a % 256, -1)
    shard = (a // 16 % 4) * 16 + a // 64
    in_b = jnp.where(a % 16 < 15, shard * 15 + a % 16, -2)
    pab = (in_a[:, None] == in_b[None, :]).astype(bf16)
    pba = (in_b[:, None] == in_a[None, :]).astype(bf16)
    pnb = (a[:QW, None] == in_b[None, :]).astype(bf16)
    return pab, pba, pnb


def per_device(inputs, cotangent, segment_ids, gain_attn, w_qkv, w_out, gain_ffn, w_gate, w_up, w_down):
    core = lax.axis_index("section")
    gx = lax.axis_index("gx")
    gy = lax.axis_index("gy")
    first = core == 0
    place = {"x": gx, "z": gy // 4, "y": gy % 4}

    pieces = jnp.stack([w_gate[0].T, w_up[0].T, w_down[0]]).reshape(3, 2, 80, 240)
    keep = jnp.where(first, pieces[:, 0], pieces[:, 1])
    got = other_core(jnp.where(first, pieces[:, 1], pieces[:, 0]))
    halves = jnp.concatenate([jnp.where(first, keep, got), jnp.where(first, got, keep)], 0)
    halves = jnp.pad(halves.reshape(FROWS, 240), ((0, 0), (0, 16)))
    def at(v, lane):
        return jnp.pad(v, ((0, 1), (lane, 11 * 256 - lane - v.shape[1])))

    attn = at(w_qkv[0][:, QW:], 0) + at(gain_attn[0][:, None], 640) + at(gain_ffn[0][:, None], 641)
    attn = attn + at(w_qkv[0][:, :QW], 768)
    for g in range(4):
        attn = attn + at(w_out[0][:, 240 * g : 240 * g + 240], QKVW + 256 * g)
    attn = attn.reshape(16, 11, 256).transpose(1, 0, 2).reshape(AROWS, 256)
    own = lax.all_gather(attn[None], ("gx", "gy"), axis=0, tiled=True)
    own_in = to_a(jnp.where(first, inputs[0, 0], inputs[1, 0]))
    cot0, cot1 = to_a(cotangent[0, 0]), to_a(cotangent[1, 0])
    cot_own, cot_other = jnp.where(first, cot0, cot1), jnp.where(first, cot1, cot0)
    segments = jnp.where(first, segment_ids[0, 0], segment_ids[1, 0])
    local_ids = lax.dynamic_slice_in_dim(segments, gx * TOK, TOK, 0)
    own_index = gx * TOK + jnp.arange(TOK, dtype=jnp.int32)
    doc_start = jnp.sum((segments[None, :] < local_ids[:, None]).astype(jnp.int32), axis=1)
    key_index = (gx - 3) * TOK + jnp.arange(LEN, dtype=jnp.int32)
    key_ids = lax.dynamic_slice_in_dim(jnp.pad(segments, (3 * TOK, 0), constant_values=-1), gx * TOK, LEN, 0)
    mask = ((local_ids[:, None] == key_ids[None, :]) & (key_index[None, :] <= own_index[:, None])).astype(f32)
    cos_kv, cos_q, sin_kv, sin_q = rope_tables(own_index - doc_start)
    beside = [cos_kv, cos_q, sin_kv, sin_q, mask, own_in, cot_own, cot_other]
    early = [halves[:80], halves[80:160], halves[160:240]]
    beside, (own, second), finish = gather_chunks(early, beside, (own, halves[240:]))
    recv = other_core(own)
    packed = lax.all_gather(second[None], ("gx", "gy"), axis=0, tiled=True).reshape(4, 16, 240, 256)
    cos_kv, cos_q, sin_kv, sin_q, mask, own_in, cot_own, cot_other, pab, pba, pnb = beside
    ffn_weights = [None, [packed] * 3]

    def ahead(v, k):
        return lax.ppermute(v, "gx", [(i, i + k) for i in range(4 - k)])

    def back(v, k):
        return lax.ppermute(v, "gx", [(i + k, i) for i in range(4 - k)])

    def added(a, b):
        return (a.astype(f32) + b.astype(f32)).astype(bf16)

    def over_gy(v):
        rows = v.shape[-2]
        return lax.psum_scatter(v.reshape(16, 4 * rows, 256), "gy", scatter_dimension=0, tiled=True).reshape(4, rows, 256)

    grid = (4, 4, 4)
    gx_now = jnp.stack([gx, gy // 4, gy % 4]).astype(jnp.int32)
    sels = [core[None].astype(jnp.int32), (1 - core)[None].astype(jnp.int32)]
    kept = []
    x, parts = own_in, None
    for section in range(2):
        sel = sels[section]
        x, norm_b, kv, gains = key_value(sel, own, recv, pab, cos_kv, sin_kv, x, parts)
        chunks = [ahead(kv, 1), ahead(kv, 2), ahead(kv, 3)]
        q = query(sel, own, recv, norm_b, cos_q, sin_q)
        if section == 0:
            q, first_ffn = finish(q)
            ffn_weights[0] = first_ffn
        attb, mid, n2 = attend(sel, own, recv, q, kv, chunks, mask, x, gains, pnb)
        n2_other = other_core(n2)
        if section == 0:
            yo, yr = ffn(section, gx_now, n2, n2_other, ffn_weights[section])
            parts = (mid, yo, other_core(yr))
        kept.append((x, norm_b, q, kv, gains, chunks, attb, mid, n2, n2_other))

    dy, dy_other = cot_own, cot_other
    grads_in, attn = [None, None], ()
    for section in (1, 0):
        sel = sels[section]
        x, norm_b, q, kv, gains, chunks, attb, mid, n2, n2_other = kept[section]
        grads, no, nr = ffn_back(section, gx_now, n2, n2_other, dy, dy_other, ffn_weights[section], attn)
        nr = other_core(nr)
        if section == 1:
            late1 = over_gy(grads)
        dmid, dproj, gg, dq, dkv, d1, d2, d3 = attend_back(
            sel, own, recv, no, nr, mid, gains, dy, q, kv, chunks, mask, pnb
        )
        back_chunks = [back(d1, 1), back(d2, 2), back(d3, 3)]
        dnq, keep_q, send_q = query_back(sel, sels[0], own, recv, dq, cos_q, sin_q, norm_b, attb, dproj)
        if section == 0:
            late1, grads, *back_chunks = lax.optimization_barrier((late1, grads, *back_chunks))
            late2 = over_gy(grads)
        send_q, *back_chunks = lax.optimization_barrier((send_q, *back_chunks))
        got_q = other_core(send_q)
        dy, keep_kv, send_kv = key_value_back(
            sel, sels[0], own, recv, dkv, *back_chunks, cos_kv, sin_kv, norm_b, x, gains, dmid, pba, dnq, gg
        )
        got_kv = other_core(send_kv)
        grads_in[section] = dy
        if section == 1:
            pairs = (keep_q, got_q, keep_kv, got_kv)
            dy, dy_other, *attn = lax.optimization_barrier((dy, other_core(dy), *pairs))
            attn = [v.reshape(grid + v.shape[1:]) for v in attn]

    _, n2, n2_other = lax.optimization_barrier((grads_in[0], *kept[1][-2:]))
    yo, yr = ffn(1, gx_now, n2, n2_other, ffn_weights[1])
    outs = [kept[1][0], (kept[1][7] + yo + other_core(yr)).astype(bf16)]

    attn0 = jnp.concatenate([added(keep_q, got_q), added(keep_kv, got_kv)], 1).reshape(grid + (96, 256))
    attn0 = reduce_axis(attn0, 2, "x", place)
    attn0, late1 = lax.optimization_barrier((attn0, reduce_axis(late1, 0, "x", place)))
    attn0 = reduce_axis(attn0, 0, "z", place)
    attn0 = reduce_axis(attn0, 0, "y", place)
    late2 = reduce_axis(late2, 0, "x", place)
    half = [jnp.concatenate([late2[:240], attn0], 0), jnp.concatenate([late1, late2[240:]], 0)]
    mine = jnp.where(first, half[0], half[1])
    theirs = other_core(jnp.where(first, half[1], half[0]))
    low, high = jnp.where(first, mine, theirs), jnp.where(first, theirs, mine)
    ff = jnp.concatenate([low[:240].reshape(3, 80, 256), high[:240].reshape(3, 80, 256)], 1)[:, :, :240].astype(f32)
    def columns(v):
        chunks = v.reshape(v.shape[0] // 16, 16, 256)[:, :15].astype(f32)
        return chunks.transpose(1, 0, 2).reshape(15, v.shape[0] * 16)

    q_grad, kv_grad = columns(low[240:304]), columns(jnp.concatenate([low[304:336], high[304:320]], 0))
    out_grad = from_a(columns(high[240:304]))
    grad_qkv = jnp.concatenate([q_grad[:, :QW], kv_grad[:, : 2 * KW]], 1)

    def placed(pair):
        a = jnp.where(first, pair[0], pair[1])
        b = other_core(jnp.where(first, pair[1], pair[0]))
        both = jnp.stack([jnp.where(first, a, b), jnp.where(first, b, a)])
        return from_a(both)[None, :, None]

    return (
        placed(outs),
        placed(grads_in),
        kv_grad[:, 640][None],
        grad_qkv[None],
        out_grad[None],
        kv_grad[:, 641][None],
        ff[0].T[None],
        ff[1].T[None],
        ff[2][None],
    )


def solution(mesh):
    return jax.shard_map(
        per_device,
        mesh=mesh,
        in_specs=(
            P(None, "gy", "gx", None),
            P(None, "gy", "gx", None),
            P(None, "gy", None),
            P("section", ("gx", "gy")),
            P("section", ("gx", "gy"), None),
            P("section", ("gx", "gy"), None),
            P("section", ("gx", "gy")),
            P("section", "gx", "gy"),
            P("section", "gx", "gy"),
            P("section", "gy", "gx"),
        ),
        out_specs=(
            P("section", None, "gy", "gx", None),
            P("section", None, "gy", "gx", None),
            P("section", ("gx", "gy")),
            P("section", ("gx", "gy"), None),
            P("section", ("gx", "gy"), None),
            P("section", ("gx", "gy")),
            P("section", "gx", "gy"),
            P("section", "gx", "gy"),
            P("section", "gy", "gx"),
        ),
        check_vma=False,
    )
```
